32 devices in a mesh: batch: 8 (over z, y), heads: 4 (over x, core).
Axes of the slice: x: 2, y: 2, z: 4, core: 2. Of those that a mesh axis runs over, the one named last changes fastest.
Arguments:
- tokens_in: bfloat16 [16384, 768], P(('batch', 'heads')), may hold values from -6 to 6
- cotangent: bfloat16 [16384, 768], P(('batch', 'heads')), may hold values from -6 to 6
- half_length: int32 [16], P('batch'), may hold values from 512 to 1024, as said below
- block_perm: int32 [12, 2], replicated, may hold values from 0 to 1, each once within a row
- w_query: bfloat16 [768, 768], P('heads'), may hold values from -0.21875 to 0.21875
- b_query: bfloat16 [768], P('heads'), may hold values from -1.5 to 1.5
- w_key: bfloat16 [768, 768], P('heads'), may hold values from -0.21875 to 0.21875
- w_value: bfloat16 [768, 768], P('heads'), may hold values from -0.21875 to 0.21875
- b_value: bfloat16 [768], P('heads'), may hold values from -1.5 to 1.5
- w_output: bfloat16 [768, 768], P('heads'), may hold values from -0.875 to 0.875
- b_output: bfloat16 [768], replicated, may hold values from -1.5 to 1.5
- norm1_gain: bfloat16 [768], replicated, may hold values from 0.5 to 1.5
- norm1_shift: bfloat16 [768], replicated, may hold values from -1.5 to 1.5
- w_inner: bfloat16 [768, 3072], P(None, 'heads'), may hold values from -0.21875 to 0.21875
- b_inner: bfloat16 [3072], P('heads'), may hold values from -1.5 to 1.5
- w_outer: bfloat16 [3072, 768], P('heads'), may hold values from -0.109375 to 0.109375
- b_outer: bfloat16 [768], replicated, may hold values from -1.5 to 1.5
- norm2_gain: bfloat16 [768], replicated, may hold values from 0.5 to 1.5
- norm2_shift: bfloat16 [768], replicated, may hold values from -1.5 to 1.5
Outputs:
- block_out: bfloat16 [16384, 768], P(('batch', 'heads'))
- grad_tokens: float32 [16384, 768], P(('batch', 'heads'))
- grad_w_query: float32 [768, 768], P('heads')
- grad_b_query: float32 [768], P('heads')
- grad_w_key: float32 [768, 768], P('heads')
- grad_w_value: float32 [768, 768], P('heads')
- grad_b_value: float32 [768], P('heads')
- grad_w_output: float32 [768, 768], P('heads')
- grad_b_output: float32 [768], replicated
- grad_norm1_gain: float32 [768], replicated
- grad_norm1_shift: float32 [768], replicated
- grad_w_inner: float32 [768, 3072], P(None, 'heads')
- grad_b_inner: float32 [3072], P('heads')
- grad_w_outer: float32 [3072, 768], P('heads')
- grad_b_outer: float32 [768], replicated
- grad_norm2_gain: float32 [768], replicated
- grad_norm2_shift: float32 [768], replicated
The draws below stay inside these ranges and needn't reach their ends.
Inputs may be any that keep to these rules, and one draw needn't show every extreme that they name: `half_length`: each entry is 1024 (one sequence) or 1024 // 2 (two sequences of that length). `block_perm`: each row is a permutation of 0 and 1.
All inputs are finite; a program needn't handle non-finite values.
Results may differ from the reference program's by a relative error of at most 0.015.
Values may be sent and summed in bfloat16 or wider, within the bound.
No kernel may reach another device: no remote copies, remote signals or barrier semaphores. Data moves between devices by JAX's collectives and lax.ppermute only.
A program may use at most 128 MiB of HBM per device.

```python
import jax
import jax.numpy as jnp
from jax import lax

HEADS = 12
HEAD_DIM = 64
D = 768
FF = 3072
HALF = 1024
HALVES_ALL = 16
TOKENS = 16384


def draw_half_length(key, part):
    key = jax.random.fold_in(key, 1)
    longs = jax.random.randint(key, (HALVES_ALL,), 0, 2)
    longs = longs.at[0].set(1).at[1].set(0)
    return (HALF // 2 + HALF // 2 * longs).astype(jnp.int32)


def steps_of(rng, shape, split, least, largest):
    level = 1.0
    for dim, blocks in split:
        heights = jax.random.uniform(jax.random.fold_in(jax.random.fold_in(rng, 6), dim), (blocks,), jnp.float32, least / len(split), largest / len(split))
        level = level * jnp.repeat(jnp.exp(heights), shape[dim] // blocks).reshape((-1,) + (1,) * (len(shape) - 1 - dim))
    return level


def centred(own_key, dims, scale, limit, cuts=(), dtype=jnp.bfloat16):
    values = jax.random.normal(own_key, dims, jnp.float32) * scale
    if len(cuts) > 0:
        values = steps_of(own_key, dims, cuts, -0.22, 0.18) * values
    return jnp.clip(values, min=-limit, max=limit).astype(dtype)


def setup_inputs(seed: int = 0) -> dict:
    keys = jax.random.split(jax.random.key(seed), 20)
    tokens_in = centred(keys[0], (TOKENS, D), 1.0, 6.0, ((0, 32),))
    cotangent = centred(keys[1], (TOKENS, D), 1.0, 6.0, ((0, 32),))
    half_length = draw_half_length(jax.random.fold_in(keys[19], 71), 0)
    block_perm = jax.vmap(lambda own: jax.random.permutation(own, 2))(jax.random.split(keys[3], HEADS)).reshape((HEADS, 2)).astype(jnp.int32)
    w_query = centred(keys[4], (D, D), D ** -0.5, 0.21875, ((0, 4),))
    b_query = centred(keys[5], (D,), 0.3, 1.5, ((0, 4),))
    w_key = centred(keys[6], (D, D), D ** -0.5, 0.21875, ((0, 4),))
    w_value = centred(keys[7], (D, D), D ** -0.5, 0.21875, ((0, 4),))
    b_value = centred(keys[8], (D,), 0.3, 1.5, ((0, 4),))
    w_output = centred(keys[9], (D, D), (D // 16) ** -0.5, 0.875, ((0, 4),))
    b_output = centred(keys[10], (D,), 0.3, 1.5)
    norm1_gain = jnp.clip(1.0 + 0.1 * jax.random.normal(keys[11], (D,), jnp.float32), 0.5, 1.5).astype(jnp.bfloat16)
    norm1_shift = centred(keys[12], (D,), 0.3, 1.5)
    w_inner = centred(keys[13], (D, FF), D ** -0.5, 0.21875, ((1, 4),))
    b_inner = centred(keys[14], (FF,), 0.3, 1.5, ((0, 4),))
    w_outer = centred(keys[15], (FF, D), FF ** -0.5, 0.109375, ((0, 4),))
    b_outer = centred(keys[16], (D,), 0.3, 1.5)
    norm2_gain = jnp.clip(1.0 + 0.1 * jax.random.normal(keys[17], (D,), jnp.float32), 0.5, 1.5).astype(jnp.bfloat16)
    norm2_shift = centred(keys[18], (D,), 0.3, 1.5)
    return {"tokens_in": tokens_in, "cotangent": cotangent, "half_length": half_length, "block_perm": block_perm, "w_query": w_query, "b_query": b_query, "w_key": w_key, "w_value": w_value, "b_value": b_value, "w_output": w_output, "b_output": b_output, "norm1_gain": norm1_gain, "norm1_shift": norm1_shift, "w_inner": w_inner, "b_inner": b_inner, "w_outer": w_outer, "b_outer": b_outer, "norm2_gain": norm2_gain, "norm2_shift": norm2_shift}


@jax.custom_vjp
def low(v):
    return lax.optimization_barrier(v.astype(jnp.bfloat16)).astype(jnp.float32)

@jax.custom_vjp
def low_back(v):
    return v

def low_keep(v):
    return (low(v), None)

def low_pass(kept, grad):
    return (grad,)

def back_keep(v):
    return (v, None)

def back_low(kept, grad):
    return (low(grad),)
low.defvjp(low_keep, low_pass)
low_back.defvjp(back_keep, back_low)
highest = lax.Precision.HIGHEST
epsilon = 1e-06
masked_score = -1e+30

def matmul(left, right):
    return jnp.dot(left, right, precision=highest)

def layer_norm(hidden, gain, shift):
    center = lax.optimization_barrier(jnp.mean(hidden, axis=-1, keepdims=True))
    spread = lax.optimization_barrier(jnp.mean(hidden * hidden, axis=-1, keepdims=True)) - center * center
    return (hidden - center) * lax.rsqrt(spread + epsilon) * gain + shift

def attend_half(queries, key_rows, value_rows, is_long, swap_flags):
    quarter = HALF // 2
    width = HEADS * HEAD_DIM
    query_q = queries.reshape(2, quarter, HEADS, HEAD_DIM)
    key_q = key_rows.reshape(2, quarter, HEADS, HEAD_DIM)
    value_q = value_rows.reshape(2, quarter, HEADS, HEAD_DIM)
    flipped = (is_long * swap_flags == 1)[None, :, None]
    within = (jnp.arange(quarter) // (quarter // 2)).astype(jnp.int32)
    allowed = (is_long == 1) | (within[None, :, None] ^ swap_flags[:, None, None] == within[None, None, :])
    pieces = []
    for half_side in range(2):
        key_sel = jnp.where(flipped, key_q[1 - half_side], key_q[half_side])
        value_sel = jnp.where(flipped, value_q[1 - half_side], value_q[half_side])
        scores = jnp.einsum('qhd,khd->hqk', query_q[half_side], key_sel, precision=highest) * HEAD_DIM ** (-0.5)
        scores = jnp.where(allowed, low_back(scores), masked_score)
        weights = jax.nn.softmax(scores, axis=-1)
        mixture = jnp.einsum('hqk,khd->qhd', low(weights), value_sel, precision=highest)
        pieces.append(mixture.reshape(quarter, width))
    return jnp.concatenate(pieces, axis=0)

def forward(tokens, is_long, swap_flags, w_query, b_query, w_key, w_value, b_value, w_output, b_output, norm1_gain, norm1_shift, w_inner, b_inner, w_outer, b_outer, norm2_gain, norm2_shift):
    queries = low(low_back(matmul(tokens, w_query.T) + b_query))
    key_rows = low(low_back(matmul(tokens, w_key.T)))
    value_rows = low(low_back(matmul(tokens, w_value.T) + b_value))
    attended = low(low_back(attend_half(queries, key_rows, value_rows, is_long, swap_flags)))
    normed = layer_norm(tokens + low_back(matmul(attended, w_output)) + b_output, norm1_gain, norm1_shift)
    inner = low_back(matmul(low(normed), w_inner) + b_inner)
    active = low(jax.nn.gelu(inner, approximate=False))
    return layer_norm(normed + low_back(matmul(active, w_outer)) + b_outer, norm2_gain, norm2_shift)

def reference(tokens_in, cotangent, half_length, block_perm, w_query, b_query, w_key, w_value, b_value, w_output, b_output, norm1_gain, norm1_shift, w_inner, b_inner, w_outer, b_outer, norm2_gain, norm2_shift):
    width = HEADS * HEAD_DIM
    is_long = (half_length == HALF).astype(jnp.int32)
    swap_flags = block_perm[:, 0].astype(jnp.int32)
    params = tuple((weight.astype(jnp.float32) for weight in (w_query, b_query, w_key, w_value, b_value, w_output, b_output, norm1_gain, norm1_shift, w_inner, b_inner, w_outer, b_outer, norm2_gain, norm2_shift)))
    token_halves = tokens_in.astype(jnp.float32).reshape(-1, HALF, width)
    cot_halves = cotangent.astype(jnp.float32).reshape(-1, HALF, width)

    def step(totals, pieces):
        half_tokens, half_cot, half_long = pieces

        def local(tokens, *weights):
            return forward(tokens, half_long, swap_flags, *weights)
        result, pullback = jax.vjp(local, half_tokens, *params)
        grads = pullback(half_cot)
        totals = tuple((total + extra for total, extra in zip(totals, grads[1:])))
        return (totals, (result, grads[0]))
    zeros = tuple((jnp.zeros(weight.shape, jnp.float32) for weight in params))
    totals, (outputs, token_grads) = lax.scan(step, zeros, (token_halves, cot_halves, is_long))
    block_out = outputs.reshape(-1, width).astype(jnp.bfloat16)
    grad_tokens = token_grads.reshape(-1, width)
    return (block_out, grad_tokens, totals[0], totals[1], totals[2], totals[3], totals[4], totals[5], totals[6], totals[7], totals[8], totals[9], totals[10], totals[11], totals[12], totals[13], totals[14])
```

```python
import functools

import jax
import jax.numpy as jnp
from jax import lax
from jax.experimental import pallas as pl
from jax.experimental.pallas import tpu as pltpu
from jax.sharding import PartitionSpec as P

HEAD_DIM = 64
HALF = 1024
SCALE = HEAD_DIM ** (-0.5)
epsilon = 1e-06

bf16 = jnp.bfloat16
f32 = jnp.float32


def dot_nn(left, right):
    return jnp.dot(left, right, preferred_element_type=f32)


def dot_nt(left, right):
    return lax.dot_general(left, right, (((1,), (1,)), ((), ())), preferred_element_type=f32)


def dot_tn(left, right):
    return lax.dot_general(left, right, (((0,), (0,)), ((), ())), preferred_element_type=f32)


def swap(value, axis, stride):
    size = lax.axis_size(axis)
    return lax.ppermute(value, axis, [(i, i ^ stride) for i in range(size)])


def piece(value, index, axis):
    half = value.shape[axis] // 2
    return lax.dynamic_slice_in_dim(value, index * half, half, axis)


def ordered(mine, other, bit, axis):
    return jnp.where(
        bit == 0,
        jnp.concatenate([mine, other], axis=axis),
        jnp.concatenate([other, mine], axis=axis),
    )


def gather_halves(block, axis):
    y_bit = lax.axis_index("batch") & 1
    first = swap(piece(block, y_bit, axis), "heads", 2)
    second = swap(first, "batch", 1)
    return first, second


def norm_rows(hidden, gain, shift):
    center = jnp.mean(hidden, axis=1, keepdims=True)
    rinv = lax.rsqrt(jnp.mean(hidden * hidden, axis=1, keepdims=True) - center * center + epsilon)
    zhat = (hidden - center) * rinv
    return (zhat * gain + shift, zhat, rinv)


def norm_back(grad_zhat, zhat, rinv):
    first_mean = jnp.mean(grad_zhat, axis=1, keepdims=True)
    second_mean = jnp.mean(grad_zhat * zhat, axis=1, keepdims=True)
    return rinv * (grad_zhat - first_mean - zhat * second_mean)


def gelu_parts(values):
    cdf = 0.5 * lax.erfc(-values * 0.7071067811865476)
    density = jnp.exp(-0.5 * values * values) * 0.3989422804014327
    return values * cdf, cdf + values * density


def attend_blocks(flags, visit):
    heads = 3

    @pl.when(flags[0] == 1)
    def _():
        for block in range(2):
            for head in range(heads):
                visit(head, block * 512, (block ^ flags[1 + head]) * 512, 512)

    @pl.when(flags[0] == 0)
    def _():
        for block in range(4):
            for head in range(heads):
                visit(head, block * 256, (block ^ flags[1 + head]) * 256, 256)


def attend_forward_kernel(flags, q_ref, k_ref, v_ref, out_ref, lse_ref):
    def visit(head, q_at, k_at, size):
        cols = slice(head * HEAD_DIM, (head + 1) * HEAD_DIM)
        q_rows = pl.ds(q_at, size)
        k_rows = pl.ds(pl.multiple_of(k_at, 256), size)
        queries = q_ref[q_rows, cols] * SCALE
        keys = k_ref[k_rows, cols]
        values_t = v_ref[k_rows, cols].astype(f32).T.astype(bf16)
        scores_t = dot_nt(keys, queries.astype(bf16))
        top = jnp.max(scores_t, axis=0, keepdims=True)
        weights_t = jnp.exp(scores_t - top)
        total = jnp.sum(weights_t, axis=0, keepdims=True)
        mixed_t = dot_nn(values_t, weights_t.astype(bf16)) * (1.0 / total)
        out_ref[q_rows, cols] = mixed_t.T.astype(bf16)
        lse_ref[head : head + 1, q_rows] = top + jnp.log(total)

    attend_blocks(flags, visit)


def attend_backward_kernel(flags, q_ref, k_ref, v_ref, g_ref, lse_ref, dq_ref, dk_ref, dv_ref):
    def visit(head, q_at, k_at, size):
        cols = slice(head * HEAD_DIM, (head + 1) * HEAD_DIM)
        q_rows = pl.ds(q_at, size)
        k_rows = pl.ds(pl.multiple_of(k_at, 256), size)
        queries = (q_ref[q_rows, cols] * SCALE).astype(bf16)
        keys = k_ref[k_rows, cols]
        keys_t = keys.astype(f32).T.astype(bf16)
        grads = g_ref[q_rows, cols]
        scores_t = dot_nt(keys, queries)
        weights_t = jnp.exp(scores_t - lse_ref[head : head + 1, q_rows])
        grad_weights_t = dot_nt(v_ref[k_rows, cols], grads)
        delta = jnp.sum(weights_t * grad_weights_t, axis=0, keepdims=True)
        grad_scores_t = (weights_t * (grad_weights_t - delta)).astype(bf16)
        dv_ref[k_rows, cols] = dot_nn(weights_t.astype(bf16), grads).astype(bf16)
        dk_ref[k_rows, cols] = dot_nn(grad_scores_t, queries).astype(bf16)
        dq_ref[q_rows, cols] = (dot_nn(keys_t, grad_scores_t).T * SCALE).astype(bf16)

    attend_blocks(flags, visit)


VMEM_SPEC = pl.BlockSpec(memory_space=pltpu.VMEM)
SMEM_SPEC = pl.BlockSpec(memory_space=pltpu.SMEM)


def attend_forward(flags, queries, keys, values):
    rows, width = queries.shape
    pairs = rows * rows // 2 * (width // HEAD_DIM)
    return pl.pallas_call(
        attend_forward_kernel,
        out_shape=(
            jax.ShapeDtypeStruct((rows, width), bf16),
            jax.ShapeDtypeStruct((8, rows), f32),
        ),
        in_specs=[SMEM_SPEC] + [VMEM_SPEC] * 3,
        out_specs=(VMEM_SPEC, VMEM_SPEC),
        compiler_params=pltpu.CompilerParams(vmem_limit_bytes=32 * 1024 * 1024),
        cost_estimate=pl.CostEstimate(
            flops=pairs * 256 * 4, bytes_accessed=rows * width * 8, transcendentals=pairs
        ),
    )(flags, queries, keys, values)


def attend_backward(flags, queries, keys, values, grads, lse):
    rows, width = queries.shape
    pairs = rows * rows // 2 * (width // HEAD_DIM)
    return pl.pallas_call(
        attend_backward_kernel,
        out_shape=(jax.ShapeDtypeStruct((rows, width), bf16),) * 3,
        in_specs=[SMEM_SPEC] + [VMEM_SPEC] * 5,
        out_specs=(VMEM_SPEC,) * 3,
        compiler_params=pltpu.CompilerParams(vmem_limit_bytes=32 * 1024 * 1024),
        cost_estimate=pl.CostEstimate(
            flops=pairs * 256 * 10, bytes_accessed=rows * width * 14, transcendentals=pairs
        ),
    )(flags, queries, keys, values, grads, lse)


def reduce_gradient(own, partner_keep, partner_send, axis):
    index = lax.axis_index("batch")
    size = lax.axis_size("batch")
    y_bit = index & 1
    got_send = swap(partner_send, "heads", 2)
    got_keep = swap(partner_keep, "heads", 2)
    send = (piece(own, 1 - y_bit, axis).astype(f32) + got_send.astype(f32)).astype(bf16)
    got = swap(send, "batch", 1)
    total = piece(own, y_bit, axis).astype(f32) + got_keep.astype(f32) + got.astype(f32)
    stride = 2
    while stride < size:
        bit = (index // stride) & 1
        got = swap(piece(total, 1 - bit, 0).astype(bf16), "batch", stride)
        total = piece(total, bit, 0) + got.astype(f32)
        stride *= 2
    whole = total.astype(bf16)
    while stride > 2:
        stride //= 2
        bit = (index // stride) & 1
        whole = ordered(whole, swap(whole, "batch", stride), bit, 0)
    return ordered(whole, swap(whole, "batch", 1), y_bit, axis).astype(f32)


def body(
    tokens_in,
    cotangent,
    half_length,
    block_perm,
    w_query,
    b_query,
    w_key,
    w_value,
    b_value,
    w_output,
    b_output,
    norm1_gain,
    norm1_shift,
    w_inner,
    b_inner,
    w_outer,
    b_outer,
    norm2_gain,
    norm2_shift,
):
    width = w_query.shape[0]
    model = w_query.shape[1]
    units = w_outer.shape[0]
    rows = tokens_in.shape[0]
    head_count = width // HEAD_DIM
    hid = lax.axis_index("heads")
    y_bit = lax.axis_index("batch") & 1
    is_long = (half_length[hid // 2] == HALF).astype(jnp.int32)

    def flags_of(owner):
        swaps = lax.dynamic_slice_in_dim(block_perm[:, 0], owner * head_count, head_count)
        return jnp.concatenate([is_long[None], swaps])

    other_tokens = swap(tokens_in, "heads", 1)
    packed_bias = jnp.concatenate(
        [
            jnp.concatenate([b_query, b_value, jnp.zeros((model - 2 * width,), bf16)])[None],
            b_inner[None],
            jnp.zeros((30, model), bf16),
        ]
    )
    qkv_weights = jnp.concatenate([w_query, w_key, w_value], axis=0)
    packed = jnp.concatenate([qkv_weights, packed_bias], axis=0)
    first, second = gather_halves(packed, 0)
    packed_x = ordered(first, second, y_bit, 0)
    w_output_x = swap(w_output, "heads", 2)
    inner_x = gather_halves(w_inner, 1)
    outer_x = gather_halves(w_outer, 0)
    w_output_mine = jnp.concatenate([w_output, w_output_x], axis=0)
    w_output_other = swap(w_output_mine, "heads", 1)

    qkv_weights_x = packed_x[: 3 * width]
    bias_x = packed_x[3 * width]
    b_inner_x = packed_x[3 * width + 1]
    b_inner_x = jnp.where(y_bit == 0, b_inner_x, jnp.roll(b_inner_x, units // 2))
    parts = (
        (qkv_weights, b_query, b_value, flags_of(hid)),
        (qkv_weights_x, bias_x[:width], bias_x[width : 2 * width], flags_of(hid ^ 2)),
    )
    ffn_parts = (
        (w_inner, b_inner, w_outer),
        (inner_x[0], b_inner_x[: units // 2], outer_x[0]),
        (inner_x[1], b_inner_x[units // 2 :], outer_x[1]),
    )

    tokens = jnp.concatenate([tokens_in, other_tokens], axis=0)
    kept = []
    for weights, bias_q, bias_v, flags in parts:
        projected = dot_nt(tokens, weights)
        queries = (projected[:, :width] + bias_q.astype(f32)).astype(bf16)
        keys = projected[:, width : 2 * width].astype(bf16)
        values = (projected[:, 2 * width :] + bias_v.astype(f32)).astype(bf16)
        mixed, lse = attend_forward(flags, queries, keys, values)
        kept.append((queries, keys, values, lse, mixed))
    attended = jnp.concatenate([kept[0][4], kept[1][4]], axis=1)
    other_attended = swap(attended[rows:], "heads", 1)
    projected = dot_nn(attended[:rows], w_output_mine) + dot_nn(other_attended, w_output_other)
    hidden_one = tokens_in.astype(f32) + projected + b_output.astype(f32)
    gain1 = norm1_gain.astype(f32)
    gain2 = norm2_gain.astype(f32)
    normed, zhat_one, rinv_one = norm_rows(hidden_one, gain1, norm1_shift.astype(f32))

    normed_bf = normed.astype(bf16)
    normed_all = jnp.concatenate([normed_bf, swap(normed_bf, "heads", 1)], axis=0)
    ffn = None
    active = []
    slopes = []
    for inner_w, inner_b, outer_w in ffn_parts:
        inner = dot_nn(normed_all, inner_w) + inner_b.astype(f32)
        value, slope = gelu_parts(inner)
        active.append(value.astype(bf16))
        slopes.append(slope.astype(bf16))
        term = dot_nn(active[-1], outer_w)
        ffn = term if ffn is None else ffn + term
    other_ffn = swap(ffn[rows:].astype(bf16), "heads", 1)
    hidden_two = normed + ffn[:rows] + other_ffn.astype(f32) + b_outer.astype(f32)
    result, zhat_two, rinv_two = norm_rows(hidden_two, gain2, norm2_shift.astype(f32))
    block_out = result.astype(bf16)

    grad_out = cotangent.astype(f32)
    grad_gain2 = jnp.sum(grad_out * zhat_two, axis=0)
    grad_shift2 = jnp.sum(grad_out, axis=0)
    grad_two = norm_back(grad_out * gain2, zhat_two, rinv_two)
    grad_b_outer = jnp.sum(grad_two, axis=0)
    grad_two_bf = grad_two.astype(bf16)
    grad_two_all = jnp.concatenate([grad_two_bf, swap(grad_two_bf, "heads", 1)], axis=0)

    outer_grads = [dot_tn(active[i], grad_two_all).astype(bf16) for i in (2, 1, 0)][::-1]
    grad_w_outer = reduce_gradient(outer_grads[0], outer_grads[1], outer_grads[2], 0)

    grad_inner = []
    for i in range(3):
        grad_active = dot_nt(grad_two_all, ffn_parts[i][2])
        grad_inner.append((grad_active * slopes[i].astype(f32)).astype(bf16))
    inner_grads = [dot_tn(normed_all, grad_inner[i]).astype(bf16) for i in (2, 1, 0)][::-1]
    grad_w_inner = reduce_gradient(inner_grads[0], inner_grads[1], inner_grads[2], 1)
    inner_sums = [jnp.sum(grad_inner[i], axis=0, dtype=f32) for i in range(3)]
    back = sum(dot_nt(grad_inner[i], ffn_parts[i][0]) for i in range(3))
    other_back = swap(back[rows:].astype(bf16), "heads", 1)
    grad_normed = grad_two + back[:rows] + other_back.astype(f32)

    grad_gain1 = jnp.sum(grad_normed * zhat_one, axis=0)
    grad_shift1 = jnp.sum(grad_normed, axis=0)
    grad_one = norm_back(grad_normed * gain1, zhat_one, rinv_one)
    grad_b_output = jnp.sum(grad_one, axis=0)
    grad_one_bf = grad_one.astype(bf16)
    grad_one_all = jnp.concatenate([grad_one_bf, swap(grad_one_bf, "heads", 1)], axis=0)

    grad_attended = dot_nt(grad_one_all, w_output_mine).astype(bf16)
    grad_w_output = dot_tn(attended, grad_one_all).astype(bf16)
    grad_rows = []
    for number, (weights, bias_q, bias_v, flags) in enumerate(parts):
        queries, keys, values, lse, _ = kept[number]
        grads = grad_attended[:, number * width : (number + 1) * width]
        grad_rows.append(
            jnp.concatenate(attend_backward(flags, queries, keys, values, grads, lse), axis=1)
        )
    attn_grads = [
        jnp.concatenate(
            [
                grad_w_output[number * width : (number + 1) * width],
                dot_tn(grad_rows[number], tokens).astype(bf16),
            ],
            axis=0,
        )
        for number in range(2)
    ]
    grad_attn = reduce_gradient(
        attn_grads[0],
        piece(attn_grads[1], y_bit, 0),
        piece(attn_grads[1], 1 - y_bit, 0),
        0,
    )
    qkv_sums = [jnp.sum(grad_rows[i], axis=0, dtype=f32) for i in range(2)]

    input_terms = dot_nn(grad_rows[0], qkv_weights) + dot_nn(grad_rows[1], qkv_weights_x)
    other_terms = swap(input_terms[rows:].astype(bf16), "heads", 1)
    grad_tokens = grad_one + input_terms[:rows] + other_terms.astype(f32)

    row_sums = jnp.stack(
        [grad_b_output, grad_gain1, grad_shift1, grad_b_outer, grad_gain2, grad_shift2]
    )
    row_sums = row_sums + swap(row_sums, "heads", 1)
    inner_sum_x = jnp.concatenate(inner_sums[1:])
    inner_sum_x = jnp.where(y_bit == 0, inner_sum_x, jnp.roll(inner_sum_x, units // 2))
    vectors = jnp.concatenate([row_sums.reshape(-1), inner_sums[0], qkv_sums[0]])
    vectors_x = jnp.concatenate([row_sums.reshape(-1), inner_sum_x, qkv_sums[1]])
    vectors = vectors + swap(vectors_x, "heads", 2)
    stride = 1
    while stride < lax.axis_size("batch"):
        vectors = vectors + swap(vectors, "batch", stride)
        stride *= 2
    row_sums = vectors[: 6 * model].reshape(6, model)
    grad_b_inner = vectors[6 * model : 6 * model + units]
    qkv_sum = vectors[6 * model + units :]

    return (
        block_out,
        grad_tokens,
        grad_attn[width : 2 * width],
        qkv_sum[:width],
        grad_attn[2 * width : 3 * width],
        grad_attn[3 * width :],
        qkv_sum[2 * width :],
        grad_attn[:width],
        row_sums[0],
        row_sums[1],
        row_sums[2],
        grad_w_inner,
        grad_b_inner,
        grad_w_outer,
        row_sums[3],
        row_sums[4],
        row_sums[5],
    )


def solution(mesh):
    placed = (
        P(("batch", "heads"), None),
        P(("batch", "heads"), None),
        P("batch"),
        P(),
        P("heads", None),
        P("heads"),
        P("heads", None),
        P("heads", None),
        P("heads"),
        P("heads", None),
        P(),
        P(),
        P(),
        P(None, "heads"),
        P("heads"),
        P("heads", None),
        P(),
        P(),
        P(),
    )
    return jax.shard_map(
        body,
        mesh=mesh,
        in_specs=placed,
        out_specs=(
            P(("batch", "heads"), None),
            P(("batch", "heads"), None),
            P("heads", None),
            P("heads"),
            P("heads", None),
            P("heads", None),
            P("heads"),
            P("heads", None),
            P(),
            P(),
            P(),
            P(None, "heads"),
            P("heads"),
            P("heads", None),
            P(),
            P(),
            P(),
        ),
        check_vma=False,
    )
```

```python
import functools

import jax
import jax.numpy as jnp
from jax import lax
from jax.experimental import pallas as pl
from jax.experimental.pallas import tpu as pltpu
from jax.sharding import PartitionSpec as P

HEAD_DIM = 64
HALF = 1024
SCALE = HEAD_DIM ** (-0.5)
epsilon = 1e-06

bf16 = jnp.bfloat16
f32 = jnp.float32


def dot_nn(left, right):
    return jnp.dot(left, right, preferred_element_type=f32)


def dot_nt(left, right):
    return lax.dot_general(left, right, (((1,), (1,)), ((), ())), preferred_element_type=f32)


def flip(value):
    return value.astype(f32).T.astype(bf16)


def swap(value, axis, stride):
    size = lax.axis_size(axis)
    pairs = [(i, i ^ stride) for i in range(size)]
    return jax.tree.map(lambda part: lax.ppermute(part, axis, pairs), value)


def row(ref):
    return ref[...].reshape(1, -1).astype(f32)


VMEM_SPEC = pl.BlockSpec(memory_space=pltpu.VMEM)
SMEM_SPEC = pl.BlockSpec(memory_space=pltpu.SMEM)
ANY_SPEC = pl.BlockSpec(memory_space=pl.ANY)
HBM_SPEC = pl.BlockSpec(memory_space=pltpu.HBM)


CHUNKS = 4


def chunked(rows, cols, dtype):
    return [((rows // CHUNKS, cols), dtype)] * CHUNKS


def whole(refs):
    return jnp.concatenate([ref[...] for ref in refs], axis=0)


def put(refs, value):
    rows = refs[0].shape[0]
    for number, ref in enumerate(refs):
        ref[...] = value[number * rows : (number + 1) * rows].astype(ref.dtype)


def after(value, *others):
    return lax.optimization_barrier((value, others))[0]


class Order:
    def __init__(self):
        self.last = None

    def call(self, kernel, scalars, inputs, outputs, **options):
        ins, tree = jax.tree.flatten(list(inputs))
        if self.last is not None:
            ins[0] = after(ins[0], self.last)
        results = call(kernel, scalars, jax.tree.unflatten(tree, ins), outputs, **options)
        self.last = min(jax.tree.leaves(results), key=lambda part: part.size)
        return results


def call(kernel, scalars, inputs, outputs, scratch=(), mib=12, name=None, remote=0, far=False):
    ins, in_tree = jax.tree.flatten(list(inputs))
    outs, out_tree = jax.tree.flatten(
        list(outputs), is_leaf=lambda entry: isinstance(entry, tuple)
    )
    out_shape = tuple(jax.ShapeDtypeStruct(shape, dtype) for shape, dtype in outs)
    near = len(ins) - remote
    first, second = len(scalars) + len(ins), len(scalars) + len(ins) + len(outs)

    def run(*refs):
        given = jax.tree.unflatten(in_tree, refs[len(scalars) : first])
        made = jax.tree.unflatten(out_tree, refs[first:second])
        kernel(*refs[: len(scalars)], *given, *made, *refs[second:])

    results = pl.pallas_call(
        run,
        out_shape=out_shape,
        in_specs=[SMEM_SPEC] * len(scalars) + [VMEM_SPEC] * near + [HBM_SPEC] * remote,
        out_specs=(ANY_SPEC if far else VMEM_SPEC,) * len(out_shape),
        scratch_shapes=list(scratch),
        compiler_params=pltpu.CompilerParams(vmem_limit_bytes=mib * 1024 * 1024),
        cost_estimate=pl.CostEstimate(flops=1000, bytes_accessed=1000, transcendentals=0),
        name=name,
    )(*scalars, *ins[:near], *(pltpu.with_memory_space_constraint(x, pltpu.HBM) for x in ins[near:]))
    return jax.tree.unflatten(out_tree, results)


def pack_attention_kernel(ids, wq, wk, wv, wo, out, sems):
    half = wq.shape[0] // 2
    at = pl.multiple_of(ids[1] * half, 16)
    copies = [
        pltpu.make_async_copy(
            weights.at[pl.ds(at, half), :],
            out.at[number * half : (number + 1) * half, :],
            sems.at[number],
        )
        for number, weights in enumerate((wq, wk, wv, wo))
    ]
    for copy in copies:
        copy.start()
    for copy in copies:
        copy.wait()


def vectors_kernel(bq, bv, bi, bo, gain1, shift1, bo2, gain2, shift2, table, lines):
    rows = [row(ref) for ref in (bo, gain1, shift1, bo2, gain2, shift2, bi)]
    heads = jnp.concatenate([row(bq), row(bv)], axis=1)
    half = lines.shape[1]
    table[...] = jnp.concatenate(
        rows + [jnp.concatenate([heads, jnp.zeros_like(heads)], axis=1)], axis=0
    )
    lines[...] = jnp.concatenate(
        [heads, rows[6][:, :half], rows[6][:, half:], jnp.zeros((13, half), f32)], axis=0
    ).astype(bf16)


def pack_ffn_kernel(ids, lines, wi, wo, out_inner, out_outer, sems):
    model, half = wi.shape[0], wo.shape[0] // 2
    copies = [
        pltpu.make_async_copy(
            wi.at[:, pl.ds(pl.multiple_of(ids[2] * half, 128), half)],
            out_inner.at[:model, :],
            sems.at[0],
        ),
        pltpu.make_async_copy(
            wo.at[pl.ds(pl.multiple_of(ids[1] * half, 128), half), :], out_outer, sems.at[1]
        ),
        pltpu.make_async_copy(lines, out_inner.at[model:, :], sems.at[2]),
    ]
    for copy in copies:
        copy.start()
    for copy in copies:
        copy.wait()


def attend_blocks(ids, lengths, perm, owner, visit):
    is_long = lengths[ids[0] // 2] == HALF
    swaps = [perm[owner * 3 + head, 0] for head in range(3)]

    @pl.when(is_long)
    def _():
        for block in range(2):
            for head in range(3):
                visit(head, block * 512, (block ^ swaps[head]) * 512, 512)

    @pl.when(jnp.logical_not(is_long))
    def _():
        for block in range(4):
            for head in range(3):
                visit(head, block * 256, (block ^ swaps[head]) * 256, 256)


def attend_forward(ids, lengths, perm, owner, q_ref, k_ref, v_ref, lse_ref, mixed, mixed_t):
    def visit(head, q_at, k_at, size):
        cols = slice(head * HEAD_DIM, (head + 1) * HEAD_DIM)
        q_rows = pl.ds(q_at, size)
        k_rows = pl.ds(pl.multiple_of(k_at, 256), size)
        queries = q_ref[q_rows, cols] * SCALE
        keys = k_ref[k_rows, cols]
        values_t = flip(v_ref[k_rows, cols])
        scores_t = dot_nt(keys, queries.astype(bf16))
        top = jnp.max(scores_t, axis=0, keepdims=True)
        weights_t = jnp.exp(scores_t - top)
        total = jnp.sum(weights_t, axis=0, keepdims=True)
        out_t = dot_nn(values_t, weights_t.astype(bf16)) * (1.0 / total)
        mixed_t[cols, q_rows] = out_t.astype(bf16)
        mixed[q_rows, cols] = out_t.T.astype(bf16)
        lse_ref[head : head + 1, q_rows] = top + jnp.log(total)

    attend_blocks(ids, lengths, perm, owner, visit)


def project_qkv(tok_a, tok_b, weights, biases, outs):
    rows = tok_a.shape[0]
    for block, tok in enumerate((tok_a, tok_b)):
        at = slice(block * rows, (block + 1) * rows)
        for weight, bias, out in zip(weights, biases, outs):
            product = dot_nt(tok[...], weight[...])
            out[at, :] = (product if bias is None else product + bias).astype(bf16)


def fetch(sources, targets, sems):
    copies = [
        pltpu.make_async_copy(source, target, sems.at[number])
        for number, (source, target) in enumerate(zip(sources, targets))
    ]
    for copy in copies:
        copy.start()
    return copies


def attention_own_kernel(
    ids, lengths, perm, tok_a, tok_b, table, wq_far, wk_far, wv_far, wo_far,
    q, k, v, lse, mixed_t, part, mixed, wq, wk, wv, wo, sems,
):
    copies = fetch((wq_far, wk_far, wv_far, wo_far), (wq, wk, wv, wo), sems)
    for copy in copies:
        copy.wait()
    width = q.shape[1]
    biases = (table[7:8, :width], None, table[7:8, width : 2 * width])
    project_qkv(tok_a, tok_b, (wq, wk, wv), biases, (q, k, v))
    attend_forward(ids, lengths, perm, ids[0], q, k, v, lse, mixed, mixed_t)
    part[...] = dot_nn(mixed[...], wo[...])


def attention_other_kernel(
    ids, lengths, perm, tok_a, tok_b, first, second, lines, part,
    q, k, v, lse, mixed_t, wx, keep, send, mixed,
):
    width = q.shape[1]
    half = width // 2
    rows = keep.shape[0]
    mine = pl.multiple_of(ids[1] * half, 16)
    other = pl.multiple_of((1 - ids[1]) * half, 16)
    for number in range(4):
        wx[number, pl.ds(mine, half), :] = first[number * half : (number + 1) * half, :]
        wx[number, pl.ds(other, half), :] = second[number * half : (number + 1) * half, :]
    line = lines[-16:, :].astype(f32)[:1]
    biases = (line[:, :width], None, line[:, width : 2 * width])
    project_qkv(tok_a, tok_b, (wx.at[0], wx.at[1], wx.at[2]), biases, (q, k, v))
    attend_forward(ids, lengths, perm, ids[0] ^ 2, q, k, v, lse, mixed, mixed_t)
    keep[...] = part[:rows, :] + dot_nn(mixed[:rows, :], wx[3])
    put(send, part[rows:, :] + dot_nn(mixed[rows:, :], wx[3]))


def attend_backward_kernel(
    ids, lengths, perm, owner, q_ref, k_ref, v_ref, lse_ref, grads_ref,
    dq, dk, dv, dqt, dkt, dvt,
):
    def visit(head, q_at, k_at, size):
        cols = slice(head * HEAD_DIM, (head + 1) * HEAD_DIM)
        q_rows = pl.ds(q_at, size)
        k_rows = pl.ds(pl.multiple_of(k_at, 256), size)
        queries = (q_ref[q_rows, cols] * SCALE).astype(bf16)
        keys = k_ref[k_rows, cols]
        grads = grads_ref[q_rows, cols]
        scores_t = dot_nt(keys, queries)
        weights_t = jnp.exp(scores_t - lse_ref[head : head + 1, q_rows])
        grad_weights_t = dot_nt(v_ref[k_rows, cols], grads)
        delta = jnp.sum(weights_t * grad_weights_t, axis=0, keepdims=True)
        grad_scores_t = (weights_t * (grad_weights_t - delta)).astype(bf16)
        grad_v = dot_nn(weights_t.astype(bf16), grads)
        grad_k = dot_nn(grad_scores_t, queries)
        grad_q_t = dot_nn(flip(keys), grad_scores_t) * SCALE
        dv[k_rows, cols] = grad_v.astype(bf16)
        dk[k_rows, cols] = grad_k.astype(bf16)
        dq[q_rows, cols] = grad_q_t.T.astype(bf16)
        dvt[cols, k_rows] = grad_v.T.astype(bf16)
        dkt[cols, k_rows] = grad_k.T.astype(bf16)
        dqt[cols, q_rows] = grad_q_t.astype(bf16)

    attend_blocks(ids, lengths, perm, owner, visit)


def backward_attention(
    ids, lengths, perm, owner, g_a, g_b, wo, q, k, v, lse, dq, dk, dv, dqt, dkt, dvt, grads
):
    for at, g in row_blocks(g_a, g_b):
        grads[at, :] = dot_nt(g, wo).astype(bf16)
    attend_backward_kernel(
        ids, lengths, perm, owner, q, k, v, lse, grads, dq, dk, dv, dqt, dkt, dvt
    )


def row_sum(left_t):
    ones = jnp.ones((8, left_t.shape[1]), bf16)
    return dot_nt(ones, left_t)[:1]


def head_weight_grads(out, lefts, rights, vectors):
    width = lefts[0].shape[0]
    for number, (left, right) in enumerate(zip(lefts, rights)):
        out[number * width : (number + 1) * width, :] = dot_nn(left[...], right).astype(bf16)
    vectors = jnp.concatenate([vectors, jnp.zeros_like(vectors)], axis=0)
    out[len(lefts) * width :, :] = vectors.astype(bf16)


def output_grad_kernel(mixed_t, g_a, g_b, out):
    out[...] = dot_nn(mixed_t[...], whole(g_a + g_b)).astype(bf16)


def bias_row(dqt, dvt):
    width = dqt.shape[0]
    return jnp.concatenate(
        [row_sum(dqt[...]), row_sum(dvt[...]), jnp.zeros((1, 2 * width), f32)], axis=1
    )


def attention_back_other_kernel(
    ids, lengths, perm, g_a, g_b, tok_a, tok_b, wx, q, k, v, lse, sums, got_sums,
    dq, dk, dv, out, dqt, dkt, dvt, grads,
):
    backward_attention(
        ids, lengths, perm, ids[0] ^ 2, g_a, g_b, wx[3], q, k, v, lse,
        dq, dk, dv, dqt, dkt, dvt, grads,
    )
    vectors = jnp.concatenate([sums[:7] + got_sums[:7], bias_row(dqt, dvt)], axis=0)
    tokens = whole([tok_a, tok_b])
    head_weight_grads(out, (dqt, dkt, dvt), (tokens,) * 3, vectors)


def attention_back_own_kernel(
    ids, lengths, perm, g_a, g_b, tok_a, tok_b, wo, q, k, v, lse, mixed_t, sums, got_sums, inner_sums,
    dq, dk, dv, out, dqt, dkt, dvt, grads,
):
    backward_attention(
        ids, lengths, perm, ids[0], g_a, g_b, wo[...], q, k, v, lse,
        dq, dk, dv, dqt, dkt, dvt, grads,
    )
    vectors = jnp.concatenate(
        [sums[:6] + got_sums[:6], inner_sums[:1], bias_row(dqt, dvt)], axis=0
    )
    tokens = whole([tok_a, tok_b])
    rights = (whole(g_a + g_b), tokens, tokens, tokens)
    head_weight_grads(out, (mixed_t, dqt, dkt, dvt), rights, vectors)


def token_grad_kernel(dq, dk, dv, wq, wk, wv, dqx, dkx, dvx, wx, grad_one, keep, send):
    rows = keep.shape[0]
    for at in (slice(rows, 2 * rows), slice(0, rows)):
        total = dot_nn(dq[at, :], wq[...]) + dot_nn(dk[at, :], wk[...])
        total += dot_nn(dv[at, :], wv[...]) + dot_nn(dqx[at, :], wx[0])
        total += dot_nn(dkx[at, :], wx[1]) + dot_nn(dvx[at, :], wx[2])
        if at.start:
            send[...] = total.astype(bf16)
        else:
            keep[...] = total + grad_one[...]


def normalize(hidden):
    center = jnp.mean(hidden, axis=1, keepdims=True)
    rinv = lax.rsqrt(jnp.mean(hidden * hidden, axis=1, keepdims=True) - center * center + epsilon)
    return (hidden - center) * rinv, rinv


def norm_back(grad_zhat, zhat, rinv):
    first_mean = jnp.mean(grad_zhat, axis=1, keepdims=True)
    second_mean = jnp.mean(grad_zhat * zhat, axis=1, keepdims=True)
    return rinv * (grad_zhat - first_mean - zhat * second_mean)


def norm_one_kernel(tokens, keep, got, table, hidden, normed, normed_all, normed_bf):
    value = tokens[...].astype(f32) + keep[...] + whole(got).astype(f32) + table[0:1, :]
    hidden[...] = value
    zhat, _ = normalize(value)
    result = zhat * table[1:2, :] + table[2:3, :]
    normed[...] = result
    normed_all[...] = result.astype(bf16)
    put(normed_bf, result)


def norm_two_kernel(
    normed, keep, got, table, cotangent,
    block_out, grad_two, grad_two_all, grad_two_bf, sums,
):
    hidden = normed[...] + keep[...] + whole(got).astype(f32) + table[3:4, :]
    zhat, rinv = normalize(hidden)
    block_out[...] = (zhat * table[4:5, :] + table[5:6, :]).astype(bf16)
    grad_out = cotangent[...].astype(f32)
    grad = norm_back(grad_out * table[4:5, :], zhat, rinv)
    grad_two[...] = grad
    grad_two_all[...] = grad.astype(bf16)
    put(grad_two_bf, grad)
    sums[...] = jnp.concatenate(
        [
            jnp.sum(grad, axis=0, keepdims=True),
            jnp.sum(grad_out * zhat, axis=0, keepdims=True),
            jnp.sum(grad_out, axis=0, keepdims=True),
            jnp.zeros((5, grad.shape[1]), f32),
        ],
        axis=0,
    )


def norm_one_back_kernel(grad_two, keep, got, hidden, table, sums_in, grad_one, grad_one_bf, sums):
    grad_normed = grad_two[...] + keep[...] + whole(got).astype(f32)
    zhat, rinv = normalize(hidden[...])
    grad = norm_back(grad_normed * table[1:2, :], zhat, rinv)
    grad_one[...] = grad
    put(grad_one_bf, grad)
    sums[...] = jnp.concatenate(
        [
            jnp.sum(grad, axis=0, keepdims=True),
            jnp.sum(grad_normed * zhat, axis=0, keepdims=True),
            jnp.sum(grad_normed, axis=0, keepdims=True),
            sums_in[:3],
            jnp.zeros((2, grad.shape[1]), f32),
        ],
        axis=0,
    )


def gelu_parts(values):
    size = jnp.abs(values)
    below = 1.0 + (0.3275911 * 0.7071067811865476) * size
    t = pl.reciprocal(below, approx=True)
    t = t * (2.0 - below * t)
    bell = jnp.exp(-0.5 * values * values)
    poly = t * (
        0.127414796
        + t * (-0.142248368 + t * (0.7107068705 + t * (-0.7265760135 + t * 0.5307027145)))
    )
    tail = poly * bell
    cdf = jnp.where(values < 0, tail, 1.0 - tail)
    return values * cdf, cdf + values * (bell * 0.3989422804014327)


BLOCK = 256


def row_blocks(first, second):
    at = 0
    for source in (first, second):
        step = max(1, BLOCK // source[0].shape[0])
        for start in range(0, len(source), step):
            block = whole(source[start : start + step])
            yield slice(at, at + block.shape[0]), block
            at += block.shape[0]


def feed_own_kernel(nrm_a, nrm_b, wi, table, wo, active_t, slope, part, normed_t):
    for at, normed in row_blocks(nrm_a, nrm_b):
        normed_t[:, at] = flip(normed)
        value, rise = gelu_parts(dot_nn(normed, wi[...]) + table[6:7, :])
        part[at, :] = dot_nn(value.astype(bf16), wo[...])
        active_t[:, at] = value.T.astype(bf16)
        slope[at, :] = rise.astype(bf16)


def feed_other_kernel(
    ids, nrm_a, nrm_b, wi_a, wi_b, wo_a, wo_b, part, slope, keep, send, wi_x, wo_x
):
    rows, half = keep.shape[0], wo_a.shape[0]
    model = keep.shape[1]
    for bit, weights in ((ids[2], wi_a), (1 - ids[2], wi_b)):
        wi_x[:, pl.ds(pl.multiple_of(bit * half, 128), half)] = weights[:model, :]
    for bit, weights in ((ids[1], wo_a), (1 - ids[1], wo_b)):
        wo_x[pl.ds(pl.multiple_of(bit * half, 128), half), :] = weights[...]
    line = wi_a[-16:, :].astype(f32)
    bias = jnp.concatenate([line[1:2], line[2:3]], axis=1)
    for at, normed in row_blocks(nrm_a, nrm_b):
        value, rise = gelu_parts(dot_nn(normed, wi_x[...]) + bias)
        slope[at, :] = rise.astype(bf16)
        total = part[at, :] + dot_nn(value.astype(bf16), wo_x[...])
        if at.start < rows:
            keep[at, :] = total
        else:
            size = send[0].shape[0]
            put(send[(at.start - rows) // size : (at.stop - rows) // size], total)


def feed_far_kernel(nrm_a, nrm_b, wi, table, active_t, slope, normed_t):
    for at, normed in row_blocks(nrm_a, nrm_b):
        normed_t[:, at] = flip(normed)
        value, rise = gelu_parts(dot_nn(normed, wi[...]) + table[6:7, :])
        active_t[:, at] = value.T.astype(bf16)
        slope[at, :] = rise.astype(bf16)


def feed_back_kernel(g_a, g_b, slope, slope_x, wi, wo, wi_x, wo_x, grad_inner, keep, send, grad_x):
    rows = keep.shape[0]
    for number, g in ((1, g_b), (0, g_a)):
        at = slice(number * rows, (number + 1) * rows)
        grad = whole(g)
        grad_inner[at, :] = (dot_nt(grad, wo[...]) * slope[at, :].astype(f32)).astype(bf16)
        grad_x[...] = (dot_nt(grad, wo_x[...]) * slope_x[at, :].astype(f32)).astype(bf16)
        total = dot_nt(grad_inner[at, :], wi[...]) + dot_nt(grad_x[...], wi_x[...])
        if number:
            put(send, total)
        else:
            keep[...] = total


def feed_weights_kernel(g_a, g_b, active_t, normed_t, grad_inner, outer, inner, sums):
    outer[...] = dot_nn(active_t[...], whole(g_a + g_b))
    inner[...] = dot_nn(normed_t[...], grad_inner[...])
    sums[...] = dot_nn(jnp.ones((8, grad_inner.shape[0]), bf16), grad_inner[...])


def feed_weights_far_kernel(
    ids, g_a, g_b, active_t, normed_t, slope, wo, outer, inner, sums_in,
    outer_keep, outer_send, inner_keep, inner_send, sums, grad_inner,
):
    for at, g in row_blocks(g_a, g_b):
        grad_inner[at, :] = (dot_nt(g, wo[...]) * slope[at, :].astype(f32)).astype(bf16)
    grads = whole(g_a + g_b)
    half = outer_keep.shape[0]
    for index, target in ((1 - ids[1], outer_send), (ids[1], outer_keep)):
        at = pl.ds(pl.multiple_of(index * half, 128), half)
        target[...] = (dot_nn(active_t[at, :], grads) + outer[at, :]).astype(target.dtype)
    for index, target in ((1 - ids[2], inner_send), (ids[2], inner_keep)):
        at = pl.ds(pl.multiple_of(index * half, 128), half)
        target[...] = (dot_nn(normed_t[at, :], grad_inner[...]) + inner[at, :]).astype(
            target.dtype
        )
    sums[...] = sums_in[...] + dot_nn(
        jnp.ones((8, grad_inner.shape[0]), bf16), grad_inner[...]
    )


Y_FIRST = (4, (0, 2, 1, 3))
Z_FIRST = (3, (0, 1, 2, 3))


def quarter_rows(ids, layout, number, rows):
    index, numbers = layout
    return pl.ds(pl.multiple_of((ids[index] ^ numbers[number]) * rows, 16), rows)


def add_heads_kernel(ids, own, got_first, got, keep, send):
    body = own.shape[0] - 16
    rows = body // 4
    line = (own[body:, :].astype(f32) + got[body - rows :, :].astype(f32)).astype(bf16)
    for number, part in enumerate([keep] + send):
        part[rows:, :] = line.astype(part.dtype)
    for quarter in range(4):
        ours = own[quarter * rows : (quarter + 1) * rows, :].astype(f32)
        theirs = got_first[...] if quarter == 0 else got[(quarter - 1) * rows : quarter * rows, :]
        total = ours + theirs.astype(f32)
        for number, part in enumerate([keep] + send):

            @pl.when((ids[3] ^ number) == quarter)
            def _():
                part[:rows, :] = total.astype(part.dtype)


def halve_kernel(which, ids, kept, got, keep, send):
    half = keep.shape[0]
    bit = ids[which]
    for index, target in ((1 - bit, send), (bit, keep)):
        at = pl.ds(pl.multiple_of(index * half, 16), half)
        target[...] = (kept[at, :] + got[at, :].astype(f32)).astype(target.dtype)


def add_four_kernel(extra, ids, keep, got, out, *scratch):
    rows = keep.shape[0] - extra
    total = keep[:rows, :]
    for part in got:
        total += part[:rows, :].astype(f32)
    out[:rows, :] = total.astype(bf16)
    if extra:
        for number, part in enumerate([keep] + got):
            scratch[0][ids[3] ^ number] = part[rows:, :].astype(f32)
        parts = [scratch[0][number] for number in range(4)]
        out[rows:, :] = (parts[0] + parts[1] + parts[2] + parts[3]).astype(bf16)


def add_two_kernel(kept, got, out):
    out[...] = (kept[...].astype(f32) + got[...].astype(f32)).astype(bf16)


def add_last_kernel(kept, got, out, vectors):
    rows = out.shape[0]
    total = kept[...].astype(f32) + got[...].astype(f32)
    out[...] = total[:rows, :].astype(bf16)
    vectors[...] = total[rows:, :]


def token_out_kernel(kept, got, out):
    out[...] = kept[...] + got[...].astype(f32)


class Group:
    def __init__(self, order, ids, name, extra, keep):
        self.order, self.ids, self.name, self.extra = order, ids, name, extra
        self.keep = keep

    def spread(self, parts):
        return [swap(part, "batch", number) for number, part in enumerate(parts, 1)]

    def halve(self, bit):
        rows, cols = self.keep.shape
        self.keep, send = self.order.call(
            functools.partial(halve_kernel, bit),
            (self.ids,),
            (self.keep, self.got),
            [((rows // 2, cols), f32), ((rows // 2, cols), bf16)],
            name=self.name + "_halve",
        )
        self.got = swap(send, "batch", bit)

    def quarter(self, parts=2):
        four = parts == 4
        (self.keep,) = self.order.call(
            functools.partial(add_four_kernel, self.extra) if four else add_two_kernel,
            (self.ids,) if four else (),
            (self.keep, self.got),
            [(self.keep.shape, bf16)],
            scratch=[pltpu.VMEM((4, self.extra, self.keep.shape[1]), f32)] if four else [],
            name=self.name + "_quarter",
        )
        stride = 4
        while 2 * stride < lax.axis_size("batch"):
            (self.keep,) = self.order.call(
                add_two_kernel,
                (),
                (self.keep, swap(self.keep, "batch", stride)),
                [(self.keep.shape, bf16)],
                name=self.name + "_%d" % stride,
            )
            stride *= 2
        self.got = swap(self.keep, "batch", stride)

    def finish(self):
        rows, cols = self.keep.shape
        outputs = [((rows - self.extra, cols), bf16)]
        if self.extra:
            outputs.append(((self.extra, cols), f32))
        results = self.order.call(
            add_last_kernel if self.extra else add_two_kernel,
            (),
            (self.keep, self.got),
            outputs,
            name=self.name + "_finish",
        )
        self.vectors = results[-1]
        self.pieces = [results[0]] + self.spread([results[0]] * 3)


def place_kernel(layout, ids, pieces, out):
    rows = pieces[0].shape[0]
    for number, part in enumerate(pieces):
        out[quarter_rows(ids, layout, number, rows), :] = part[...].astype(f32)


def place_heads_kernel(ids, pieces, vectors, grads, lines, biases, scratch):
    for number, part in enumerate(pieces):
        scratch[ids[3] ^ number] = part[...].astype(f32)
    for number, out in enumerate(grads):
        out[...] = scratch[number]
    for number, out in enumerate(lines):
        out[...] = vectors[number : number + 1, :].reshape(out.shape)
    for number, out in enumerate(biases):
        width = out.shape[0]
        line = vectors[7:8, number * width : (number + 1) * width]
        out[...] = line.reshape(out.shape)


def body(
    tokens_in,
    cotangent,
    half_length,
    block_perm,
    w_query,
    b_query,
    w_key,
    w_value,
    b_value,
    w_output,
    b_output,
    norm1_gain,
    norm1_shift,
    w_inner,
    b_inner,
    w_outer,
    b_outer,
    norm2_gain,
    norm2_shift,
):
    width = w_query.shape[0]
    model = w_query.shape[1]
    units = w_outer.shape[0]
    rows = tokens_in.shape[0]
    both = 2 * rows
    half = model // 2
    index = lax.axis_index("batch")
    ids = jnp.stack(
        [
            lax.axis_index("heads"),
            index & 1,
            (index >> 1) & 1,
            index & 3,
            (index & 1) * 2 + ((index >> 1) & 1),
        ]
    ).astype(jnp.int32)
    scalars = (ids, half_length, block_perm)
    order = Order()

    (packed,) = order.call(
        pack_attention_kernel,
        (ids,),
        (w_query, w_key, w_value, w_output),
        [((2 * width, model), bf16)],
        scratch=[pltpu.SemaphoreType.DMA((4,))],
        name="pack_attention",
        remote=4,
        far=True,
    )
    first = swap(packed, "heads", 2)
    other_tokens = swap(tokens_in, "heads", 1)
    table, lines = order.call(
        vectors_kernel,
        (),
        (
            b_query,
            b_value,
            b_inner,
            b_output,
            norm1_gain,
            norm1_shift,
            b_outer,
            norm2_gain,
            norm2_shift,
        ),
        [((8, model), f32), ((16, half), bf16)],
        name="vectors",
    )
    inner_half, outer_half = order.call(
        pack_ffn_kernel,
        (ids,),
        (lines, w_inner, w_outer),
        [((model + 16, units // 2), bf16), ((units // 2, model), bf16)],
        scratch=[pltpu.SemaphoreType.DMA((3,))],
        name="pack_ffn",
        remote=2,
    )
    inner_a = swap(inner_half, "heads", 2)
    outer_a = swap(outer_half, "heads", 2)
    second = swap(first, "batch", 1)
    inner_b = swap(inner_a, "batch", 2)
    outer_b = swap(outer_a, "batch", 1)

    head_outputs = [
        ((both, width), bf16),
        ((both, width), bf16),
        ((both, width), bf16),
        ((8, both), f32),
        ((width, both), bf16),
    ]
    mixed = pltpu.VMEM((both, width), bf16)
    q, k, v, lse, mixed_t, part = order.call(
        attention_own_kernel,
        scalars,
        (tokens_in, other_tokens, table, w_query, w_key, w_value, w_output),
        head_outputs + [((both, model), f32)],
        scratch=[mixed]
        + [pltpu.VMEM((width, model), bf16)] * 4
        + [pltpu.SemaphoreType.DMA((4,))],
        name="attention_own",
        remote=4,
    )
    qx, kx, vx, lse_x, mixed_tx, wx, keep, send = order.call(
        attention_other_kernel,
        scalars,
        (tokens_in, other_tokens, first, after(second, inner_a), inner_a, part),
        head_outputs
        + [((4, width, model), bf16), ((rows, model), f32), chunked(rows, model, bf16)],
        scratch=[mixed],
        name="attention_other",
    )
    hidden_one, normed, normed_all, normed_bf = order.call(
        norm_one_kernel,
        (),
        (
            tokens_in,
            keep,
            after(swap(send, "heads", 1), outer_a),
            table,
        ),
        [
            ((rows, model), f32),
            ((rows, model), f32),
            ((rows, model), bf16),
            chunked(rows, model, bf16),
        ],
        name="norm_one",
    )

    other_normed = swap(normed_bf, "heads", 1)
    far_normed = swap([normed_all], "heads", 2)
    active_t, slope, part, normed_t = order.call(
        feed_own_kernel,
        (),
        (normed_bf, other_normed, w_inner, table, w_outer),
        [
            ((units, both), bf16),
            ((both, units), bf16),
            ((both, model), f32),
            ((model, both), bf16),
        ],
        name="feed_own",
    )
    slope_x, keep, send, wi_x, wo_x = order.call(
        feed_other_kernel,
        (ids,),
        (normed_bf, other_normed, inner_a, inner_b, outer_a, outer_b, part),
        [
            ((both, units), bf16),
            ((rows, model), f32),
            chunked(rows, model, bf16),
            ((model, units), bf16),
            ((units, model), bf16),
        ],
        name="feed_other",
    )
    far_normed = after(far_normed, keep)
    far_other_normed = swap(far_normed, "heads", 1)
    block_out, grad_two, grad_two_all, grad_two_bf, sums_two = order.call(
        norm_two_kernel,
        (),
        (
            normed,
            keep,
            after(swap(send, "heads", 1), far_normed),
            table,
            cotangent,
        ),
        [
            ((rows, model), bf16),
            ((rows, model), f32),
            ((rows, model), bf16),
            chunked(rows, model, bf16),
            ((8, model), f32),
        ],
        name="norm_two",
    )

    other_grad_two = swap(grad_two_bf, "heads", 1)
    far_grad_two = swap([grad_two_all], "heads", 2)
    active_f, slope_f, normed_f = order.call(
        feed_far_kernel,
        (),
        (far_normed, far_other_normed, w_inner, table),
        [((units, both), bf16), ((both, units), bf16), ((model, both), bf16)],
        name="feed_far",
    )
    grad_inner, keep, send = order.call(
        feed_back_kernel,
        (),
        (grad_two_bf, other_grad_two, slope, slope_x, w_inner, w_outer, wi_x, wo_x),
        [((both, units), bf16), ((rows, model), f32), chunked(rows, model, bf16)],
        scratch=[pltpu.VMEM((rows, units), bf16)],
        name="feed_back",
    )
    outer_part, inner_part, part_sums = order.call(
        feed_weights_kernel,
        (),
        (grad_two_bf, other_grad_two, active_t, normed_t, grad_inner),
        [((units, model), f32), ((model, units), f32), ((8, units), f32)],
        name="feed_weights",
    )
    grad_one, grad_one_bf, sums_one = order.call(
        norm_one_back_kernel,
        (),
        (grad_two, keep, swap(send, "heads", 1), hidden_one, table, sums_two),
        [((rows, model), f32), chunked(rows, model, bf16), ((8, model), f32)],
        name="norm_one_back",
    )

    grads_one = (grad_one_bf, swap(grad_one_bf, "heads", 1))
    row_sums = (sums_one, swap(sums_one, "heads", 1))
    head_grads = [((both, width), bf16)] * 3
    group = [((4 * width + 16, model), bf16)]
    head_scratch = [pltpu.VMEM((width, both), bf16)] * 3 + [pltpu.VMEM((both, width), bf16)]
    (far_output,) = order.call(
        output_grad_kernel,
        (),
        (mixed_tx, *grads_one),
        [((width, model), bf16)],
        name="output_grad_other",
    )
    got_output = swap(far_output, "heads", 2)
    dqx, dkx, dvx, far_heads = order.call(
        attention_back_other_kernel,
        scalars,
        (*grads_one, tokens_in, other_tokens, wx, qx, kx, vx, lse_x, *row_sums),
        head_grads + [((3 * width + 16, model), bf16)],
        scratch=head_scratch,
        name="attention_back_other",
    )
    got_heads = swap(far_heads, "heads", 2)

    far_grad_two = after(far_grad_two, far_heads)
    far_other_grad_two = swap(far_grad_two, "heads", 1)
    halves = [((units // 2, model), f32), ((units // 2, model), bf16)]
    outer_keep, outer_send, inner_keep, inner_send, inner_sums = order.call(
        feed_weights_far_kernel,
        (ids,),
        (
            far_grad_two,
            far_other_grad_two,
            active_f,
            normed_f,
            slope_f,
            w_outer,
            outer_part,
            inner_part,
            part_sums,
        ),
        halves + halves + [((8, units), f32)],
        scratch=[pltpu.VMEM((both, units), bf16)],
        name="feed_weights_far",
    )
    outer = Group(order, ids, "outer", 0, outer_keep)
    outer.got = swap(outer_send, "batch", 1)
    inner = Group(order, ids, "inner", 0, inner_keep)
    inner.got = swap(inner_send, "batch", 2)

    dq, dk, dv, own_heads = order.call(
        attention_back_own_kernel,
        scalars,
        (
            *grads_one,
            tokens_in,
            other_tokens,
            w_output,
            q,
            k,
            v,
            lse,
            mixed_t,
            *row_sums,
            inner_sums,
        ),
        head_grads + group,
        scratch=head_scratch,
        name="attention_back_own",
    )
    outer.halve(2)
    inner.halve(1)
    heads_keep, heads_send = order.call(
        add_heads_kernel,
        (ids,),
        (own_heads, got_output, got_heads),
        [((width + 16, model), f32), [((width + 16, model), bf16)] * 3],
        name="heads_add",
    )
    heads = Group(order, ids, "heads", 16, heads_keep)
    heads.got = heads.spread(heads_send)
    token_keep, token_send = order.call(
        token_grad_kernel,
        (),
        (dq, dk, dv, w_query, w_key, w_value, dqx, dkx, dvx, wx, grad_one),
        [((rows, model), f32), ((rows, model), bf16)],
        name="token_grad",
    )
    token_got = swap(token_send, "heads", 1)
    outer.quarter()
    inner.quarter()
    heads.quarter(4)
    outer.finish()
    inner.finish()
    (grad_w_outer,) = order.call(
        functools.partial(place_kernel, Y_FIRST),
        (ids,),
        (outer.pieces,),
        [((units, model), f32)],
        name="place_outer",
    )
    heads.finish()
    (grad_tokens,) = order.call(
        token_out_kernel, (), (token_keep, token_got), [((rows, model), f32)], name="token_out"
    )
    (grad_w_inner,) = order.call(
        functools.partial(place_kernel, Z_FIRST),
        (ids,),
        (inner.pieces,),
        [((model, units), f32)],
        name="place_inner",
    )
    (grad_o, grad_q, grad_k, grad_v), lines, biases = order.call(
        place_heads_kernel,
        (ids,),
        (heads.pieces, heads.vectors),
        [[((width, model), f32)] * 4, [((model,), f32)] * 7, [((width,), f32)] * 2],
        scratch=[pltpu.VMEM((4, width, model), f32)],
        name="place_heads",
    )

    return (
        block_out,
        grad_tokens,
        grad_q,
        biases[0],
        grad_k,
        grad_v,
        biases[1],
        grad_o,
        lines[0],
        lines[1],
        lines[2],
        grad_w_inner,
        lines[6],
        grad_w_outer,
        lines[3],
        lines[4],
        lines[5],
    )


def solution(mesh):
    placed = (
        P(("batch", "heads"), None),
        P(("batch", "heads"), None),
        P("batch"),
        P(),
        P("heads", None),
        P("heads"),
        P("heads", None),
        P("heads", None),
        P("heads"),
        P("heads", None),
        P(),
        P(),
        P(),
        P(None, "heads"),
        P("heads"),
        P("heads", None),
        P(),
        P(),
        P(),
    )
    return jax.shard_map(
        body,
        mesh=mesh,
        in_specs=placed,
        out_specs=(
            P(("batch", "heads"), None),
            P(("batch", "heads"), None),
            P("heads", None),
            P("heads"),
            P("heads", None),
            P("heads", None),
            P("heads"),
            P("heads", None),
            P(),
            P(),
            P(),
            P(None, "heads"),
            P("heads"),
            P("heads", None),
            P(),
            P(),
            P(),
        ),
        check_vma=False,
    )
```

```python
import functools

import jax
import jax.numpy as jnp
from jax import lax
from jax.experimental import pallas as pl
from jax.experimental.pallas import tpu as pltpu
from jax.sharding import PartitionSpec as P

HEAD_DIM = 64
HALF = 1024
SCALE = HEAD_DIM ** (-0.5)
epsilon = 1e-06

bf16 = jnp.bfloat16
f32 = jnp.float32


def dot_nn(left, right):
    return jnp.dot(left, right, preferred_element_type=f32)


def dot_nt(left, right):
    return lax.dot_general(left, right, (((1,), (1,)), ((), ())), preferred_element_type=f32)


def swap(value, axis, stride):
    size = lax.axis_size(axis)
    pairs = [(i, i ^ stride) for i in range(size)]
    return jax.tree.map(lambda part: lax.ppermute(part, axis, pairs), value)


def row(ref):
    return ref[...].reshape(1, -1).astype(f32)


VMEM_SPEC = pl.BlockSpec(memory_space=pltpu.VMEM)
SMEM_SPEC = pl.BlockSpec(memory_space=pltpu.SMEM)
ANY_SPEC = pl.BlockSpec(memory_space=pl.ANY)
HBM_SPEC = pl.BlockSpec(memory_space=pltpu.HBM)


PIECES = {"projected": 4, "normed": 4, "fed": 4, "grad_two": 4, "back": 4, "grad_one": 4}


def chunked(rows, cols, name):
    return [((rows // PIECES[name], cols), bf16)] * PIECES[name]


def whole(refs):
    return jnp.concatenate([ref[...] for ref in refs], axis=0)


def put(refs, value):
    rows = refs[0].shape[0]
    for number, ref in enumerate(refs):
        ref[...] = value[number * rows : (number + 1) * rows].astype(ref.dtype)


def after(value, *others):
    return lax.optimization_barrier((value, others))[0]


class Order:
    def __init__(self):
        self.last = None

    def call(self, kernel, scalars, inputs, outputs, **options):
        ins, tree = jax.tree.flatten(list(inputs))
        if self.last is not None:
            ins[0] = after(ins[0], self.last)
        results = call(kernel, scalars, jax.tree.unflatten(tree, ins), outputs, **options)
        self.last = min(jax.tree.leaves(results), key=lambda part: part.size)
        return results


def call(kernel, scalars, inputs, outputs, scratch=(), mib=12, name=None, remote=0, far=False):
    ins, in_tree = jax.tree.flatten(list(inputs))
    outs, out_tree = jax.tree.flatten(
        list(outputs), is_leaf=lambda entry: isinstance(entry, tuple)
    )
    out_shape = tuple(jax.ShapeDtypeStruct(shape, dtype) for shape, dtype in outs)
    near = len(ins) - remote
    first, second = len(scalars) + len(ins), len(scalars) + len(ins) + len(outs)

    def run(*refs):
        given = jax.tree.unflatten(in_tree, refs[len(scalars) : first])
        made = jax.tree.unflatten(out_tree, refs[first:second])
        kernel(*refs[: len(scalars)], *given, *made, *refs[second:])

    results = pl.pallas_call(
        run,
        out_shape=out_shape,
        in_specs=[SMEM_SPEC] * len(scalars) + [VMEM_SPEC] * near + [HBM_SPEC] * remote,
        out_specs=(ANY_SPEC if far else VMEM_SPEC,) * len(out_shape),
        scratch_shapes=list(scratch),
        compiler_params=pltpu.CompilerParams(vmem_limit_bytes=mib * 1024 * 1024),
        cost_estimate=pl.CostEstimate(flops=1000, bytes_accessed=1000, transcendentals=0),
        name=name,
    )(*scalars, *ins[:near], *(pltpu.with_memory_space_constraint(x, pltpu.HBM) for x in ins[near:]))
    return jax.tree.unflatten(out_tree, results)


def pack_attention_kernel(ids, wq, wk, wv, wo, out, sems):
    half = wq.shape[0] // 2
    at = pl.multiple_of(ids[1] * half, 16)
    copies = [
        pltpu.make_async_copy(
            weights.at[pl.ds(at, half), :],
            out.at[number * half : (number + 1) * half, :],
            sems.at[number],
        )
        for number, weights in enumerate((wq, wk, wv, wo))
    ]
    for copy in copies:
        copy.start()
    for copy in copies:
        copy.wait()


def vectors_kernel(bq, bv, bi, bo, gain1, shift1, bo2, gain2, shift2, table, lines):
    rows = [row(ref) for ref in (bo, gain1, shift1, bo2, gain2, shift2, bi)]
    heads = jnp.concatenate([row(bq), row(bv)], axis=1)
    half = lines.shape[1]
    table[...] = jnp.concatenate(
        rows + [jnp.concatenate([heads, jnp.zeros_like(heads)], axis=1)], axis=0
    )
    lines[...] = jnp.concatenate(
        [heads, rows[6][:, :half], rows[6][:, half:], jnp.zeros((13, half), f32)], axis=0
    ).astype(bf16)


def pack_ffn_kernel(ids, lines, wi, wo, out_inner, out_outer, sems):
    model, half = wi.shape[0], wo.shape[0] // 2
    copies = [
        pltpu.make_async_copy(
            wi.at[:, pl.ds(pl.multiple_of(ids[2] * half, 128), half)],
            out_inner.at[:model, :],
            sems.at[0],
        ),
        pltpu.make_async_copy(
            wo.at[pl.ds(pl.multiple_of(ids[1] * half, 128), half), :], out_outer, sems.at[1]
        ),
        pltpu.make_async_copy(lines, out_inner.at[model:, :], sems.at[2]),
    ]
    for copy in copies:
        copy.start()
    for copy in copies:
        copy.wait()


def attend_blocks(ids, lengths, perm, owner, visit):
    is_long = lengths[ids[0] // 2] == HALF
    swaps = [perm[owner * 3 + head, 0] for head in range(3)]

    @pl.when(is_long)
    def _():
        for block in range(2):
            for head in range(3):
                visit(head, block * 512, (block ^ swaps[head]) * 512, 512)

    @pl.when(jnp.logical_not(is_long))
    def _():
        for block in range(4):
            for head in range(3):
                visit(head, block * 256, (block ^ swaps[head]) * 256, 256)


def attend_forward(ids, lengths, perm, owner, q_ref, k_ref, v_ref, lse_ref, mixed, mixed_t):
    def visit(head, q_at, k_at, size):
        cols = slice(head * HEAD_DIM, (head + 1) * HEAD_DIM)
        q_rows = pl.ds(q_at, size)
        k_rows = pl.ds(pl.multiple_of(k_at, 256), size)
        queries = q_ref[q_rows, cols] * SCALE
        keys = k_ref[k_rows, cols]
        values_t = v_ref[k_rows, cols].T
        scores_t = dot_nt(keys, queries.astype(bf16))
        top = jnp.max(scores_t, axis=0, keepdims=True)
        weights_t = jnp.exp(scores_t - top)
        total = jnp.sum(weights_t, axis=0, keepdims=True)
        out_t = (dot_nn(values_t, weights_t.astype(bf16)) * (1.0 / total)).astype(bf16)
        mixed_t[cols, q_rows] = out_t
        mixed[q_rows, cols] = out_t.T
        lse_ref[head : head + 1, q_rows] = top + jnp.log(total)

    attend_blocks(ids, lengths, perm, owner, visit)


def project_qkv(tok_a, tok_b, weights, biases, outs):
    rows = tok_a.shape[0]
    for block, tok in enumerate((tok_a, tok_b)):
        at = slice(block * rows, (block + 1) * rows)
        for weight, bias, out in zip(weights, biases, outs):
            product = dot_nt(tok[...], weight[...])
            out[at, :] = (product if bias is None else product + bias).astype(bf16)


def fetch(sources, targets, sems):
    copies = [
        pltpu.make_async_copy(source, target, sems.at[number])
        for number, (source, target) in enumerate(zip(sources, targets))
    ]
    for copy in copies:
        copy.start()
    return copies


def attention_own_kernel(
    ids, lengths, perm, tok_a, tok_b, table, wq_far, wk_far, wv_far, wo_far,
    q, k, v, lse, mixed_t, part, mixed, wq, wk, wv, wo, sems,
):
    copies = fetch((wq_far, wk_far, wv_far, wo_far), (wq, wk, wv, wo), sems)
    for copy in copies:
        copy.wait()
    width = q.shape[1]
    biases = (table[7:8, :width], None, table[7:8, width : 2 * width])
    project_qkv(tok_a, tok_b, (wq, wk, wv), biases, (q, k, v))
    attend_forward(ids, lengths, perm, ids[0], q, k, v, lse, mixed, mixed_t)
    part[...] = dot_nn(mixed[...], wo[...])


def attention_other_kernel(
    ids, lengths, perm, tok_a, tok_b, first, second, lines, part,
    q, k, v, lse, mixed_t, wx, keep, send, mixed,
):
    width = q.shape[1]
    half = width // 2
    rows = keep.shape[0]
    mine = pl.multiple_of(ids[1] * half, 16)
    other = pl.multiple_of((1 - ids[1]) * half, 16)
    for number in range(4):
        wx[number, pl.ds(mine, half), :] = first[number * half : (number + 1) * half, :]
        wx[number, pl.ds(other, half), :] = second[number * half : (number + 1) * half, :]
    line = lines[-16:, :].astype(f32)[:1]
    biases = (line[:, :width], None, line[:, width : 2 * width])
    project_qkv(tok_a, tok_b, (wx.at[0], wx.at[1], wx.at[2]), biases, (q, k, v))
    attend_forward(ids, lengths, perm, ids[0] ^ 2, q, k, v, lse, mixed, mixed_t)
    keep[...] = part[:rows, :] + dot_nn(mixed[:rows, :], wx[3])
    put(send, part[rows:, :] + dot_nn(mixed[rows:, :], wx[3]))


def attend_backward_kernel(
    ids, lengths, perm, owner, q_ref, k_ref, v_ref, lse_ref, grads_ref,
    dq, dk, dv, dqt, dkt, dvt,
):
    def visit(head, q_at, k_at, size):
        cols = slice(head * HEAD_DIM, (head + 1) * HEAD_DIM)
        q_rows = pl.ds(q_at, size)
        k_rows = pl.ds(pl.multiple_of(k_at, 256), size)
        queries = (q_ref[q_rows, cols] * SCALE).astype(bf16)
        keys = k_ref[k_rows, cols]
        grads = grads_ref[q_rows, cols]
        scores_t = dot_nt(keys, queries)
        weights_t = jnp.exp(scores_t - lse_ref[head : head + 1, q_rows])
        grad_weights_t = dot_nt(v_ref[k_rows, cols], grads)
        delta = jnp.sum(weights_t * grad_weights_t, axis=0, keepdims=True)
        grad_scores_t = (weights_t * (grad_weights_t - delta)).astype(bf16)
        grad_v = dot_nn(weights_t.astype(bf16), grads).astype(bf16)
        grad_k = dot_nn(grad_scores_t, queries).astype(bf16)
        grad_q_t = (dot_nn(keys.T, grad_scores_t) * SCALE).astype(bf16)
        dv[k_rows, cols] = grad_v
        dk[k_rows, cols] = grad_k
        dq[q_rows, cols] = grad_q_t.T
        dvt[cols, k_rows] = grad_v.T
        dkt[cols, k_rows] = grad_k.T
        dqt[cols, q_rows] = grad_q_t

    attend_blocks(ids, lengths, perm, owner, visit)


def backward_attention(
    ids, lengths, perm, owner, g_a, g_b, wo, q, k, v, lse, dq, dk, dv, dqt, dkt, dvt, grads
):
    for at, g in row_blocks(g_a, g_b):
        grads[at, :] = dot_nt(g, wo).astype(bf16)
    attend_backward_kernel(
        ids, lengths, perm, owner, q, k, v, lse, grads, dq, dk, dv, dqt, dkt, dvt
    )


def row_sum(left_t):
    ones = jnp.ones((8, left_t.shape[1]), bf16)
    return dot_nt(ones, left_t)[:1]


def head_weight_grads(out, lefts, rights, vectors):
    width = lefts[0].shape[0]
    for number, (left, right) in enumerate(zip(lefts, rights)):
        out[number * width : (number + 1) * width, :] = dot_nn(left[...], right).astype(bf16)
    vectors = jnp.concatenate([vectors, jnp.zeros_like(vectors)], axis=0)
    out[len(lefts) * width :, :] = vectors.astype(bf16)


def bias_row(dqt, dvt):
    width = dqt.shape[0]
    return jnp.concatenate(
        [row_sum(dqt[...]), row_sum(dvt[...]), jnp.zeros((1, 2 * width), f32)], axis=1
    )


def attention_back_other_kernel(
    ids, lengths, perm, g_a, g_b, tok_a, tok_b, wx, q, k, v, lse, mixed_t, sums, got_sums,
    dq, dk, dv, out, dqt, dkt, dvt, grads,
):
    backward_attention(
        ids, lengths, perm, ids[0] ^ 2, g_a, g_b, wx[3], q, k, v, lse,
        dq, dk, dv, dqt, dkt, dvt, grads,
    )
    vectors = jnp.concatenate([sums[:7] + got_sums[:7], bias_row(dqt, dvt)], axis=0)
    tokens = whole([tok_a, tok_b])
    rights = (whole(g_a + g_b), tokens, tokens, tokens)
    head_weight_grads(out, (mixed_t, dqt, dkt, dvt), rights, vectors)


def attention_back_own_kernel(
    ids, lengths, perm, g_a, g_b, tok_a, tok_b, wo, q, k, v, lse, mixed_t, sums, got_sums, inner_sums,
    dq, dk, dv, out, dqt, dkt, dvt, grads,
):
    backward_attention(
        ids, lengths, perm, ids[0], g_a, g_b, wo[...], q, k, v, lse,
        dq, dk, dv, dqt, dkt, dvt, grads,
    )
    vectors = jnp.concatenate(
        [sums[:6] + got_sums[:6], inner_sums[:1], bias_row(dqt, dvt)], axis=0
    )
    tokens = whole([tok_a, tok_b])
    rights = (whole(g_a + g_b), tokens, tokens, tokens)
    head_weight_grads(out, (mixed_t, dqt, dkt, dvt), rights, vectors)


def token_grad_other_kernel(dq, dk, dv, wx, grad_one, out):
    rows = grad_one.shape[0]
    total = dot_nn(dq[...], wx[0]) + dot_nn(dk[...], wx[1]) + dot_nn(dv[...], wx[2])
    out[:rows, :] = total[:rows, :] + grad_one[...]
    out[rows:, :] = total[rows:, :]


def token_grad_own_kernel(dq, dk, dv, wq, wk, wv, part, keep, send):
    rows = keep.shape[0]
    total = dot_nn(dq[...], wq[...]) + dot_nn(dk[...], wk[...]) + dot_nn(dv[...], wv[...])
    send[...] = (part[rows:, :] + total[rows:, :]).astype(bf16)
    keep[...] = part[:rows, :] + total[:rows, :]


def normalize(hidden):
    center = jnp.mean(hidden, axis=1, keepdims=True)
    rinv = lax.rsqrt(jnp.mean(hidden * hidden, axis=1, keepdims=True) - center * center + epsilon)
    return (hidden - center) * rinv, rinv


def norm_back(grad_zhat, zhat, rinv):
    first_mean = jnp.mean(grad_zhat, axis=1, keepdims=True)
    second_mean = jnp.mean(grad_zhat * zhat, axis=1, keepdims=True)
    return rinv * (grad_zhat - first_mean - zhat * second_mean)


def norm_one_kernel(tokens, keep, got, table, hidden, normed, normed_all, normed_bf):
    value = tokens[...].astype(f32) + keep[...] + whole(got).astype(f32) + table[0:1, :]
    hidden[...] = value
    zhat, _ = normalize(value)
    result = zhat * table[1:2, :] + table[2:3, :]
    normed[...] = result
    normed_all[...] = result.astype(bf16)
    put(normed_bf, result)


def norm_two_kernel(
    normed, keep, got, table, cotangent,
    block_out, grad_two, grad_two_all, grad_two_bf, sums,
):
    hidden = normed[...] + keep[...] + whole(got).astype(f32) + table[3:4, :]
    zhat, rinv = normalize(hidden)
    block_out[...] = (zhat * table[4:5, :] + table[5:6, :]).astype(bf16)
    grad_out = cotangent[...].astype(f32)
    grad = norm_back(grad_out * table[4:5, :], zhat, rinv)
    grad_two[...] = grad
    grad_two_all[...] = grad.astype(bf16)
    put(grad_two_bf, grad)
    sums[...] = jnp.concatenate(
        [
            jnp.sum(grad, axis=0, keepdims=True),
            jnp.sum(grad_out * zhat, axis=0, keepdims=True),
            jnp.sum(grad_out, axis=0, keepdims=True),
            jnp.zeros((5, grad.shape[1]), f32),
        ],
        axis=0,
    )


def norm_one_back_kernel(grad_two, keep, got, hidden, table, sums_in, grad_one, grad_one_bf, sums):
    grad_normed = grad_two[...] + keep[...] + whole(got).astype(f32)
    zhat, rinv = normalize(hidden[...])
    grad = norm_back(grad_normed * table[1:2, :], zhat, rinv)
    grad_one[...] = grad
    put(grad_one_bf, grad)
    sums[...] = jnp.concatenate(
        [
            jnp.sum(grad, axis=0, keepdims=True),
            jnp.sum(grad_normed * zhat, axis=0, keepdims=True),
            jnp.sum(grad_normed, axis=0, keepdims=True),
            sums_in[:3],
            jnp.zeros((2, grad.shape[1]), f32),
        ],
        axis=0,
    )


def gelu_parts(values):
    cdf = 0.5 + 0.5 * lax.erf(values * 0.7071067811865476)
    bell = jnp.exp2((-0.5 * 1.4426950408889634) * (values * values))
    return values * cdf, cdf + values * (bell * 0.3989422804014327)


BLOCK = 256


def row_blocks(first, second):
    at = 0
    for source in (first, second):
        step = max(1, BLOCK // source[0].shape[0])
        for start in range(0, len(source), step):
            block = whole(source[start : start + step])
            yield slice(at, at + block.shape[0]), block
            at += block.shape[0]


def feed_own_kernel(nrm_a, nrm_b, wi, table, wo, active_t, slope, part, normed_t):
    for at, normed in row_blocks(nrm_a, nrm_b):
        normed_t[:, at] = normed.T
        value, rise = gelu_parts(dot_nn(normed, wi[...]) + table[6:7, :])
        part[at, :] = dot_nn(value.astype(bf16), wo[...])
        active_t[:, at] = value.astype(bf16).T
        slope[at, :] = rise.astype(bf16)


def feed_other_kernel(
    ids, nrm_a, nrm_b, wi_a, wi_b, wo_a, wo_b, part, slope, keep, send, wi_x, wo_x
):
    rows, half = keep.shape[0], wo_a.shape[0]
    model = keep.shape[1]
    for bit, weights in ((ids[2], wi_a), (1 - ids[2], wi_b)):
        wi_x[:, pl.ds(pl.multiple_of(bit * half, 128), half)] = weights[:model, :]
    for bit, weights in ((ids[1], wo_a), (1 - ids[1], wo_b)):
        wo_x[pl.ds(pl.multiple_of(bit * half, 128), half), :] = weights[...]
    line = wi_a[-16:, :].astype(f32)
    bias = jnp.concatenate([line[1:2], line[2:3]], axis=1)
    for at, normed in row_blocks(nrm_a, nrm_b):
        value, rise = gelu_parts(dot_nn(normed, wi_x[...]) + bias)
        slope[at, :] = rise.astype(bf16)
        total = part[at, :] + dot_nn(value.astype(bf16), wo_x[...])
        if at.start < rows:
            keep[at, :] = total
        else:
            size = send[0].shape[0]
            put(send[(at.start - rows) // size : (at.stop - rows) // size], total)


def feed_far_kernel(nrm_a, nrm_b, wi, table, active_t, slope, normed_t):
    for at, normed in row_blocks(nrm_a, nrm_b):
        normed_t[:, at] = normed.T
        value, rise = gelu_parts(dot_nn(normed, wi[...]) + table[6:7, :])
        active_t[:, at] = value.astype(bf16).T
        slope[at, :] = rise.astype(bf16)


def feed_back_kernel(g_a, g_b, slope, slope_x, wi, wo, wi_x, wo_x, grad_inner, keep, send, grad_x):
    rows = keep.shape[0]
    for number, g in ((1, g_b), (0, g_a)):
        at = slice(number * rows, (number + 1) * rows)
        grad = whole(g)
        grad_inner[at, :] = (dot_nt(grad, wo[...]) * slope[at, :].astype(f32)).astype(bf16)
        grad_x[...] = (dot_nt(grad, wo_x[...]) * slope_x[at, :].astype(f32)).astype(bf16)
        total = dot_nt(grad_inner[at, :], wi[...]) + dot_nt(grad_x[...], wi_x[...])
        if number:
            put(send, total)
        else:
            keep[...] = total


def feed_weights_kernel(g_a, g_b, active_t, normed_t, grad_inner, outer, inner, sums):
    outer[...] = dot_nn(active_t[...], whole(g_a + g_b))
    inner[...] = dot_nn(normed_t[...], grad_inner[...])
    sums[...] = dot_nn(jnp.ones((8, grad_inner.shape[0]), bf16), grad_inner[...])


def feed_weights_far_kernel(
    ids, g_a, g_b, active_t, normed_t, slope, wo, outer, inner, sums_in,
    outer_keep, outer_send, inner_keep, inner_send, sums, grad_inner,
):
    for at, g in row_blocks(g_a, g_b):
        grad_inner[at, :] = (dot_nt(g, wo[...]) * slope[at, :].astype(f32)).astype(bf16)
    grads = whole(g_a + g_b)
    half = outer_keep.shape[0]
    for index, target in ((1 - ids[1], outer_send), (ids[1], outer_keep)):
        at = pl.ds(pl.multiple_of(index * half, 128), half)
        target[...] = (dot_nn(active_t[at, :], grads) + outer[at, :]).astype(target.dtype)
    for index, target in ((1 - ids[2], inner_send), (ids[2], inner_keep)):
        at = pl.ds(pl.multiple_of(index * half, 128), half)
        target[...] = (dot_nn(normed_t[at, :], grad_inner[...]) + inner[at, :]).astype(
            target.dtype
        )
    sums[...] = sums_in[...] + dot_nn(
        jnp.ones((8, grad_inner.shape[0]), bf16), grad_inner[...]
    )


Y_FIRST = (4, (0, 2, 1, 3))
Z_FIRST = (3, (0, 1, 2, 3))


def quarter_rows(ids, layout, number, rows):
    index, numbers = layout
    return pl.ds(pl.multiple_of((ids[index] ^ numbers[number]) * rows, 16), rows)


def halve_kernel(which, extra, ids, kept, got, keep, send):
    body = kept.shape[0] - extra
    half = body // 2
    bit = ids[which]
    for index, target in ((1 - bit, send), (bit, keep)):
        at = pl.ds(pl.multiple_of(index * half, 16), half)
        target[:half, :] = (kept[at, :].astype(f32) + got[at, :].astype(f32)).astype(target.dtype)
    if extra:
        total = (kept[body:, :].astype(f32) + got[body:, :].astype(f32)).astype(bf16)
        send[half:, :] = total
        keep[half:, :] = total.astype(f32)


def add_two_kernel(kept, got, out):
    out[...] = (kept[...].astype(f32) + got[...].astype(f32)).astype(bf16)


def add_last_kernel(kept, got, out, vectors):
    rows = out.shape[0]
    total = kept[...].astype(f32) + got[...].astype(f32)
    out[...] = total[:rows, :].astype(bf16)
    vectors[...] = total[rows:, :]


def token_out_kernel(kept, got, out):
    out[...] = kept[...] + got[...].astype(f32)


STEPS = (
    "outer_halve",
    "inner_halve",
    "heads_whole",
    "outer_quarter",
    "inner_quarter",
    "token_grad",
    "token_out",
    "heads_halve",
    "outer_finish",
    "heads_quarter",
    "inner_finish",
    "outer_place",
    "heads_finish",
    "inner_place",
)
PATHS = ("y", "y", "direct")
HEADS_BITS = (1, 2)


class Group:
    def __init__(self, order, ids, name, extra, keep):
        self.order, self.ids, self.name, self.extra = order, ids, name, extra
        self.keep = keep

    def halve(self, bit):
        rows, cols = self.keep.shape
        half = (rows - self.extra) // 2 + self.extra
        self.keep, send = self.order.call(
            functools.partial(halve_kernel, bit, self.extra),
            (self.ids,),
            (self.keep, self.got),
            [((half, cols), f32), ((half, cols), bf16)],
            name=self.name + "_halve",
        )
        self.got = swap(send, "batch", bit)

    def quarter(self):
        (self.keep,) = self.order.call(
            add_two_kernel,
            (),
            (self.keep, self.got),
            [(self.keep.shape, bf16)],
            name=self.name + "_quarter",
        )
        stride = 4
        while 2 * stride < lax.axis_size("batch"):
            (self.keep,) = self.order.call(
                add_two_kernel,
                (),
                (self.keep, swap(self.keep, "batch", stride)),
                [(self.keep.shape, bf16)],
                name=self.name + "_%d" % stride,
            )
            stride *= 2
        self.got = swap(self.keep, "batch", stride)

    def finish(self, path):
        rows, cols = self.keep.shape
        outputs = [((rows - self.extra, cols), bf16)]
        if self.extra:
            outputs.append(((self.extra, cols), f32))
        results = self.order.call(
            add_last_kernel if self.extra else add_two_kernel,
            (),
            (self.keep, self.got),
            outputs,
            name=self.name + "_finish",
        )
        self.vectors = results[-1]
        mine = results[0]
        far, near = swap(mine, "batch", 1), swap(mine, "batch", 2)
        if path == "direct":
            across = swap(mine, "batch", 3)
        elif path == "y":
            across = swap(after(near, far), "batch", 1)
        else:
            across = swap(after(far, near), "batch", 2)
        self.pieces = [mine, far, near, across]


def place_kernel(layout, ids, pieces, out):
    rows = pieces[0].shape[0]
    for number, part in enumerate(pieces):
        out[quarter_rows(ids, layout, number, rows), :] = part[...].astype(f32)


def place_heads_kernel(ids, pieces, vectors, grads, lines, biases, scratch):
    index, numbers = Y_FIRST if HEADS_BITS == (1, 2) else Z_FIRST
    for number, part in enumerate(pieces):
        scratch[ids[index] ^ numbers[number]] = part[...].astype(f32)
    for number, out in enumerate(grads):
        out[...] = scratch[number]
    for number, out in enumerate(lines):
        out[...] = vectors[number : number + 1, :].reshape(out.shape)
    for number, out in enumerate(biases):
        width = out.shape[0]
        line = vectors[7:8, number * width : (number + 1) * width]
        out[...] = line.reshape(out.shape)


def body(
    tokens_in,
    cotangent,
    half_length,
    block_perm,
    w_query,
    b_query,
    w_key,
    w_value,
    b_value,
    w_output,
    b_output,
    norm1_gain,
    norm1_shift,
    w_inner,
    b_inner,
    w_outer,
    b_outer,
    norm2_gain,
    norm2_shift,
):
    width = w_query.shape[0]
    model = w_query.shape[1]
    units = w_outer.shape[0]
    rows = tokens_in.shape[0]
    both = 2 * rows
    half = model // 2
    index = lax.axis_index("batch")
    ids = jnp.stack(
        [
            lax.axis_index("heads"),
            index & 1,
            (index >> 1) & 1,
            index & 3,
            (index & 1) * 2 + ((index >> 1) & 1),
        ]
    ).astype(jnp.int32)
    scalars = (ids, half_length, block_perm)
    order = Order()

    (packed,) = order.call(
        pack_attention_kernel,
        (ids,),
        (w_query, w_key, w_value, w_output),
        [((2 * width, model), bf16)],
        scratch=[pltpu.SemaphoreType.DMA((4,))],
        name="pack_attention",
        remote=4,
        far=True,
    )
    first = swap(packed, "heads", 2)
    other_tokens = swap(tokens_in, "heads", 1)
    table, lines = order.call(
        vectors_kernel,
        (),
        (
            b_query,
            b_value,
            b_inner,
            b_output,
            norm1_gain,
            norm1_shift,
            b_outer,
            norm2_gain,
            norm2_shift,
        ),
        [((8, model), f32), ((16, half), bf16)],
        name="vectors",
    )
    inner_half, outer_half = order.call(
        pack_ffn_kernel,
        (ids,),
        (lines, w_inner, w_outer),
        [((model + 16, units // 2), bf16), ((units // 2, model), bf16)],
        scratch=[pltpu.SemaphoreType.DMA((3,))],
        name="pack_ffn",
        remote=2,
    )
    inner_a = swap(inner_half, "heads", 2)
    outer_a = swap(outer_half, "heads", 2)
    second = swap(first, "batch", 1)
    inner_b = swap(inner_a, "batch", 2)
    outer_b = swap(outer_a, "batch", 1)

    head_outputs = [
        ((both, width), bf16),
        ((both, width), bf16),
        ((both, width), bf16),
        ((8, both), f32),
        ((width, both), bf16),
    ]
    mixed = pltpu.VMEM((both, width), bf16)
    q, k, v, lse, mixed_t, part = order.call(
        attention_own_kernel,
        scalars,
        (tokens_in, other_tokens, table, w_query, w_key, w_value, w_output),
        head_outputs + [((both, model), f32)],
        scratch=[mixed]
        + [pltpu.VMEM((width, model), bf16)] * 4
        + [pltpu.SemaphoreType.DMA((4,))],
        name="attention_own",
        remote=4,
    )
    qx, kx, vx, lse_x, mixed_tx, wx, keep, send = order.call(
        attention_other_kernel,
        scalars,
        (tokens_in, other_tokens, first, after(second, inner_a), inner_a, part),
        head_outputs
        + [((4, width, model), bf16), ((rows, model), f32), chunked(rows, model, "projected")],
        scratch=[mixed],
        name="attention_other",
    )
    hidden_one, normed, normed_all, normed_bf = order.call(
        norm_one_kernel,
        (),
        (
            tokens_in,
            keep,
            after(swap(send, "heads", 1), outer_a),
            table,
        ),
        [
            ((rows, model), f32),
            ((rows, model), f32),
            ((rows, model), bf16),
            chunked(rows, model, "normed"),
        ],
        name="norm_one",
    )

    other_normed = swap(normed_bf, "heads", 1)
    far_normed = swap([normed_all], "heads", 2)
    active_t, slope, part, normed_t = order.call(
        feed_own_kernel,
        (),
        (normed_bf, other_normed, w_inner, table, w_outer),
        [
            ((units, both), bf16),
            ((both, units), bf16),
            ((both, model), f32),
            ((model, both), bf16),
        ],
        name="feed_own",
    )
    slope_x, keep, send, wi_x, wo_x = order.call(
        feed_other_kernel,
        (ids,),
        (normed_bf, other_normed, inner_a, inner_b, outer_a, outer_b, part),
        [
            ((both, units), bf16),
            ((rows, model), f32),
            chunked(rows, model, "fed"),
            ((model, units), bf16),
            ((units, model), bf16),
        ],
        name="feed_other",
    )
    other_ffn = swap(send, "heads", 1)
    far_normed = after(far_normed, other_ffn)
    far_other_normed = swap(far_normed, "heads", 1)
    block_out, grad_two, grad_two_all, grad_two_bf, sums_two = order.call(
        norm_two_kernel,
        (),
        (
            normed,
            keep,
            after(other_ffn, far_normed),
            table,
            cotangent,
        ),
        [
            ((rows, model), bf16),
            ((rows, model), f32),
            ((rows, model), bf16),
            chunked(rows, model, "grad_two"),
            ((8, model), f32),
        ],
        name="norm_two",
    )

    other_grad_two = swap(grad_two_bf, "heads", 1)
    far_grad_two = swap([grad_two_all], "heads", 2)
    active_f, slope_f, normed_f = order.call(
        feed_far_kernel,
        (),
        (far_normed, far_other_normed, w_inner, table),
        [((units, both), bf16), ((both, units), bf16), ((model, both), bf16)],
        name="feed_far",
    )
    grad_inner, keep, send = order.call(
        feed_back_kernel,
        (),
        (grad_two_bf, other_grad_two, slope, slope_x, w_inner, w_outer, wi_x, wo_x),
        [((both, units), bf16), ((rows, model), f32), chunked(rows, model, "back")],
        scratch=[pltpu.VMEM((rows, units), bf16)],
        name="feed_back",
    )
    outer_part, inner_part, part_sums = order.call(
        feed_weights_kernel,
        (),
        (grad_two_bf, other_grad_two, active_t, normed_t, grad_inner),
        [((units, model), f32), ((model, units), f32), ((8, units), f32)],
        name="feed_weights",
    )
    grad_one, grad_one_bf, sums_one = order.call(
        norm_one_back_kernel,
        (),
        (grad_two, keep, swap(send, "heads", 1), hidden_one, table, sums_two),
        [((rows, model), f32), chunked(rows, model, "grad_one"), ((8, model), f32)],
        name="norm_one_back",
    )

    grads_one = (grad_one_bf, swap(grad_one_bf, "heads", 1))
    row_sums = (sums_one, swap(sums_one, "heads", 1))
    head_grads = [((both, width), bf16)] * 3
    group = [((4 * width + 16, model), bf16)]
    head_scratch = [pltpu.VMEM((width, both), bf16)] * 3 + [pltpu.VMEM((both, width), bf16)]
    dqx, dkx, dvx, far_heads = order.call(
        attention_back_other_kernel,
        scalars,
        (*grads_one, tokens_in, other_tokens, wx, qx, kx, vx, lse_x, mixed_tx, *row_sums),
        head_grads + group,
        scratch=head_scratch,
        name="attention_back_other",
    )
    got_heads = swap(far_heads, "heads", 2)

    far_grad_two = after(far_grad_two, far_heads)
    far_other_grad_two = swap(far_grad_two, "heads", 1)
    (token_part,) = order.call(
        token_grad_other_kernel,
        (),
        (dqx, dkx, dvx, wx, grad_one),
        [((both, model), f32)],
        name="token_grad_other",
    )
    halves = [((units // 2, model), f32), ((units // 2, model), bf16)]
    outer_keep, outer_send, inner_keep, inner_send, inner_sums = order.call(
        feed_weights_far_kernel,
        (ids,),
        (
            far_grad_two,
            far_other_grad_two,
            active_f,
            normed_f,
            slope_f,
            w_outer,
            outer_part,
            inner_part,
            part_sums,
        ),
        halves + halves + [((8, units), f32)],
        scratch=[pltpu.VMEM((both, units), bf16)],
        name="feed_weights_far",
    )
    outer = Group(order, ids, "outer", 0, outer_keep)
    outer.got = swap(outer_send, "batch", 1)
    inner = Group(order, ids, "inner", 0, inner_keep)
    inner.got = swap(inner_send, "batch", 2)

    dq, dk, dv, own_heads = order.call(
        attention_back_own_kernel,
        scalars,
        (
            *grads_one,
            tokens_in,
            other_tokens,
            w_output,
            q,
            k,
            v,
            lse,
            mixed_t,
            *row_sums,
            inner_sums,
        ),
        head_grads + group,
        scratch=head_scratch,
        name="attention_back_own",
    )
    heads = Group(order, ids, "heads", 16, own_heads)
    heads.got = got_heads
    tokens_sum = {}

    def token_grad():
        tokens_sum["keep"], send = order.call(
            token_grad_own_kernel,
            (),
            (dq, dk, dv, w_query, w_key, w_value, token_part),
            [((rows, model), f32), ((rows, model), bf16)],
            name="token_grad_own",
        )
        tokens_sum["got"] = swap(send, "heads", 1)

    def token_out():
        (tokens_sum["out"],) = order.call(
            token_out_kernel,
            (),
            (tokens_sum["keep"], tokens_sum["got"]),
            [((rows, model), f32)],
            name="token_out",
        )

    def place(group, layout, shape):
        (group.whole,) = order.call(
            functools.partial(place_kernel, layout),
            (ids,),
            (group.pieces,),
            [(shape, f32)],
            name="place_" + group.name,
        )

    steps = {
        "outer_halve": lambda: outer.halve(2),
        "outer_quarter": outer.quarter,
        "outer_finish": lambda: outer.finish(PATHS[0]),
        "outer_place": lambda: place(outer, Y_FIRST, (units, model)),
        "inner_halve": lambda: inner.halve(1),
        "inner_quarter": inner.quarter,
        "inner_finish": lambda: inner.finish(PATHS[1]),
        "inner_place": lambda: place(inner, Z_FIRST, (model, units)),
        "heads_whole": lambda: heads.halve(HEADS_BITS[0]),
        "heads_halve": lambda: heads.halve(HEADS_BITS[1]),
        "heads_quarter": heads.quarter,
        "heads_finish": lambda: heads.finish(PATHS[2]),
        "token_grad": token_grad,
        "token_out": token_out,
    }
    for step in STEPS:
        steps[step]()
    grad_tokens, grad_w_outer, grad_w_inner = tokens_sum["out"], outer.whole, inner.whole
    (grad_o, grad_q, grad_k, grad_v), lines, biases = order.call(
        place_heads_kernel,
        (ids,),
        (heads.pieces, heads.vectors),
        [[((width, model), f32)] * 4, [((model,), f32)] * 7, [((width,), f32)] * 2],
        scratch=[pltpu.VMEM((4, width, model), f32)],
        name="place_heads",
    )

    return (
        block_out,
        grad_tokens,
        grad_q,
        biases[0],
        grad_k,
        grad_v,
        biases[1],
        grad_o,
        lines[0],
        lines[1],
        lines[2],
        grad_w_inner,
        lines[6],
        grad_w_outer,
        lines[3],
        lines[4],
        lines[5],
    )


def solution(mesh):
    placed = (
        P(("batch", "heads"), None),
        P(("batch", "heads"), None),
        P("batch"),
        P(),
        P("heads", None),
        P("heads"),
        P("heads", None),
        P("heads", None),
        P("heads"),
        P("heads", None),
        P(),
        P(),
        P(),
        P(None, "heads"),
        P("heads"),
        P("heads", None),
        P(),
        P(),
        P(),
    )
    return jax.shard_map(
        body,
        mesh=mesh,
        in_specs=placed,
        out_specs=(
            P(("batch", "heads"), None),
            P(("batch", "heads"), None),
            P("heads", None),
            P("heads"),
            P("heads", None),
            P("heads", None),
            P("heads"),
            P("heads", None),
            P(),
            P(),
            P(),
            P(None, "heads"),
            P("heads"),
            P("heads", None),
            P(),
            P(),
            P(),
        ),
        check_vma=False,
    )
```

```python
import functools

import jax
import jax.numpy as jnp
from jax import lax
from jax.experimental import pallas as pl
from jax.experimental.pallas import tpu as pltpu
from jax.sharding import PartitionSpec as P

HEAD_DIM = 64
HALF = 1024
SCALE = HEAD_DIM ** (-0.5)
epsilon = 1e-06

bf16 = jnp.bfloat16
f32 = jnp.float32


def dot_nn(left, right):
    return jnp.dot(left, right, preferred_element_type=f32)


def dot_nt(left, right):
    return lax.dot_general(left, right, (((1,), (1,)), ((), ())), preferred_element_type=f32)


def swap(value, axis, stride):
    size = lax.axis_size(axis)
    pairs = [(i, i ^ stride) for i in range(size)]
    return jax.tree.map(lambda part: lax.ppermute(part, axis, pairs), value)


def row(ref):
    return ref[...].reshape(1, -1).astype(f32)


VMEM_SPEC = pl.BlockSpec(memory_space=pltpu.VMEM)
SMEM_SPEC = pl.BlockSpec(memory_space=pltpu.SMEM)
ANY_SPEC = pl.BlockSpec(memory_space=pl.ANY)
HBM_SPEC = pl.BlockSpec(memory_space=pltpu.HBM)


PIECES = {"projected": 2, "normed": 4, "fed": 4, "grad_two": 1, "back": 4, "grad_one": 2, "tokens": 2}


def chunked(rows, cols, name):
    return [((rows // PIECES[name], cols), bf16)] * PIECES[name]


def whole(refs):
    return jnp.concatenate([ref[...] for ref in refs], axis=0)


def put(refs, value):
    rows = refs[0].shape[0]
    for number, ref in enumerate(refs):
        ref[...] = value[number * rows : (number + 1) * rows].astype(ref.dtype)


def after(value, *others):
    return lax.optimization_barrier((value, others))[0]


class Order:
    def __init__(self):
        self.last = None

    def call(self, kernel, scalars, inputs, outputs, **options):
        ins, tree = jax.tree.flatten(list(inputs))
        if self.last is not None:
            ins[0] = after(ins[0], self.last)
        results = call(kernel, scalars, jax.tree.unflatten(tree, ins), outputs, **options)
        self.last = min(jax.tree.leaves(results), key=lambda part: part.size)
        return results


def call(kernel, scalars, inputs, outputs, scratch=(), mib=12, name=None, remote=0, far=False, aliases=None):
    ins, in_tree = jax.tree.flatten(list(inputs))
    outs, out_tree = jax.tree.flatten(
        list(outputs), is_leaf=lambda entry: isinstance(entry, tuple)
    )
    out_shape = tuple(jax.ShapeDtypeStruct(shape, dtype) for shape, dtype in outs)
    near = len(ins) - remote
    first, second = len(scalars) + len(ins), len(scalars) + len(ins) + len(outs)

    def run(*refs):
        given = jax.tree.unflatten(in_tree, refs[len(scalars) : first])
        made = jax.tree.unflatten(out_tree, refs[first:second])
        kernel(*refs[: len(scalars)], *given, *made, *refs[second:])

    results = pl.pallas_call(
        run,
        out_shape=out_shape,
        in_specs=[SMEM_SPEC] * len(scalars) + [VMEM_SPEC] * near + [HBM_SPEC] * remote,
        out_specs=(ANY_SPEC if far else VMEM_SPEC,) * len(out_shape),
        scratch_shapes=list(scratch),
        input_output_aliases=aliases or {},
        compiler_params=pltpu.CompilerParams(vmem_limit_bytes=mib * 1024 * 1024),
        cost_estimate=pl.CostEstimate(flops=1000, bytes_accessed=1000, transcendentals=0),
        name=name,
    )(*scalars, *ins[:near], *(pltpu.with_memory_space_constraint(x, pltpu.HBM) for x in ins[near:]))
    return jax.tree.unflatten(out_tree, results)


def pack_attention_kernel(ids, wq, wk, wv, wo, out, sems):
    half = wq.shape[0] // 2
    at = pl.multiple_of(ids[1] * half, 16)
    copies = [
        pltpu.make_async_copy(
            weights.at[pl.ds(at, half), :],
            out.at[number * half : (number + 1) * half, :],
            sems.at[number],
        )
        for number, weights in enumerate((wq, wk, wv, wo))
    ]
    for copy in copies:
        copy.start()
    for copy in copies:
        copy.wait()


def vectors_kernel(bq, bv, bi, bo, gain1, shift1, bo2, gain2, shift2, table, lines):
    rows = [row(ref) for ref in (bo, gain1, shift1, bo2, gain2, shift2, bi)]
    heads = jnp.concatenate([row(bq), row(bv)], axis=1)
    half = lines.shape[1]
    table[...] = jnp.concatenate(
        rows + [jnp.concatenate([heads, jnp.zeros_like(heads)], axis=1)], axis=0
    )
    lines[...] = jnp.concatenate(
        [heads, rows[6][:, :half], rows[6][:, half:], jnp.zeros((13, half), f32)], axis=0
    ).astype(bf16)


def pack_ffn_kernel(ids, lines, wi, wo, out_inner, out_outer, sems):
    model, half = wi.shape[0], wo.shape[0] // 2
    copies = [
        pltpu.make_async_copy(
            wi.at[:, pl.ds(pl.multiple_of(ids[2] * half, 128), half)],
            out_inner.at[:model, :],
            sems.at[0],
        ),
        pltpu.make_async_copy(
            wo.at[pl.ds(pl.multiple_of(ids[1] * half, 128), half), :], out_outer, sems.at[1]
        ),
        pltpu.make_async_copy(lines, out_inner.at[model:, :], sems.at[2]),
    ]
    for copy in copies:
        copy.start()
    for copy in copies:
        copy.wait()


def attend_blocks(ids, lengths, perm, owner, probs, visit, halves=(0, 1)):
    is_long = lengths[ids[0] // 2] == HALF
    swaps = [perm[owner * 3 + head, 0] for head in range(3)]

    @pl.when(is_long)
    def _():
        for block in halves:
            for head in range(3):
                kept = probs.at[head, block]
                visit(head, block * 512, (block ^ swaps[head]) * 512, 512, kept)

    @pl.when(jnp.logical_not(is_long))
    def _():
        @pl.loop(2 * halves[0], 2 * halves[-1] + 2)
        def _(block):
            for head in range(3):
                at = pl.multiple_of(block * 256, 256)
                cols = pl.ds(pl.multiple_of((block & 1) * 256, 256), 256)
                kept = probs.at[head, block >> 1, :256, cols]
                visit(head, at, (block ^ swaps[head]) * 256, 256, kept)


def attend_forward(ids, lengths, perm, owner, q_ref, k_ref, v_ref, probs, mixed, mixed_t):
    def visit(head, q_at, k_at, size, kept):
        cols = slice(head * HEAD_DIM, (head + 1) * HEAD_DIM)
        q_rows = pl.ds(q_at, size)
        k_rows = pl.ds(pl.multiple_of(k_at, 256), size)
        queries = q_ref[q_rows, cols] * SCALE
        scores_t = dot_nt(k_ref[k_rows, cols], queries.astype(bf16))
        weights_t = jnp.exp(scores_t - jnp.max(scores_t, axis=0, keepdims=True))
        total = jnp.sum(weights_t, axis=0, keepdims=True)
        probs_t = (weights_t * (1.0 / total)).astype(bf16)
        kept[...] = probs_t
        out_t = dot_nn(v_ref[k_rows, cols].T, probs_t).astype(bf16)
        mixed_t[cols, q_rows] = out_t
        mixed[q_rows, cols] = out_t.T

    attend_blocks(ids, lengths, perm, owner, probs, visit)


def project_qkv(tok_a, tok_b, weights, biases, outs):
    rows = tok_a.shape[0]
    for block, tok in enumerate((tok_a, tok_b)):
        at = slice(block * rows, (block + 1) * rows)
        for weight, bias, out in zip(weights, biases, outs):
            product = dot_nt(tok[...], weight[...])
            out[at, :] = (product if bias is None else product + bias).astype(bf16)


def fetch(sources, targets, sems):
    copies = [
        pltpu.make_async_copy(source, target, sems.at[number])
        for number, (source, target) in enumerate(zip(sources, targets))
    ]
    for copy in copies:
        copy.start()
    return copies


def attention_own_kernel(
    ids, lengths, perm, tok_a, tok_b, table, wq_far, wk_far, wv_far, wo_far,
    q, k, v, probs, mixed_t, part, mixed, wq, wk, wv, wo, sems,
):
    copies = fetch((wq_far, wk_far, wv_far, wo_far), (wq, wk, wv, wo), sems)
    for copy in copies:
        copy.wait()
    width = q.shape[1]
    biases = (table[7:8, :width], None, table[7:8, width : 2 * width])
    project_qkv(tok_a, tok_b, (wq, wk, wv), biases, (q, k, v))
    attend_forward(ids, lengths, perm, ids[0], q, k, v, probs, mixed, mixed_t)
    part[...] = dot_nn(mixed[...], wo[...])


def attention_other_kernel(
    ids, lengths, perm, tok_a, tok_b, first, second, lines, part,
    q, k, v, probs, mixed_t, wx, keep, send, mixed,
):
    width = q.shape[1]
    half = width // 2
    rows = keep.shape[0]
    mine = pl.multiple_of(ids[1] * half, 16)
    other = pl.multiple_of((1 - ids[1]) * half, 16)
    for number in range(4):
        wx[number, pl.ds(mine, half), :] = first[number * half : (number + 1) * half, :]
        wx[number, pl.ds(other, half), :] = second[number * half : (number + 1) * half, :]
    line = lines[-16:, :].astype(f32)[:1]
    biases = (line[:, :width], None, line[:, width : 2 * width])
    project_qkv(tok_a, tok_b, (wx.at[0], wx.at[1], wx.at[2]), biases, (q, k, v))
    attend_forward(ids, lengths, perm, ids[0] ^ 2, q, k, v, probs, mixed, mixed_t)
    keep[...] = part[:rows, :] + dot_nn(mixed[:rows, :], wx[3])
    put(send, part[rows:, :] + dot_nn(mixed[rows:, :], wx[3]))


def attend_backward_kernel(
    ids, lengths, perm, owner, q_ref, k_ref, v_ref, probs, grads_ref,
    dq, dk, dv, dqt, dkt, dvt, halves=(0, 1),
):
    def visit(head, q_at, k_at, size, kept):
        cols = slice(head * HEAD_DIM, (head + 1) * HEAD_DIM)
        q_rows = pl.ds(q_at, size)
        k_rows = pl.ds(pl.multiple_of(k_at, 256), size)
        queries = (q_ref[q_rows, cols] * SCALE).astype(bf16)
        keys = k_ref[k_rows, cols]
        grads = grads_ref[q_rows, cols]
        grad_probs_t = dot_nt(v_ref[k_rows, cols], grads)
        probs_t = kept[...]
        wide = probs_t.astype(f32)
        delta = jnp.sum(wide * grad_probs_t, axis=0, keepdims=True)
        grad_scores_t = (wide * (grad_probs_t - delta)).astype(bf16)
        grad_v = dot_nn(probs_t, grads).astype(bf16)
        grad_k = dot_nn(grad_scores_t, queries).astype(bf16)
        grad_q_t = (dot_nn(keys.T, grad_scores_t) * SCALE).astype(bf16)
        dv[k_rows, cols] = grad_v
        dk[k_rows, cols] = grad_k
        dq[q_rows, cols] = grad_q_t.T
        dvt[cols, k_rows] = grad_v.T
        dkt[cols, k_rows] = grad_k.T
        dqt[cols, q_rows] = grad_q_t

    attend_blocks(ids, lengths, perm, owner, probs, visit, halves)


def backward_attention(
    ids, lengths, perm, owner, g_a, g_b, wo, q, k, v, probs, dq, dk, dv, dqt, dkt, dvt, grads
):
    for at, g in row_blocks(g_a, g_b):
        grads[at, :] = dot_nt(g, wo).astype(bf16)
    attend_backward_kernel(
        ids, lengths, perm, owner, q, k, v, probs, grads, dq, dk, dv, dqt, dkt, dvt
    )


def row_sum(left_t):
    ones = jnp.ones((8, left_t.shape[1]), bf16)
    return dot_nt(ones, left_t)[:1]


def head_weight_grads(out, lefts, rights, vectors):
    width = lefts[0].shape[0]
    for number, (left, right) in enumerate(zip(lefts, rights)):
        out[number * width : (number + 1) * width, :] = dot_nn(left[...], right).astype(bf16)
    vectors = jnp.concatenate([vectors, jnp.zeros_like(vectors)], axis=0)
    out[len(lefts) * width :, :] = vectors.astype(bf16)


def bias_row(dqt, dvt):
    width = dqt.shape[0]
    return jnp.concatenate(
        [row_sum(dqt[...]), row_sum(dvt[...]), jnp.zeros((1, 2 * width), f32)], axis=1
    )


def attention_back_other_kernel(half, ids, lengths, perm, g, wx, q, k, v, probs, *refs):
    dq, dk, dv, dqt, dkt, dvt, grads = refs[-7:]
    rows = grads.shape[0] // 2
    grads[half * rows : (half + 1) * rows, :] = dot_nt(whole(g), wx[3]).astype(bf16)
    attend_backward_kernel(
        ids, lengths, perm, ids[0] ^ 2, q, k, v, probs, grads,
        dq, dk, dv, dqt, dkt, dvt, halves=(half,),
    )


def heads_grad_other_kernel(
    mixed_t, dqt, dkt, dvt, g_a, g_b, tok_a, tok_b, sums, got_sums, out
):
    vectors = jnp.concatenate([sums[:7] + got_sums[:7], bias_row(dqt, dvt)], axis=0)
    tokens = whole([tok_a, tok_b])
    rights = (whole(g_a + g_b), tokens, tokens, tokens)
    head_weight_grads(out, (mixed_t, dqt, dkt, dvt), rights, vectors)


def attention_back_own_kernel(
    ids, lengths, perm, g_a, g_b, tok_a, tok_b, wo, q, k, v, probs, mixed_t, sums, got_sums, inner_sums,
    dq, dk, dv, out, dqt, dkt, dvt, grads,
):
    backward_attention(
        ids, lengths, perm, ids[0], g_a, g_b, wo[...], q, k, v, probs,
        dq, dk, dv, dqt, dkt, dvt, grads,
    )
    vectors = jnp.concatenate(
        [sums[:6] + got_sums[:6], inner_sums[:1], bias_row(dqt, dvt)], axis=0
    )
    tokens = whole([tok_a, tok_b])
    rights = (whole(g_a + g_b), tokens, tokens, tokens)
    head_weight_grads(out, (mixed_t, dqt, dkt, dvt), rights, vectors)


def token_grad_other_kernel(dq, dk, dv, wx, grad_one, out):
    rows = grad_one.shape[0]
    total = dot_nn(dq[...], wx[0]) + dot_nn(dk[...], wx[1]) + dot_nn(dv[...], wx[2])
    out[:rows, :] = total[:rows, :] + grad_one[...]
    out[rows:, :] = total[rows:, :]


def token_grad_own_kernel(dq, dk, dv, wq, wk, wv, part, keep, send):
    rows = keep.shape[0]
    total = dot_nn(dq[...], wq[...]) + dot_nn(dk[...], wk[...]) + dot_nn(dv[...], wv[...])
    put(send, part[rows:, :] + total[rows:, :])
    keep[...] = part[:rows, :] + total[:rows, :]


def normalize(hidden):
    center = jnp.mean(hidden, axis=1, keepdims=True)
    rinv = lax.rsqrt(jnp.mean(hidden * hidden, axis=1, keepdims=True) - center * center + epsilon)
    return (hidden - center) * rinv, rinv


def norm_back(grad_zhat, zhat, rinv):
    first_mean = jnp.mean(grad_zhat, axis=1, keepdims=True)
    second_mean = jnp.mean(grad_zhat * zhat, axis=1, keepdims=True)
    return rinv * (grad_zhat - first_mean - zhat * second_mean)


def norm_one_kernel(tokens, keep, got, table, hidden, normed, normed_all, normed_bf):
    value = tokens[...].astype(f32) + keep[...] + whole(got).astype(f32) + table[0:1, :]
    hidden[...] = value
    zhat, _ = normalize(value)
    result = zhat * table[1:2, :] + table[2:3, :]
    normed[...] = result
    normed_all[...] = result.astype(bf16)
    put(normed_bf, result)


def norm_two_kernel(
    normed, keep, got, table, cotangent,
    block_out, grad_two, grad_two_all, grad_two_bf, sums,
):
    hidden = normed[...] + keep[...] + whole(got).astype(f32) + table[3:4, :]
    zhat, rinv = normalize(hidden)
    block_out[...] = (zhat * table[4:5, :] + table[5:6, :]).astype(bf16)
    grad_out = cotangent[...].astype(f32)
    grad = norm_back(grad_out * table[4:5, :], zhat, rinv)
    grad_two[...] = grad
    grad_two_all[...] = grad.astype(bf16)
    put(grad_two_bf, grad)
    sums[...] = jnp.concatenate(
        [
            jnp.sum(grad, axis=0, keepdims=True),
            jnp.sum(grad_out * zhat, axis=0, keepdims=True),
            jnp.sum(grad_out, axis=0, keepdims=True),
            jnp.zeros((5, grad.shape[1]), f32),
        ],
        axis=0,
    )


def norm_one_back_kernel(grad_two, keep, got, hidden, table, sums_in, grad_one, grad_one_bf, sums):
    grad_normed = grad_two[...] + keep[...] + whole(got).astype(f32)
    zhat, rinv = normalize(hidden[...])
    grad = norm_back(grad_normed * table[1:2, :], zhat, rinv)
    grad_one[...] = grad
    put(grad_one_bf, grad)
    sums[...] = jnp.concatenate(
        [
            jnp.sum(grad, axis=0, keepdims=True),
            jnp.sum(grad_normed * zhat, axis=0, keepdims=True),
            jnp.sum(grad_normed, axis=0, keepdims=True),
            sums_in[:3],
            jnp.zeros((2, grad.shape[1]), f32),
        ],
        axis=0,
    )


def gelu_parts(values):
    cdf = 0.5 + 0.5 * lax.erf(values * 0.7071067811865476)
    bell = jnp.exp2((-0.5 * 1.4426950408889634) * (values * values))
    return values * cdf, cdf + values * (bell * 0.3989422804014327)


BLOCK = 256


def row_blocks(*sources):
    at = 0
    for source in sources:
        step = max(1, BLOCK // source[0].shape[0])
        for start in range(0, len(source), step):
            block = whole(source[start : start + step])
            yield slice(at, at + block.shape[0]), block
            at += block.shape[0]


def feed_own_kernel(nrm_a, nrm_b, wi, table, wo, active_t, slope, part, normed_t):
    for at, normed in row_blocks(nrm_a, nrm_b):
        normed_t[:, at] = normed.T
        value, rise = gelu_parts(dot_nn(normed, wi[...]) + table[6:7, :])
        part[at, :] = dot_nn(value.astype(bf16), wo[...])
        active_t[:, at] = value.astype(bf16).T
        slope[at, :] = rise.astype(bf16)


def feed_other_kernel(ids, nrm, wi_a, wi_b, wo_a, wo_b, part, slope, send, wi_x, wo_x):
    half, model = wo_a.shape
    for bit, weights in ((ids[2], wi_a), (1 - ids[2], wi_b)):
        wi_x[:, pl.ds(pl.multiple_of(bit * half, 128), half)] = weights[:model, :]
    for bit, weights in ((ids[1], wo_a), (1 - ids[1], wo_b)):
        wo_x[pl.ds(pl.multiple_of(bit * half, 128), half), :] = weights[...]
    rows = slope.shape[0]
    feed_units(nrm, wi_a, wi_x, wo_x, part.at[rows:, :], slope, lambda at, total: put_rows(send, at, total))


def feed_other_own_kernel(nrm, lines, wi_x, wo_x, part, slope, keep):
    def store(at, total):
        keep[at, :] = total

    feed_units(nrm, lines, wi_x, wo_x, part, slope, store)


def put_rows(refs, at, value):
    size = refs[0].shape[0]
    put(refs[at.start // size : at.stop // size], value)


def feed_units(nrm, lines, wi, wo, part, slope, store):
    line = lines[-16:, :].astype(f32)
    bias = jnp.concatenate([line[1:2], line[2:3]], axis=1)
    for at, normed in row_blocks(nrm):
        value, rise = gelu_parts(dot_nn(normed, wi[...]) + bias)
        slope[at, :] = rise.astype(bf16)
        store(at, part[at, :] + dot_nn(value.astype(bf16), wo[...]))


def feed_far_kernel(nrm_a, nrm_b, wi, table, active_t, slope, normed_t):
    for at, normed in row_blocks(nrm_a, nrm_b):
        normed_t[:, at] = normed.T
        value, rise = gelu_parts(dot_nn(normed, wi[...]) + table[6:7, :])
        active_t[:, at] = value.astype(bf16).T
        slope[at, :] = rise.astype(bf16)


def feed_back_kernel(half, g, slope, slope_x, wi, wo, wi_x, wo_x, grad_inner, out):
    rows = grad_inner.shape[0]
    grad = whole(g)
    rise = slope[half * rows : (half + 1) * rows, :].astype(f32)
    grad_inner[...] = (dot_nt(grad, wo[...]) * rise).astype(bf16)
    grad_x = (dot_nt(grad, wo_x[...]) * slope_x[...].astype(f32)).astype(bf16)
    total = dot_nt(grad_inner[...], wi[...]) + dot_nt(grad_x, wi_x[...])
    if half:
        put(out, total)
    else:
        out[...] = total


def feed_weights_kernel(g_a, g_b, active_t, normed_t, grad_inner, outer, inner, sums):
    outer[...] = dot_nn(active_t[...], whole(g_a + g_b))
    grads = whole(grad_inner)
    inner[...] = dot_nn(normed_t[...], grads)
    sums[...] = dot_nn(jnp.ones((8, grads.shape[0]), bf16), grads)


def feed_weights_far_kernel(
    ids, g_a, g_b, active_t, normed_t, slope, wo, outer, inner, sums_in,
    outer_keep, outer_send, inner_keep, inner_send, sums, grad_inner,
):
    for at, g in row_blocks(g_a, g_b):
        grad_inner[at, :] = (dot_nt(g, wo[...]) * slope[at, :].astype(f32)).astype(bf16)
    grads = whole(g_a + g_b)
    half = outer_keep.shape[0]
    for index, target in ((1 - ids[1], outer_send), (ids[1], outer_keep)):
        at = pl.ds(pl.multiple_of(index * half, 128), half)
        target[...] = (dot_nn(active_t[at, :], grads) + outer[at, :]).astype(target.dtype)
    for index, target in ((1 - ids[2], inner_send), (ids[2], inner_keep)):
        at = pl.ds(pl.multiple_of(index * half, 128), half)
        target[...] = (dot_nn(normed_t[at, :], grad_inner[...]) + inner[at, :]).astype(
            target.dtype
        )
    sums[...] = sums_in[...] + dot_nn(
        jnp.ones((8, grad_inner.shape[0]), bf16), grad_inner[...]
    )


Y_FIRST = (4, (0, 2, 1, 3))
Z_FIRST = (3, (0, 1, 2, 3))


def quarter_rows(ids, layout, number, rows):
    index, numbers = layout
    return pl.ds(pl.multiple_of((ids[index] ^ numbers[number]) * rows, 16), rows)


def halve_kernel(which, extra, ids, kept, got, keep, send):
    body = kept.shape[0] - extra
    half = body // 2
    bit = ids[which]
    for index, target in ((1 - bit, send), (bit, keep)):
        at = pl.ds(pl.multiple_of(index * half, 16), half)
        target[:half, :] = (kept[at, :].astype(f32) + got[at, :].astype(f32)).astype(target.dtype)
    if extra:
        total = (kept[body:, :].astype(f32) + got[body:, :].astype(f32)).astype(bf16)
        send[half:, :] = total
        keep[half:, :] = total.astype(f32)


def add_two_kernel(kept, got, out):
    out[...] = (kept[...].astype(f32) + got[...].astype(f32)).astype(bf16)


def add_last_kernel(kept, got, out, vectors):
    rows = out.shape[0]
    total = kept[...].astype(f32) + got[...].astype(f32)
    out[...] = total[:rows, :].astype(bf16)
    vectors[...] = total[rows:, :]


def token_out_kernel(kept, got, out):
    out[...] = kept[...] + whole(got).astype(f32)


STEPS = (
    "outer_halve",
    "inner_halve",
    "heads_whole",
    "outer_quarter",
    "inner_quarter",
    "token_grad",
    "token_out",
    "heads_halve",
    "inner_finish",
    "outer_finish",
    "heads_quarter",
    "heads_finish",
    "inner_place",
    "outer_place",
)
PATHS = ("direct", "y", "direct")
HEADS_BITS = (1, 2)


class Group:
    def __init__(self, order, ids, name, extra, keep):
        self.order, self.ids, self.name, self.extra = order, ids, name, extra
        self.keep = keep

    def halve(self, bit):
        rows, cols = self.keep.shape
        half = (rows - self.extra) // 2 + self.extra
        self.keep, send = self.order.call(
            functools.partial(halve_kernel, bit, self.extra),
            (self.ids,),
            (self.keep, self.got),
            [((half, cols), f32), ((half, cols), bf16)],
            name=self.name + "_halve",
        )
        self.got = swap(send, "batch", bit)

    def quarter(self):
        (self.keep,) = self.order.call(
            add_two_kernel,
            (),
            (self.keep, self.got),
            [(self.keep.shape, bf16)],
            name=self.name + "_quarter",
        )
        stride = 4
        while 2 * stride < lax.axis_size("batch"):
            (self.keep,) = self.order.call(
                add_two_kernel,
                (),
                (self.keep, swap(self.keep, "batch", stride)),
                [(self.keep.shape, bf16)],
                name=self.name + "_%d" % stride,
            )
            stride *= 2
        self.got = swap(self.keep, "batch", stride)

    def finish(self, path):
        rows, cols = self.keep.shape
        outputs = [((rows - self.extra, cols), bf16)]
        if self.extra:
            outputs.append(((self.extra, cols), f32))
        results = self.order.call(
            add_last_kernel if self.extra else add_two_kernel,
            (),
            (self.keep, self.got),
            outputs,
            name=self.name + "_finish",
        )
        self.vectors = results[-1]
        mine = results[0]
        far, near = swap(mine, "batch", 1), swap(mine, "batch", 2)
        if path == "direct":
            across = swap(mine, "batch", 3)
        elif path == "y":
            across = swap(after(near, far), "batch", 1)
        else:
            across = swap(after(far, near), "batch", 2)
        self.pieces = [mine, far, near, across]


def place_kernel(layout, ids, pieces, out):
    rows = pieces[0].shape[0]
    for number, part in enumerate(pieces):
        out[quarter_rows(ids, layout, number, rows), :] = part[...].astype(f32)


def place_heads_kernel(ids, pieces, vectors, grads, lines, biases, scratch):
    index, numbers = Y_FIRST if HEADS_BITS == (1, 2) else Z_FIRST
    for number, part in enumerate(pieces):
        scratch[ids[index] ^ numbers[number]] = part[...].astype(f32)
    for number, out in enumerate(grads):
        out[...] = scratch[number]
    for number, out in enumerate(lines):
        out[...] = vectors[number : number + 1, :].reshape(out.shape)
    for number, out in enumerate(biases):
        width = out.shape[0]
        line = vectors[7:8, number * width : (number + 1) * width]
        out[...] = line.reshape(out.shape)


def body(
    tokens_in,
    cotangent,
    half_length,
    block_perm,
    w_query,
    b_query,
    w_key,
    w_value,
    b_value,
    w_output,
    b_output,
    norm1_gain,
    norm1_shift,
    w_inner,
    b_inner,
    w_outer,
    b_outer,
    norm2_gain,
    norm2_shift,
):
    width = w_query.shape[0]
    model = w_query.shape[1]
    units = w_outer.shape[0]
    rows = tokens_in.shape[0]
    both = 2 * rows
    half = model // 2
    index = lax.axis_index("batch")
    ids = jnp.stack(
        [
            lax.axis_index("heads"),
            index & 1,
            (index >> 1) & 1,
            index & 3,
            (index & 1) * 2 + ((index >> 1) & 1),
        ]
    ).astype(jnp.int32)
    scalars = (ids, half_length, block_perm)
    order = Order()

    (packed,) = order.call(
        pack_attention_kernel,
        (ids,),
        (w_query, w_key, w_value, w_output),
        [((2 * width, model), bf16)],
        scratch=[pltpu.SemaphoreType.DMA((4,))],
        name="pack_attention",
        remote=4,
        far=True,
    )
    first = swap(packed, "heads", 2)
    other_tokens = swap(tokens_in, "heads", 1)
    table, lines = order.call(
        vectors_kernel,
        (),
        (
            b_query,
            b_value,
            b_inner,
            b_output,
            norm1_gain,
            norm1_shift,
            b_outer,
            norm2_gain,
            norm2_shift,
        ),
        [((8, model), f32), ((16, half), bf16)],
        name="vectors",
    )
    inner_half, outer_half = order.call(
        pack_ffn_kernel,
        (ids,),
        (lines, w_inner, w_outer),
        [((model + 16, units // 2), bf16), ((units // 2, model), bf16)],
        scratch=[pltpu.SemaphoreType.DMA((3,))],
        name="pack_ffn",
        remote=2,
    )
    inner_a = swap(inner_half, "heads", 2)
    outer_a = swap(outer_half, "heads", 2)
    second = swap(first, "batch", 1)
    inner_b = swap(inner_a, "batch", 2)
    outer_b = swap(outer_a, "batch", 1)

    head_outputs = [
        ((both, width), bf16),
        ((both, width), bf16),
        ((both, width), bf16),
        ((3, 2, both // 2, both // 2), bf16),
        ((width, both), bf16),
    ]
    mixed = pltpu.VMEM((both, width), bf16)
    q, k, v, probs, mixed_t, part = order.call(
        attention_own_kernel,
        scalars,
        (tokens_in, other_tokens, table, w_query, w_key, w_value, w_output),
        head_outputs + [((both, model), f32)],
        scratch=[mixed]
        + [pltpu.VMEM((width, model), bf16)] * 4
        + [pltpu.SemaphoreType.DMA((4,))],
        name="attention_own",
        remote=4,
    )
    qx, kx, vx, probs_x, mixed_tx, wx, keep, send = order.call(
        attention_other_kernel,
        scalars,
        (tokens_in, other_tokens, first, after(second, inner_a), inner_a, part),
        head_outputs
        + [((4, width, model), bf16), ((rows, model), f32), chunked(rows, model, "projected")],
        scratch=[mixed],
        name="attention_other",
    )
    hidden_one, normed, normed_all, normed_bf = order.call(
        norm_one_kernel,
        (),
        (
            tokens_in,
            keep,
            after(swap(send, "heads", 1), outer_a),
            table,
        ),
        [
            ((rows, model), f32),
            ((rows, model), f32),
            ((rows, model), bf16),
            chunked(rows, model, "normed"),
        ],
        name="norm_one",
    )

    other_normed = swap(normed_bf, "heads", 1)
    far_normed = swap([normed_all], "heads", 2)
    active_t, slope, part, normed_t = order.call(
        feed_own_kernel,
        (),
        (normed_bf, other_normed, w_inner, table, w_outer),
        [
            ((units, both), bf16),
            ((both, units), bf16),
            ((both, model), f32),
            ((model, both), bf16),
        ],
        name="feed_own",
    )
    slope_xb, send, wi_x, wo_x = order.call(
        feed_other_kernel,
        (ids,),
        (other_normed, inner_a, inner_b, outer_a, outer_b, part),
        [
            ((rows, units), bf16),
            chunked(rows, model, "fed"),
            ((model, units), bf16),
            ((units, model), bf16),
        ],
        name="feed_other",
    )
    slope_xa, keep = order.call(
        feed_other_own_kernel,
        (),
        (normed_bf, inner_a, wi_x, wo_x, part),
        [((rows, units), bf16), ((rows, model), f32)],
        name="feed_other_own",
    )
    block_out, grad_two, grad_two_all, grad_two_bf, sums_two = order.call(
        norm_two_kernel,
        (),
        (
            normed,
            keep,
            swap(send, "heads", 1),
            table,
            cotangent,
        ),
        [
            ((rows, model), bf16),
            ((rows, model), f32),
            ((rows, model), bf16),
            chunked(rows, model, "grad_two"),
            ((8, model), f32),
        ],
        name="norm_two",
    )

    far_normed = after(far_normed, sums_two)
    far_other_normed = swap(far_normed, "heads", 1)
    other_grad_two = swap(grad_two_bf, "heads", 1)
    far_grad_two = swap([grad_two_all], "heads", 2)
    grad_inner = [None, None]
    grad_inner[0], keep = order.call(
        functools.partial(feed_back_kernel, 0),
        (),
        (grad_two_bf, slope, slope_xa, w_inner, w_outer, wi_x, wo_x),
        [((rows, units), bf16), ((rows, model), f32)],
        name="feed_back_own",
    )
    grad_inner[1], send = order.call(
        functools.partial(feed_back_kernel, 1),
        (),
        (other_grad_two, slope, slope_xb, w_inner, w_outer, wi_x, wo_x),
        [((rows, units), bf16), chunked(rows, model, "back")],
        name="feed_back_other",
    )
    active_f, slope_f, normed_f = order.call(
        feed_far_kernel,
        (),
        (far_normed, far_other_normed, w_inner, table),
        [((units, both), bf16), ((both, units), bf16), ((model, both), bf16)],
        name="feed_far",
    )
    grad_one, grad_one_bf, sums_one = order.call(
        norm_one_back_kernel,
        (),
        (grad_two, keep, swap(send, "heads", 1), hidden_one, table, sums_two),
        [((rows, model), f32), chunked(rows, model, "grad_one"), ((8, model), f32)],
        name="norm_one_back",
    )

    grads_one = (grad_one_bf, swap(grad_one_bf, "heads", 1))
    row_sums = (sums_one, swap(sums_one, "heads", 1))
    grads_one = (grads_one[0], after(grads_one[1], row_sums[1]))
    head_grads = [((both, width), bf16)] * 3
    group = [((4 * width + 16, model), bf16)]
    head_scratch = [pltpu.VMEM((width, both), bf16)] * 3 + [pltpu.VMEM((both, width), bf16)]
    head_blocks = [((both, width), bf16)] * 3 + [((width, both), bf16)] * 3
    results = []
    for number in range(2):
        results = order.call(
            functools.partial(attention_back_other_kernel, number),
            scalars,
            (grads_one[number], wx, qx, kx, vx, probs_x, *results),
            head_blocks,
            scratch=[pltpu.VMEM((both, width), bf16)],
            name="attention_back_other",
            aliases={
                3 + len(grads_one[number]) + 5 + i: i for i in range(6) if len(results) > 0
            },
        )
    dqx, dkx, dvx, *back_t = results
    outer_part, inner_part, part_sums = order.call(
        feed_weights_kernel,
        (),
        (grad_two_bf, other_grad_two, active_t, normed_t, grad_inner),
        [((units, model), f32), ((model, units), f32), ((8, units), f32)],
        name="feed_weights",
    )
    far_grad_two = after(far_grad_two, part_sums)
    far_other_grad_two = swap(far_grad_two, "heads", 1)
    (far_heads,) = order.call(
        heads_grad_other_kernel,
        (),
        (mixed_tx, *back_t, *grads_one, tokens_in, other_tokens, *row_sums),
        group,
        name="heads_grad_other",
    )
    got_heads = swap(far_heads, "heads", 2)

    halves = [((units // 2, model), f32), ((units // 2, model), bf16)]
    outer_keep, outer_send, inner_keep, inner_send, inner_sums = order.call(
        feed_weights_far_kernel,
        (ids,),
        (
            far_grad_two,
            far_other_grad_two,
            active_f,
            normed_f,
            slope_f,
            w_outer,
            outer_part,
            inner_part,
            part_sums,
        ),
        halves + halves + [((8, units), f32)],
        scratch=[pltpu.VMEM((both, units), bf16)],
        name="feed_weights_far",
    )
    outer = Group(order, ids, "outer", 0, outer_keep)
    outer.got = swap(outer_send, "batch", 1)
    inner = Group(order, ids, "inner", 0, inner_keep)
    inner.got = swap(inner_send, "batch", 2)

    (token_part,) = order.call(
        token_grad_other_kernel,
        (),
        (dqx, dkx, dvx, wx, grad_one),
        [((both, model), f32)],
        name="token_grad_other",
    )
    dq, dk, dv, own_heads = order.call(
        attention_back_own_kernel,
        scalars,
        (
            *grads_one,
            tokens_in,
            other_tokens,
            w_output,
            q,
            k,
            v,
            probs,
            mixed_t,
            *row_sums,
            inner_sums,
        ),
        head_grads + group,
        scratch=head_scratch,
        name="attention_back_own",
    )
    heads = Group(order, ids, "heads", 16, own_heads)
    heads.got = got_heads
    tokens_sum = {}

    def token_grad():
        tokens_sum["keep"], send = order.call(
            token_grad_own_kernel,
            (),
            (dq, dk, dv, w_query, w_key, w_value, token_part),
            [((rows, model), f32), chunked(rows, model, "tokens")],
            name="token_grad_own",
        )
        tokens_sum["got"] = swap(send, "heads", 1)

    def token_out():
        (tokens_sum["out"],) = order.call(
            token_out_kernel,
            (),
            (tokens_sum["keep"], tokens_sum["got"]),
            [((rows, model), f32)],
            name="token_out",
        )

    def place(group, layout, shape):
        (group.whole,) = order.call(
            functools.partial(place_kernel, layout),
            (ids,),
            (group.pieces,),
            [(shape, f32)],
            name="place_" + group.name,
        )

    steps = {
        "outer_halve": lambda: outer.halve(2),
        "outer_quarter": outer.quarter,
        "outer_finish": lambda: outer.finish(PATHS[0]),
        "outer_place": lambda: place(outer, Y_FIRST, (units, model)),
        "inner_halve": lambda: inner.halve(1),
        "inner_quarter": inner.quarter,
        "inner_finish": lambda: inner.finish(PATHS[1]),
        "inner_place": lambda: place(inner, Z_FIRST, (model, units)),
        "heads_whole": lambda: heads.halve(HEADS_BITS[0]),
        "heads_halve": lambda: heads.halve(HEADS_BITS[1]),
        "heads_quarter": heads.quarter,
        "heads_finish": lambda: heads.finish(PATHS[2]),
        "token_grad": token_grad,
        "token_out": token_out,
    }
    for step in STEPS:
        steps[step]()
    grad_tokens, grad_w_outer, grad_w_inner = tokens_sum["out"], outer.whole, inner.whole
    (grad_o, grad_q, grad_k, grad_v), lines, biases = order.call(
        place_heads_kernel,
        (ids,),
        (heads.pieces, heads.vectors),
        [[((width, model), f32)] * 4, [((model,), f32)] * 7, [((width,), f32)] * 2],
        scratch=[pltpu.VMEM((4, width, model), f32)],
        name="place_heads",
    )

    return (
        block_out,
        grad_tokens,
        grad_q,
        biases[0],
        grad_k,
        grad_v,
        biases[1],
        grad_o,
        lines[0],
        lines[1],
        lines[2],
        grad_w_inner,
        lines[6],
        grad_w_outer,
        lines[3],
        lines[4],
        lines[5],
    )


def solution(mesh):
    placed = (
        P(("batch", "heads"), None),
        P(("batch", "heads"), None),
        P("batch"),
        P(),
        P("heads", None),
        P("heads"),
        P("heads", None),
        P("heads", None),
        P("heads"),
        P("heads", None),
        P(),
        P(),
        P(),
        P(None, "heads"),
        P("heads"),
        P("heads", None),
        P(),
        P(),
        P(),
    )
    return jax.shard_map(
        body,
        mesh=mesh,
        in_specs=placed,
        out_specs=(
            P(("batch", "heads"), None),
            P(("batch", "heads"), None),
            P("heads", None),
            P("heads"),
            P("heads", None),
            P("heads", None),
            P("heads"),
            P("heads", None),
            P(),
            P(),
            P(),
            P(None, "heads"),
            P("heads"),
            P("heads", None),
            P(),
            P(),
            P(),
        ),
        check_vma=False,
    )
```

```python
import functools

import jax
import jax.numpy as jnp
from jax import lax
from jax.experimental import pallas as pl
from jax.experimental.pallas import tpu as pltpu
from jax.sharding import PartitionSpec as P

HEAD_DIM = 64
HALF = 1024
SCALE = HEAD_DIM ** (-0.5)
epsilon = 1e-06

bf16 = jnp.bfloat16
f32 = jnp.float32


def dot_nn(left, right):
    return jnp.dot(left, right, preferred_element_type=f32)


def dot_nt(left, right):
    return lax.dot_general(left, right, (((1,), (1,)), ((), ())), preferred_element_type=f32)


def swap(value, axis, stride):
    size = lax.axis_size(axis)
    pairs = [(i, i ^ stride) for i in range(size)]
    return jax.tree.map(lambda part: lax.ppermute(part, axis, pairs), value)


def row(ref):
    return ref[...].reshape(1, -1).astype(f32)


VMEM_SPEC = pl.BlockSpec(memory_space=pltpu.VMEM)
SMEM_SPEC = pl.BlockSpec(memory_space=pltpu.SMEM)
ANY_SPEC = pl.BlockSpec(memory_space=pl.ANY)
HBM_SPEC = pl.BlockSpec(memory_space=pltpu.HBM)


PIECES = {"projected": 2, "normed": 4, "fed": 2, "grad_two": 1, "back": 4, "grad_one": 2, "tokens": 2}


def chunked(rows, cols, name):
    return [((rows // PIECES[name], cols), bf16)] * PIECES[name]


def whole(refs):
    return jnp.concatenate([ref[...] for ref in refs], axis=0)


def put(refs, value):
    rows = refs[0].shape[0]
    for number, ref in enumerate(refs):
        ref[...] = value[number * rows : (number + 1) * rows].astype(ref.dtype)


def after(value, *others):
    return lax.optimization_barrier((value, others))[0]


class Order:
    def __init__(self):
        self.last = None

    def call(self, kernel, scalars, inputs, outputs, **options):
        ins, tree = jax.tree.flatten(list(inputs))
        if self.last is not None:
            ins[0] = after(ins[0], self.last)
        results = call(kernel, scalars, jax.tree.unflatten(tree, ins), outputs, **options)
        self.last = min(jax.tree.leaves(results), key=lambda part: part.size)
        return results


def call(kernel, scalars, inputs, outputs, scratch=(), mib=12, name=None, remote=0, far=False, aliases=None):
    ins, in_tree = jax.tree.flatten(list(inputs))
    outs, out_tree = jax.tree.flatten(
        list(outputs), is_leaf=lambda entry: isinstance(entry, tuple)
    )
    out_shape = tuple(jax.ShapeDtypeStruct(shape, dtype) for shape, dtype in outs)
    near = len(ins) - remote
    first, second = len(scalars) + len(ins), len(scalars) + len(ins) + len(outs)

    def run(*refs):
        given = jax.tree.unflatten(in_tree, refs[len(scalars) : first])
        made = jax.tree.unflatten(out_tree, refs[first:second])
        kernel(*refs[: len(scalars)], *given, *made, *refs[second:])

    results = pl.pallas_call(
        run,
        out_shape=out_shape,
        in_specs=[SMEM_SPEC] * len(scalars) + [VMEM_SPEC] * near + [HBM_SPEC] * remote,
        out_specs=(ANY_SPEC if far else VMEM_SPEC,) * len(out_shape),
        scratch_shapes=list(scratch),
        input_output_aliases=aliases or {},
        compiler_params=pltpu.CompilerParams(vmem_limit_bytes=mib * 1024 * 1024),
        cost_estimate=pl.CostEstimate(flops=1000, bytes_accessed=1000, transcendentals=0),
        name=name,
    )(*scalars, *ins[:near], *(pltpu.with_memory_space_constraint(x, pltpu.HBM) for x in ins[near:]))
    return jax.tree.unflatten(out_tree, results)


def pack_attention_kernel(ids, wq, wk, wv, wo, out, sems):
    half = wq.shape[0] // 2
    at = pl.multiple_of(ids[1] * half, 16)
    copies = [
        pltpu.make_async_copy(
            weights.at[pl.ds(at, half), :],
            out.at[number * half : (number + 1) * half, :],
            sems.at[number],
        )
        for number, weights in enumerate((wq, wk, wv, wo))
    ]
    for copy in copies:
        copy.start()
    for copy in copies:
        copy.wait()


def vectors_kernel(bq, bv, bi, bo, gain1, shift1, bo2, gain2, shift2, table, lines):
    rows = [row(ref) for ref in (bo, gain1, shift1, bo2, gain2, shift2, bi)]
    heads = jnp.concatenate([row(bq), row(bv)], axis=1)
    half = lines.shape[1]
    table[...] = jnp.concatenate(
        rows + [jnp.concatenate([heads, jnp.zeros_like(heads)], axis=1)], axis=0
    )
    lines[...] = jnp.concatenate(
        [heads, rows[6][:, :half], rows[6][:, half:], jnp.zeros((13, half), f32)], axis=0
    ).astype(bf16)


OUTER_PIECES = 1


def pack_ffn_kernel(ids, lines, wi, wo, out_inner, out_outer, sems):
    model, half = wi.shape[0], wo.shape[0] // 2
    rows = out_outer[0].shape[0]
    at = pl.multiple_of(ids[1] * half, 64)
    cols = pl.ds(pl.multiple_of(ids[2] * half, 128), half)
    copies = [
        pltpu.make_async_copy(wi.at[:, cols], out_inner.at[:model, :], sems.at[0]),
        pltpu.make_async_copy(lines, out_inner.at[model:, :], sems.at[1]),
    ]
    for number, part in enumerate(out_outer):
        source = wo.at[pl.ds(at + number * rows, rows), :]
        copies.append(pltpu.make_async_copy(source, part, sems.at[2 + number]))
    for copy in copies:
        copy.start()
    for copy in copies:
        copy.wait()


def attend_blocks(ids, lengths, perm, owner, probs, visit, halves=(0, 1)):
    is_long = lengths[ids[0] // 2] == HALF
    swaps = [perm[owner * 3 + head, 0] for head in range(3)]

    @pl.when(is_long)
    def _():
        for block in halves:
            for head in range(3):
                kept = probs.at[head, block]
                visit(head, block * 512, (block ^ swaps[head]) * 512, 512, kept)

    @pl.when(jnp.logical_not(is_long))
    def _():
        @pl.loop(2 * halves[0], 2 * halves[-1] + 2)
        def _(block):
            for head in range(3):
                at = pl.multiple_of(block * 256, 256)
                cols = pl.ds(pl.multiple_of((block & 1) * 256, 256), 256)
                kept = probs.at[head, block >> 1, :256, cols]
                visit(head, at, (block ^ swaps[head]) * 256, 256, kept)


def attend_forward(ids, lengths, perm, owner, q_ref, k_ref, v_ref, probs, mixed, mixed_t):
    def visit(head, q_at, k_at, size, kept):
        cols = slice(head * HEAD_DIM, (head + 1) * HEAD_DIM)
        q_rows = pl.ds(q_at, size)
        k_rows = pl.ds(pl.multiple_of(k_at, 256), size)
        queries = q_ref[q_rows, cols] * SCALE
        scores_t = dot_nt(k_ref[k_rows, cols], queries.astype(bf16))
        weights_t = jnp.exp(scores_t - jnp.max(scores_t, axis=0, keepdims=True))
        total = jnp.sum(weights_t, axis=0, keepdims=True)
        probs_t = (weights_t * (1.0 / total)).astype(bf16)
        kept[...] = probs_t
        out_t = dot_nn(v_ref[k_rows, cols].T, probs_t).astype(bf16)
        mixed_t[cols, q_rows] = out_t
        mixed[q_rows, cols] = out_t.T

    attend_blocks(ids, lengths, perm, owner, probs, visit)


def project_qkv(tok_a, tok_b, weights, biases, outs):
    rows = tok_a.shape[0]
    for block, tok in enumerate((tok_a, tok_b)):
        at = slice(block * rows, (block + 1) * rows)
        for weight, bias, out in zip(weights, biases, outs):
            product = dot_nt(tok[...], weight[...])
            out[at, :] = (product if bias is None else product + bias).astype(bf16)


def fetch(sources, targets, sems):
    copies = [
        pltpu.make_async_copy(source, target, sems.at[number])
        for number, (source, target) in enumerate(zip(sources, targets))
    ]
    for copy in copies:
        copy.start()
    return copies


def attention_own_kernel(
    ids, lengths, perm, tok_a, tok_b, table, wq_far, wk_far, wv_far, wo_far,
    q, k, v, probs, mixed_t, part, mixed, wq, wk, wv, wo, sems,
):
    copies = fetch((wq_far, wk_far, wv_far, wo_far), (wq, wk, wv, wo), sems)
    for copy in copies:
        copy.wait()
    width = q.shape[1]
    biases = (table[7:8, :width], None, table[7:8, width : 2 * width])
    project_qkv(tok_a, tok_b, (wq, wk, wv), biases, (q, k, v))
    attend_forward(ids, lengths, perm, ids[0], q, k, v, probs, mixed, mixed_t)
    part[...] = dot_nn(mixed[...], wo[...])


def attention_other_kernel(
    ids, lengths, perm, tok_a, tok_b, first, second, lines, part,
    q, k, v, probs, mixed_t, wx, keep, send, mixed,
):
    width = q.shape[1]
    half = width // 2
    rows = keep.shape[0]
    mine = pl.multiple_of(ids[1] * half, 16)
    other = pl.multiple_of((1 - ids[1]) * half, 16)
    for number in range(4):
        wx[number, pl.ds(mine, half), :] = first[number * half : (number + 1) * half, :]
        wx[number, pl.ds(other, half), :] = second[number * half : (number + 1) * half, :]
    line = lines[-16:, :].astype(f32)[:1]
    biases = (line[:, :width], None, line[:, width : 2 * width])
    project_qkv(tok_a, tok_b, (wx.at[0], wx.at[1], wx.at[2]), biases, (q, k, v))
    attend_forward(ids, lengths, perm, ids[0] ^ 2, q, k, v, probs, mixed, mixed_t)
    keep[...] = part[:rows, :] + dot_nn(mixed[:rows, :], wx[3])
    put(send, part[rows:, :] + dot_nn(mixed[rows:, :], wx[3]))


def attend_backward_kernel(
    ids, lengths, perm, owner, q_ref, k_ref, v_ref, probs, grads_ref,
    dq, dk, dv, dqt, dkt, dvt, halves=(0, 1),
):
    def visit(head, q_at, k_at, size, kept):
        cols = slice(head * HEAD_DIM, (head + 1) * HEAD_DIM)
        q_rows = pl.ds(q_at, size)
        k_rows = pl.ds(pl.multiple_of(k_at, 256), size)
        queries = (q_ref[q_rows, cols] * SCALE).astype(bf16)
        keys = k_ref[k_rows, cols]
        grads = grads_ref[q_rows, cols]
        grad_probs_t = dot_nt(v_ref[k_rows, cols], grads)
        probs_t = kept[...]
        wide = probs_t.astype(f32)
        delta = jnp.sum(wide * grad_probs_t, axis=0, keepdims=True)
        grad_scores_t = (wide * (grad_probs_t - delta)).astype(bf16)
        grad_v = dot_nn(probs_t, grads).astype(bf16)
        grad_k = dot_nn(grad_scores_t, queries).astype(bf16)
        grad_q_t = (dot_nn(keys.T, grad_scores_t) * SCALE).astype(bf16)
        dv[k_rows, cols] = grad_v
        dk[k_rows, cols] = grad_k
        dq[q_rows, cols] = grad_q_t.T
        dvt[cols, k_rows] = grad_v.T
        dkt[cols, k_rows] = grad_k.T
        dqt[cols, q_rows] = grad_q_t

    attend_blocks(ids, lengths, perm, owner, probs, visit, halves)


def backward_attention(
    ids, lengths, perm, owner, g_a, g_b, wo, q, k, v, probs, dq, dk, dv, dqt, dkt, dvt, grads
):
    for at, g in row_blocks(g_a, g_b):
        grads[at, :] = dot_nt(g, wo).astype(bf16)
    attend_backward_kernel(
        ids, lengths, perm, owner, q, k, v, probs, grads, dq, dk, dv, dqt, dkt, dvt
    )


def row_sum(left_t):
    ones = jnp.ones((8, left_t.shape[1]), bf16)
    return dot_nt(ones, left_t)[:1]


def head_weight_grads(out, lefts, rights, vectors):
    width = lefts[0].shape[0]
    for number, (left, right) in enumerate(zip(lefts, rights)):
        out[number * width : (number + 1) * width, :] = dot_nn(left[...], right).astype(bf16)
    vectors = jnp.concatenate([vectors, jnp.zeros_like(vectors)], axis=0)
    out[len(lefts) * width :, :] = vectors.astype(bf16)


def bias_row(dqt, dvt):
    width = dqt.shape[0]
    return jnp.concatenate(
        [row_sum(dqt[...]), row_sum(dvt[...]), jnp.zeros((1, 2 * width), f32)], axis=1
    )


def attention_back_other_kernel(half, ids, lengths, perm, g, wx, q, k, v, probs, *refs):
    dq, dk, dv, dqt, dkt, dvt, grads = refs[-7:]
    rows = grads.shape[0] // 2
    grads[half * rows : (half + 1) * rows, :] = dot_nt(whole(g), wx[3]).astype(bf16)
    attend_backward_kernel(
        ids, lengths, perm, ids[0] ^ 2, q, k, v, probs, grads,
        dq, dk, dv, dqt, dkt, dvt, halves=(half,),
    )


def heads_grad_other_kernel(
    mixed_t, dqt, dkt, dvt, g_a, g_b, tok_a, tok_b, sums, got_sums, out
):
    vectors = jnp.concatenate([sums[:7] + got_sums[:7], bias_row(dqt, dvt)], axis=0)
    tokens = whole([tok_a, tok_b])
    rights = (whole(g_a + g_b), tokens, tokens, tokens)
    head_weight_grads(out, (mixed_t, dqt, dkt, dvt), rights, vectors)


def attention_back_own_kernel(
    ids, lengths, perm, g_a, g_b, tok_a, tok_b, wo, q, k, v, probs, mixed_t, sums, got_sums, inner_sums,
    dq, dk, dv, out, dqt, dkt, dvt, grads,
):
    backward_attention(
        ids, lengths, perm, ids[0], g_a, g_b, wo[...], q, k, v, probs,
        dq, dk, dv, dqt, dkt, dvt, grads,
    )
    vectors = jnp.concatenate(
        [sums[:6] + got_sums[:6], inner_sums[:1], bias_row(dqt, dvt)], axis=0
    )
    tokens = whole([tok_a, tok_b])
    rights = (whole(g_a + g_b), tokens, tokens, tokens)
    head_weight_grads(out, (mixed_t, dqt, dkt, dvt), rights, vectors)


def token_grad_other_kernel(dq, dk, dv, wx, grad_one, out):
    rows = grad_one.shape[0]
    total = dot_nn(dq[...], wx[0]) + dot_nn(dk[...], wx[1]) + dot_nn(dv[...], wx[2])
    out[:rows, :] = total[:rows, :] + grad_one[...]
    out[rows:, :] = total[rows:, :]


def token_grad_own_kernel(dq, dk, dv, wq, wk, wv, part, keep, send):
    rows = keep.shape[0]
    total = dot_nn(dq[...], wq[...]) + dot_nn(dk[...], wk[...]) + dot_nn(dv[...], wv[...])
    put(send, part[rows:, :] + total[rows:, :])
    keep[...] = part[:rows, :] + total[:rows, :]


def normalize(hidden):
    center = jnp.mean(hidden, axis=1, keepdims=True)
    rinv = lax.rsqrt(jnp.mean(hidden * hidden, axis=1, keepdims=True) - center * center + epsilon)
    return (hidden - center) * rinv, rinv


def norm_back(grad_zhat, zhat, rinv):
    first_mean = jnp.mean(grad_zhat, axis=1, keepdims=True)
    second_mean = jnp.mean(grad_zhat * zhat, axis=1, keepdims=True)
    return rinv * (grad_zhat - first_mean - zhat * second_mean)


def norm_one_kernel(tokens, keep, got, table, hidden, normed, normed_all, normed_bf):
    value = tokens[...].astype(f32) + keep[...] + whole(got).astype(f32) + table[0:1, :]
    hidden[...] = value
    zhat, _ = normalize(value)
    result = zhat * table[1:2, :] + table[2:3, :]
    normed[...] = result
    normed_all[...] = result.astype(bf16)
    put(normed_bf, result)


def norm_two_kernel(
    normed, keep, got, table, cotangent,
    block_out, grad_two, grad_two_all, grad_two_bf, sums,
):
    hidden = normed[...] + keep[...] + whole(got).astype(f32) + table[3:4, :]
    zhat, rinv = normalize(hidden)
    block_out[...] = (zhat * table[4:5, :] + table[5:6, :]).astype(bf16)
    grad_out = cotangent[...].astype(f32)
    grad = norm_back(grad_out * table[4:5, :], zhat, rinv)
    grad_two[...] = grad
    grad_two_all[...] = grad.astype(bf16)
    put(grad_two_bf, grad)
    sums[...] = jnp.concatenate(
        [
            jnp.sum(grad, axis=0, keepdims=True),
            jnp.sum(grad_out * zhat, axis=0, keepdims=True),
            jnp.sum(grad_out, axis=0, keepdims=True),
            jnp.zeros((5, grad.shape[1]), f32),
        ],
        axis=0,
    )


def norm_one_back_kernel(grad_two, keep, got, hidden, table, sums_in, grad_one, grad_one_bf, sums):
    grad_normed = grad_two[...] + keep[...] + whole(got).astype(f32)
    zhat, rinv = normalize(hidden[...])
    grad = norm_back(grad_normed * table[1:2, :], zhat, rinv)
    grad_one[...] = grad
    put(grad_one_bf, grad)
    sums[...] = jnp.concatenate(
        [
            jnp.sum(grad, axis=0, keepdims=True),
            jnp.sum(grad_normed * zhat, axis=0, keepdims=True),
            jnp.sum(grad_normed, axis=0, keepdims=True),
            sums_in[:3],
            jnp.zeros((2, grad.shape[1]), f32),
        ],
        axis=0,
    )


def gelu_parts(values):
    cdf = 0.5 + 0.5 * lax.erf(values * 0.7071067811865476)
    bell = jnp.exp2((-0.5 * 1.4426950408889634) * (values * values))
    return values * cdf, cdf + values * (bell * 0.3989422804014327)


BLOCK = 256


def row_blocks(*sources):
    at = 0
    for source in sources:
        step = max(1, BLOCK // source[0].shape[0])
        for start in range(0, len(source), step):
            block = whole(source[start : start + step])
            yield slice(at, at + block.shape[0]), block
            at += block.shape[0]


def feed_own_kernel(nrm_a, nrm_b, wi, table, wo, active_t, slope, part, normed_t):
    for at, normed in row_blocks(nrm_a, nrm_b):
        normed_t[:, at] = normed.T
        value, rise = gelu_parts(dot_nn(normed, wi[...]) + table[6:7, :])
        part[at, :] = dot_nn(value.astype(bf16), wo[...])
        active_t[:, at] = value.astype(bf16).T
        slope[at, :] = rise.astype(bf16)


def feed_other_kernel(ids, nrm, wi_a, wi_b, wo_a, wo_b, part, slope, send, wi_x, wo_x):
    half, model = wi_a.shape[1], wo_x.shape[1]
    for bit, weights in ((ids[2], wi_a), (1 - ids[2], wi_b)):
        wi_x[:, pl.ds(pl.multiple_of(bit * half, 128), half)] = weights[:model, :]
    for bit, weights in ((ids[1], wo_a), (1 - ids[1], wo_b)):
        wo_x[pl.ds(pl.multiple_of(bit * half, 128), half), :] = whole(weights)
    rows = slope.shape[0]
    feed_units(nrm, wi_a, wi_x, wo_x, part.at[rows:, :], slope, lambda at, total: put_rows(send, at, total))


def feed_other_own_kernel(nrm, lines, wi_x, wo_x, part, slope, keep):
    def store(at, total):
        keep[at, :] = total

    feed_units(nrm, lines, wi_x, wo_x, part, slope, store)


def put_rows(refs, at, value):
    size = refs[0].shape[0]
    put(refs[at.start // size : at.stop // size], value)


def feed_units(nrm, lines, wi, wo, part, slope, store):
    line = lines[-16:, :].astype(f32)
    bias = jnp.concatenate([line[1:2], line[2:3]], axis=1)
    for at, normed in row_blocks(nrm):
        value, rise = gelu_parts(dot_nn(normed, wi[...]) + bias)
        slope[at, :] = rise.astype(bf16)
        store(at, part[at, :] + dot_nn(value.astype(bf16), wo[...]))


def feed_far_kernel(nrm_a, nrm_b, wi, table, active_t, slope, normed_t):
    for at, normed in row_blocks(nrm_a, nrm_b):
        normed_t[:, at] = normed.T
        value, rise = gelu_parts(dot_nn(normed, wi[...]) + table[6:7, :])
        active_t[:, at] = value.astype(bf16).T
        slope[at, :] = rise.astype(bf16)


def feed_back_kernel(half, g, slope, slope_x, wi, wo, wi_x, wo_x, grad_inner, out):
    rows = grad_inner.shape[0]
    grad = whole(g)
    rise = slope[half * rows : (half + 1) * rows, :].astype(f32)
    grad_inner[...] = (dot_nt(grad, wo[...]) * rise).astype(bf16)
    grad_x = (dot_nt(grad, wo_x[...]) * slope_x[...].astype(f32)).astype(bf16)
    total = dot_nt(grad_inner[...], wi[...]) + dot_nt(grad_x, wi_x[...])
    if half:
        put(out, total)
    else:
        out[...] = total


def feed_weights_kernel(g_a, g_b, active_t, normed_t, grad_inner, outer, inner, sums):
    outer[...] = dot_nn(active_t[...], whole(g_a + g_b))
    grads = whole(grad_inner)
    inner[...] = dot_nn(normed_t[...], grads)
    sums[...] = dot_nn(jnp.ones((8, grads.shape[0]), bf16), grads)


def feed_weights_far_kernel(
    ids, g_a, g_b, active_t, normed_t, slope, wo, outer, inner, sums_in,
    outer_keep, outer_send, inner_keep, inner_send, sums, grad_inner,
):
    for at, g in row_blocks(g_a, g_b):
        grad_inner[at, :] = (dot_nt(g, wo[...]) * slope[at, :].astype(f32)).astype(bf16)
    grads = whole(g_a + g_b)
    half = outer_keep.shape[0]
    for index, target in ((1 - ids[1], outer_send), (ids[1], outer_keep)):
        at = pl.ds(pl.multiple_of(index * half, 128), half)
        target[...] = (dot_nn(active_t[at, :], grads) + outer[at, :]).astype(target.dtype)
    for index, target in ((1 - ids[2], inner_send), (ids[2], inner_keep)):
        at = pl.ds(pl.multiple_of(index * half, 128), half)
        target[...] = (dot_nn(normed_t[at, :], grad_inner[...]) + inner[at, :]).astype(
            target.dtype
        )
    sums[...] = sums_in[...] + dot_nn(
        jnp.ones((8, grad_inner.shape[0]), bf16), grad_inner[...]
    )


Y_FIRST = (4, (0, 2, 1, 3))
Z_FIRST = (3, (0, 1, 2, 3))


def quarter_rows(ids, layout, number, rows):
    index, numbers = layout
    return pl.ds(pl.multiple_of((ids[index] ^ numbers[number]) * rows, 16), rows)


def halve_kernel(which, extra, ids, kept, got, keep, send):
    body = kept.shape[0] - extra
    half = body // 2
    bit = ids[which]
    for index, target in ((1 - bit, send), (bit, keep)):
        at = pl.ds(pl.multiple_of(index * half, 16), half)
        target[:half, :] = (kept[at, :].astype(f32) + got[at, :].astype(f32)).astype(target.dtype)
    if extra:
        total = (kept[body:, :].astype(f32) + got[body:, :].astype(f32)).astype(bf16)
        send[half:, :] = total
        keep[half:, :] = total.astype(f32)


def add_two_kernel(kept, got, out):
    out[...] = (kept[...].astype(f32) + got[...].astype(f32)).astype(bf16)


def add_last_kernel(kept, got, out, vectors):
    rows = out.shape[0]
    total = kept[...].astype(f32) + got[...].astype(f32)
    out[...] = total[:rows, :].astype(bf16)
    vectors[...] = total[rows:, :]


def token_out_kernel(kept, got, out):
    out[...] = kept[...] + whole(got).astype(f32)


STEPS = (
    "token_grad",
    "outer_halve",
    "inner_halve",
    "heads_whole",
    "inner_quarter",
    "outer_quarter",
    "token_out",
    "heads_halve",
    "inner_finish",
    "outer_finish",
    "heads_quarter",
    "heads_finish",
    "inner_place",
    "outer_place",
)
PATHS = ("direct", "y", "direct")
HEADS_BITS = (1, 2)


class Group:
    def __init__(self, order, ids, name, extra, keep):
        self.order, self.ids, self.name, self.extra = order, ids, name, extra
        self.keep = keep

    def halve(self, bit):
        rows, cols = self.keep.shape
        half = (rows - self.extra) // 2 + self.extra
        self.keep, send = self.order.call(
            functools.partial(halve_kernel, bit, self.extra),
            (self.ids,),
            (self.keep, self.got),
            [((half, cols), f32), ((half, cols), bf16)],
            name=self.name + "_halve",
        )
        self.got = swap(send, "batch", bit)

    def quarter(self):
        (self.keep,) = self.order.call(
            add_two_kernel,
            (),
            (self.keep, self.got),
            [(self.keep.shape, bf16)],
            name=self.name + "_quarter",
        )
        stride = 4
        while 2 * stride < lax.axis_size("batch"):
            (self.keep,) = self.order.call(
                add_two_kernel,
                (),
                (self.keep, swap(self.keep, "batch", stride)),
                [(self.keep.shape, bf16)],
                name=self.name + "_%d" % stride,
            )
            stride *= 2
        self.got = swap(self.keep, "batch", stride)

    def finish(self, path):
        rows, cols = self.keep.shape
        outputs = [((rows - self.extra, cols), bf16)]
        if self.extra:
            outputs.append(((self.extra, cols), f32))
        results = self.order.call(
            add_last_kernel if self.extra else add_two_kernel,
            (),
            (self.keep, self.got),
            outputs,
            name=self.name + "_finish",
        )
        self.vectors = results[-1]
        mine = results[0]
        far, near = swap(mine, "batch", 1), swap(mine, "batch", 2)
        if path == "direct":
            across = swap(mine, "batch", 3)
        elif path == "y":
            across = swap(after(near, far), "batch", 1)
        else:
            across = swap(after(far, near), "batch", 2)
        self.pieces = [mine, far, near, across]


def place_kernel(layout, ids, pieces, out):
    rows = pieces[0].shape[0]
    for number, part in enumerate(pieces):
        out[quarter_rows(ids, layout, number, rows), :] = part[...].astype(f32)


def place_heads_kernel(ids, pieces, vectors, grads, lines, biases, scratch):
    index, numbers = Y_FIRST if HEADS_BITS == (1, 2) else Z_FIRST
    for number, part in enumerate(pieces):
        scratch[ids[index] ^ numbers[number]] = part[...].astype(f32)
    for number, out in enumerate(grads):
        out[...] = scratch[number]
    for number, out in enumerate(lines):
        out[...] = vectors[number : number + 1, :].reshape(out.shape)
    for number, out in enumerate(biases):
        width = out.shape[0]
        line = vectors[7:8, number * width : (number + 1) * width]
        out[...] = line.reshape(out.shape)


def body(
    tokens_in,
    cotangent,
    half_length,
    block_perm,
    w_query,
    b_query,
    w_key,
    w_value,
    b_value,
    w_output,
    b_output,
    norm1_gain,
    norm1_shift,
    w_inner,
    b_inner,
    w_outer,
    b_outer,
    norm2_gain,
    norm2_shift,
):
    width = w_query.shape[0]
    model = w_query.shape[1]
    units = w_outer.shape[0]
    rows = tokens_in.shape[0]
    both = 2 * rows
    half = model // 2
    index = lax.axis_index("batch")
    ids = jnp.stack(
        [
            lax.axis_index("heads"),
            index & 1,
            (index >> 1) & 1,
            index & 3,
            (index & 1) * 2 + ((index >> 1) & 1),
        ]
    ).astype(jnp.int32)
    scalars = (ids, half_length, block_perm)
    order = Order()

    (packed,) = order.call(
        pack_attention_kernel,
        (ids,),
        (w_query, w_key, w_value, w_output),
        [((2 * width, model), bf16)],
        scratch=[pltpu.SemaphoreType.DMA((4,))],
        name="pack_attention",
        remote=4,
        far=True,
    )
    first = swap(packed, "heads", 2)
    other_tokens = swap(tokens_in, "heads", 1)
    table, lines = order.call(
        vectors_kernel,
        (),
        (
            b_query,
            b_value,
            b_inner,
            b_output,
            norm1_gain,
            norm1_shift,
            b_outer,
            norm2_gain,
            norm2_shift,
        ),
        [((8, model), f32), ((16, half), bf16)],
        name="vectors",
    )
    inner_half, outer_half = order.call(
        pack_ffn_kernel,
        (ids,),
        (lines, w_inner, w_outer),
        [
            ((model + 16, units // 2), bf16),
            [((units // 2 // OUTER_PIECES, model), bf16)] * OUTER_PIECES,
        ],
        scratch=[pltpu.SemaphoreType.DMA((2 + OUTER_PIECES,))],
        name="pack_ffn",
        remote=2,
    )
    inner_a = swap(inner_half, "heads", 2)
    outer_a = swap(outer_half, "heads", 2)
    second = swap(first, "batch", 1)
    inner_b = swap(inner_a, "batch", 2)
    outer_b = swap(outer_a, "batch", 1)

    head_outputs = [
        ((both, width), bf16),
        ((both, width), bf16),
        ((both, width), bf16),
        ((3, 2, both // 2, both // 2), bf16),
        ((width, both), bf16),
    ]
    mixed = pltpu.VMEM((both, width), bf16)
    q, k, v, probs, mixed_t, part = order.call(
        attention_own_kernel,
        scalars,
        (tokens_in, other_tokens, table, w_query, w_key, w_value, w_output),
        head_outputs + [((both, model), f32)],
        scratch=[mixed]
        + [pltpu.VMEM((width, model), bf16)] * 4
        + [pltpu.SemaphoreType.DMA((4,))],
        name="attention_own",
        remote=4,
    )
    qx, kx, vx, probs_x, mixed_tx, wx, keep, send = order.call(
        attention_other_kernel,
        scalars,
        (tokens_in, other_tokens, first, after(second, inner_a), inner_a, part),
        head_outputs
        + [((4, width, model), bf16), ((rows, model), f32), chunked(rows, model, "projected")],
        scratch=[mixed],
        name="attention_other",
    )
    hidden_one, normed, normed_all, normed_bf = order.call(
        norm_one_kernel,
        (),
        (
            tokens_in,
            keep,
            after(swap(send, "heads", 1), outer_a),
            table,
        ),
        [
            ((rows, model), f32),
            ((rows, model), f32),
            ((rows, model), bf16),
            chunked(rows, model, "normed"),
        ],
        name="norm_one",
    )

    other_normed = swap(normed_bf, "heads", 1)
    far_normed = swap([normed_all], "heads", 2)
    active_t, slope, part, normed_t = order.call(
        feed_own_kernel,
        (),
        (normed_bf, other_normed, w_inner, table, w_outer),
        [
            ((units, both), bf16),
            ((both, units), bf16),
            ((both, model), f32),
            ((model, both), bf16),
        ],
        name="feed_own",
    )
    slope_xb, send, wi_x, wo_x = order.call(
        feed_other_kernel,
        (ids,),
        (other_normed, inner_a, inner_b, outer_a, outer_b, part),
        [
            ((rows, units), bf16),
            chunked(rows, model, "fed"),
            ((model, units), bf16),
            ((units, model), bf16),
        ],
        name="feed_other",
    )
    slope_xa, keep = order.call(
        feed_other_own_kernel,
        (),
        (normed_bf, inner_a, wi_x, wo_x, part),
        [((rows, units), bf16), ((rows, model), f32)],
        name="feed_other_own",
    )
    block_out, grad_two, grad_two_all, grad_two_bf, sums_two = order.call(
        norm_two_kernel,
        (),
        (
            normed,
            keep,
            swap(send, "heads", 1),
            table,
            cotangent,
        ),
        [
            ((rows, model), bf16),
            ((rows, model), f32),
            ((rows, model), bf16),
            chunked(rows, model, "grad_two"),
            ((8, model), f32),
        ],
        name="norm_two",
    )

    far_normed = after(far_normed, sums_two)
    far_other_normed = swap(far_normed, "heads", 1)
    other_grad_two = swap(grad_two_bf, "heads", 1)
    far_grad_two = swap([grad_two_all], "heads", 2)
    grad_inner = [None, None]
    grad_inner[0], keep = order.call(
        functools.partial(feed_back_kernel, 0),
        (),
        (grad_two_bf, slope, slope_xa, w_inner, w_outer, wi_x, wo_x),
        [((rows, units), bf16), ((rows, model), f32)],
        name="feed_back_own",
    )
    grad_inner[1], send = order.call(
        functools.partial(feed_back_kernel, 1),
        (),
        (other_grad_two, slope, slope_xb, w_inner, w_outer, wi_x, wo_x),
        [((rows, units), bf16), chunked(rows, model, "back")],
        name="feed_back_other",
    )
    active_f, slope_f, normed_f = order.call(
        feed_far_kernel,
        (),
        (far_normed, far_other_normed, w_inner, table),
        [((units, both), bf16), ((both, units), bf16), ((model, both), bf16)],
        name="feed_far",
    )
    grad_one, grad_one_bf, sums_one = order.call(
        norm_one_back_kernel,
        (),
        (grad_two, keep, swap(send, "heads", 1), hidden_one, table, sums_two),
        [((rows, model), f32), chunked(rows, model, "grad_one"), ((8, model), f32)],
        name="norm_one_back",
    )

    grads_one = (grad_one_bf, swap(grad_one_bf, "heads", 1))
    row_sums = (sums_one, swap(sums_one, "heads", 1))
    grads_one = (grads_one[0], after(grads_one[1], row_sums[1]))
    head_grads = [((both, width), bf16)] * 3
    group = [((4 * width + 16, model), bf16)]
    head_scratch = [pltpu.VMEM((width, both), bf16)] * 3 + [pltpu.VMEM((both, width), bf16)]
    head_blocks = [((both, width), bf16)] * 3 + [((width, both), bf16)] * 3
    results = []
    for number in range(2):
        results = order.call(
            functools.partial(attention_back_other_kernel, number),
            scalars,
            (grads_one[number], wx, qx, kx, vx, probs_x, *results),
            head_blocks,
            scratch=[pltpu.VMEM((both, width), bf16)],
            name="attention_back_other",
            aliases={
                3 + len(grads_one[number]) + 5 + i: i for i in range(6) if len(results) > 0
            },
        )
    dqx, dkx, dvx, *back_t = results
    far_grad_two = after(far_grad_two, dqx)
    far_other_grad_two = swap(far_grad_two, "heads", 1)
    (far_heads,) = order.call(
        heads_grad_other_kernel,
        (),
        (mixed_tx, *back_t, *grads_one, tokens_in, other_tokens, *row_sums),
        group,
        name="heads_grad_other",
    )
    got_heads = swap(far_heads, "heads", 2)

    outer_part, inner_part, part_sums = order.call(
        feed_weights_kernel,
        (),
        (grad_two_bf, other_grad_two, active_t, normed_t, grad_inner),
        [((units, model), f32), ((model, units), f32), ((8, units), f32)],
        name="feed_weights",
    )
    halves = [((units // 2, model), f32), ((units // 2, model), bf16)]
    outer_keep, outer_send, inner_keep, inner_send, inner_sums = order.call(
        feed_weights_far_kernel,
        (ids,),
        (
            far_grad_two,
            far_other_grad_two,
            active_f,
            normed_f,
            slope_f,
            w_outer,
            outer_part,
            inner_part,
            part_sums,
        ),
        halves + halves + [((8, units), f32)],
        scratch=[pltpu.VMEM((both, units), bf16)],
        name="feed_weights_far",
    )
    outer = Group(order, ids, "outer", 0, outer_keep)
    outer.got = swap(outer_send, "batch", 1)
    inner = Group(order, ids, "inner", 0, inner_keep)
    inner.got = swap(inner_send, "batch", 2)

    (token_part,) = order.call(
        token_grad_other_kernel,
        (),
        (dqx, dkx, dvx, wx, grad_one),
        [((both, model), f32)],
        name="token_grad_other",
    )
    dq, dk, dv, own_heads = order.call(
        attention_back_own_kernel,
        scalars,
        (
            *grads_one,
            tokens_in,
            other_tokens,
            w_output,
            q,
            k,
            v,
            probs,
            mixed_t,
            *row_sums,
            inner_sums,
        ),
        head_grads + group,
        scratch=head_scratch,
        name="attention_back_own",
    )
    heads = Group(order, ids, "heads", 16, own_heads)
    heads.got = got_heads
    tokens_sum = {}

    def token_grad():
        tokens_sum["keep"], send = order.call(
            token_grad_own_kernel,
            (),
            (dq, dk, dv, w_query, w_key, w_value, token_part),
            [((rows, model), f32), chunked(rows, model, "tokens")],
            name="token_grad_own",
        )
        tokens_sum["send"] = send

    def token_out():
        tokens_sum["got"] = swap(after(tokens_sum["send"], order.last), "heads", 1)
        (tokens_sum["out"],) = order.call(
            token_out_kernel,
            (),
            (tokens_sum["keep"], tokens_sum["got"]),
            [((rows, model), f32)],
            name="token_out",
        )

    def place(group, layout, shape):
        (group.whole,) = order.call(
            functools.partial(place_kernel, layout),
            (ids,),
            (group.pieces,),
            [(shape, f32)],
            name="place_" + group.name,
        )

    steps = {
        "outer_halve": lambda: outer.halve(2),
        "outer_quarter": outer.quarter,
        "outer_finish": lambda: outer.finish(PATHS[0]),
        "outer_place": lambda: place(outer, Y_FIRST, (units, model)),
        "inner_halve": lambda: inner.halve(1),
        "inner_quarter": inner.quarter,
        "inner_finish": lambda: inner.finish(PATHS[1]),
        "inner_place": lambda: place(inner, Z_FIRST, (model, units)),
        "heads_whole": lambda: heads.halve(HEADS_BITS[0]),
        "heads_halve": lambda: heads.halve(HEADS_BITS[1]),
        "heads_quarter": heads.quarter,
        "heads_finish": lambda: heads.finish(PATHS[2]),
        "token_grad": token_grad,
        "token_out": token_out,
    }
    for step in STEPS:
        steps[step]()
    grad_tokens, grad_w_outer, grad_w_inner = tokens_sum["out"], outer.whole, inner.whole
    (grad_o, grad_q, grad_k, grad_v), lines, biases = order.call(
        place_heads_kernel,
        (ids,),
        (heads.pieces, heads.vectors),
        [[((width, model), f32)] * 4, [((model,), f32)] * 7, [((width,), f32)] * 2],
        scratch=[pltpu.VMEM((4, width, model), f32)],
        name="place_heads",
    )

    return (
        block_out,
        grad_tokens,
        grad_q,
        biases[0],
        grad_k,
        grad_v,
        biases[1],
        grad_o,
        lines[0],
        lines[1],
        lines[2],
        grad_w_inner,
        lines[6],
        grad_w_outer,
        lines[3],
        lines[4],
        lines[5],
    )


def solution(mesh):
    placed = (
        P(("batch", "heads"), None),
        P(("batch", "heads"), None),
        P("batch"),
        P(),
        P("heads", None),
        P("heads"),
        P("heads", None),
        P("heads", None),
        P("heads"),
        P("heads", None),
        P(),
        P(),
        P(),
        P(None, "heads"),
        P("heads"),
        P("heads", None),
        P(),
        P(),
        P(),
    )
    return jax.shard_map(
        body,
        mesh=mesh,
        in_specs=placed,
        out_specs=(
            P(("batch", "heads"), None),
            P(("batch", "heads"), None),
            P("heads", None),
            P("heads"),
            P("heads", None),
            P("heads", None),
            P("heads"),
            P("heads", None),
            P(),
            P(),
            P(),
            P(None, "heads"),
            P("heads"),
            P("heads", None),
            P(),
            P(),
            P(),
        ),
        check_vma=False,
    )
```

```python
import functools

import jax
import jax.numpy as jnp
from jax import lax
from jax.experimental import pallas as pl
from jax.experimental.pallas import tpu as pltpu
from jax.sharding import PartitionSpec as P

HEAD_DIM = 64
HALF = 1024
SCALE = HEAD_DIM ** (-0.5)
epsilon = 1e-06

bf16 = jnp.bfloat16
f32 = jnp.float32


def dot_nn(left, right):
    return jnp.dot(left, right, preferred_element_type=f32)


def dot_nt(left, right):
    return lax.dot_general(left, right, (((1,), (1,)), ((), ())), preferred_element_type=f32)


def swap(value, axis, stride):
    size = lax.axis_size(axis)
    pairs = [(i, i ^ stride) for i in range(size)]
    return jax.tree.map(lambda part: lax.ppermute(part, axis, pairs), value)


def row(ref):
    return ref[...].reshape(1, -1).astype(f32)


VMEM_SPEC = pl.BlockSpec(memory_space=pltpu.VMEM)
SMEM_SPEC = pl.BlockSpec(memory_space=pltpu.SMEM)
ANY_SPEC = pl.BlockSpec(memory_space=pl.ANY)
HBM_SPEC = pl.BlockSpec(memory_space=pltpu.HBM)


PIECES = {"projected": 2, "normed": 4, "fed": 2, "grad_two": 1, "back": 4, "grad_one": 2, "tokens": 2}


def chunked(rows, cols, name):
    return [((rows // PIECES[name], cols), bf16)] * PIECES[name]


def whole(refs):
    return jnp.concatenate([ref[...] for ref in refs], axis=0)


def put(refs, value):
    rows = refs[0].shape[0]
    for number, ref in enumerate(refs):
        ref[...] = value[number * rows : (number + 1) * rows].astype(ref.dtype)


def after(value, *others):
    return lax.optimization_barrier((value, others))[0]


class Order:
    def __init__(self):
        self.last = None

    def call(self, kernel, scalars, inputs, outputs, **options):
        ins, tree = jax.tree.flatten(list(inputs))
        if self.last is not None:
            ins[0] = after(ins[0], self.last)
        results = call(kernel, scalars, jax.tree.unflatten(tree, ins), outputs, **options)
        self.last = min(jax.tree.leaves(results), key=lambda part: part.size)
        return results


def call(kernel, scalars, inputs, outputs, scratch=(), mib=12, name=None, remote=0, far=False, aliases=None):
    ins, in_tree = jax.tree.flatten(list(inputs))
    outs, out_tree = jax.tree.flatten(
        list(outputs), is_leaf=lambda entry: isinstance(entry, tuple)
    )
    out_shape = tuple(jax.ShapeDtypeStruct(shape, dtype) for shape, dtype in outs)
    near = len(ins) - remote
    first, second = len(scalars) + len(ins), len(scalars) + len(ins) + len(outs)

    def run(*refs):
        given = jax.tree.unflatten(in_tree, refs[len(scalars) : first])
        made = jax.tree.unflatten(out_tree, refs[first:second])
        kernel(*refs[: len(scalars)], *given, *made, *refs[second:])

    results = pl.pallas_call(
        run,
        out_shape=out_shape,
        in_specs=[SMEM_SPEC] * len(scalars) + [VMEM_SPEC] * near + [HBM_SPEC] * remote,
        out_specs=(ANY_SPEC if far else VMEM_SPEC,) * len(out_shape),
        scratch_shapes=list(scratch),
        input_output_aliases=aliases or {},
        compiler_params=pltpu.CompilerParams(vmem_limit_bytes=mib * 1024 * 1024),
        cost_estimate=pl.CostEstimate(flops=1000, bytes_accessed=1000, transcendentals=0),
        name=name,
    )(*scalars, *ins[:near], *(pltpu.with_memory_space_constraint(x, pltpu.HBM) for x in ins[near:]))
    return jax.tree.unflatten(out_tree, results)


def pack_attention_kernel(ids, wq, wk, wv, wo, out, sems):
    half = wq.shape[0] // 2
    at = pl.multiple_of(ids[1] * half, 16)
    copies = [
        pltpu.make_async_copy(
            weights.at[pl.ds(at, half), :],
            out.at[number * half : (number + 1) * half, :],
            sems.at[number],
        )
        for number, weights in enumerate((wq, wk, wv, wo))
    ]
    for copy in copies:
        copy.start()
    for copy in copies:
        copy.wait()


def vectors_kernel(bq, bv, bi, bo, gain1, shift1, bo2, gain2, shift2, table, lines):
    rows = [row(ref) for ref in (bo, gain1, shift1, bo2, gain2, shift2, bi)]
    heads = jnp.concatenate([row(bq), row(bv)], axis=1)
    half = lines.shape[1]
    table[...] = jnp.concatenate(
        rows + [jnp.concatenate([heads, jnp.zeros_like(heads)], axis=1)], axis=0
    )
    lines[...] = jnp.concatenate(
        [heads, rows[6][:, :half], rows[6][:, half:], jnp.zeros((13, half), f32)], axis=0
    ).astype(bf16)


OUTER_PIECES = 1


def pack_ffn_kernel(ids, lines, wi, wo, out_inner, out_outer, sems):
    model, half = wi.shape[0], wo.shape[0] // 2
    rows = out_outer[0].shape[0]
    at = pl.multiple_of(ids[1] * half, 64)
    cols = pl.ds(pl.multiple_of(ids[2] * half, 128), half)
    copies = [
        pltpu.make_async_copy(wi.at[:, cols], out_inner.at[:model, :], sems.at[0]),
        pltpu.make_async_copy(lines, out_inner.at[model:, :], sems.at[1]),
    ]
    for number, part in enumerate(out_outer):
        source = wo.at[pl.ds(at + number * rows, rows), :]
        copies.append(pltpu.make_async_copy(source, part, sems.at[2 + number]))
    for copy in copies:
        copy.start()
    for copy in copies:
        copy.wait()


def attend_blocks(ids, lengths, perm, owner, probs, visit, halves=(0, 1)):
    is_long = lengths[ids[0] // 2] == HALF
    swaps = [perm[owner * 3 + head, 0] for head in range(3)]

    @pl.when(is_long)
    def _():
        for block in halves:
            for head in range(3):
                kept = probs.at[head, block]
                visit(head, block * 512, (block ^ swaps[head]) * 512, 512, kept)

    @pl.when(jnp.logical_not(is_long))
    def _():
        @pl.loop(2 * halves[0], 2 * halves[-1] + 2)
        def _(block):
            for head in range(3):
                at = pl.multiple_of(block * 256, 256)
                cols = pl.ds(pl.multiple_of((block & 1) * 256, 256), 256)
                kept = probs.at[head, block >> 1, :256, cols]
                visit(head, at, (block ^ swaps[head]) * 256, 256, kept)


def attend_forward(ids, lengths, perm, owner, q_ref, k_ref, v_ref, probs, mixed, mixed_t):
    def visit(head, q_at, k_at, size, kept):
        cols = slice(head * HEAD_DIM, (head + 1) * HEAD_DIM)
        q_rows = pl.ds(q_at, size)
        k_rows = pl.ds(pl.multiple_of(k_at, 256), size)
        queries = q_ref[q_rows, cols] * SCALE
        scores_t = dot_nt(k_ref[k_rows, cols], queries.astype(bf16))
        weights_t = jnp.exp(scores_t - jnp.max(scores_t, axis=0, keepdims=True))
        total = jnp.sum(weights_t, axis=0, keepdims=True)
        probs_t = (weights_t * (1.0 / total)).astype(bf16)
        kept[...] = probs_t
        out_t = dot_nn(v_ref[k_rows, cols].T, probs_t).astype(bf16)
        mixed_t[cols, q_rows] = out_t
        mixed[q_rows, cols] = out_t.T

    attend_blocks(ids, lengths, perm, owner, probs, visit)


def project_qkv(tok_a, tok_b, weights, biases, outs):
    rows = tok_a.shape[0]
    for block, tok in enumerate((tok_a, tok_b)):
        at = slice(block * rows, (block + 1) * rows)
        for weight, bias, out in zip(weights, biases, outs):
            product = dot_nt(tok[...], weight[...])
            out[at, :] = (product if bias is None else product + bias).astype(bf16)


def fetch(sources, targets, sems):
    copies = [
        pltpu.make_async_copy(source, target, sems.at[number])
        for number, (source, target) in enumerate(zip(sources, targets))
    ]
    for copy in copies:
        copy.start()
    return copies


def attention_own_kernel(
    ids, lengths, perm, tok_a, tok_b, table, wq_far, wk_far, wv_far, wo_far,
    q, k, v, probs, mixed_t, part, mixed, wq, wk, wv, wo, sems,
):
    copies = fetch((wq_far, wk_far, wv_far, wo_far), (wq, wk, wv, wo), sems)
    for copy in copies:
        copy.wait()
    width = q.shape[1]
    biases = (table[7:8, :width], None, table[7:8, width : 2 * width])
    project_qkv(tok_a, tok_b, (wq, wk, wv), biases, (q, k, v))
    attend_forward(ids, lengths, perm, ids[0], q, k, v, probs, mixed, mixed_t)
    part[...] = dot_nn(mixed[...], wo[...])


def attention_other_kernel(
    ids, lengths, perm, tok_a, tok_b, first, second, lines, part,
    q, k, v, probs, mixed_t, wx, keep, send, mixed,
):
    width = q.shape[1]
    half = width // 2
    rows = keep.shape[0]
    mine = pl.multiple_of(ids[1] * half, 16)
    other = pl.multiple_of((1 - ids[1]) * half, 16)
    for number in range(4):
        wx[number, pl.ds(mine, half), :] = first[number * half : (number + 1) * half, :]
        wx[number, pl.ds(other, half), :] = second[number * half : (number + 1) * half, :]
    line = lines[-16:, :].astype(f32)[:1]
    biases = (line[:, :width], None, line[:, width : 2 * width])
    project_qkv(tok_a, tok_b, (wx.at[0], wx.at[1], wx.at[2]), biases, (q, k, v))
    attend_forward(ids, lengths, perm, ids[0] ^ 2, q, k, v, probs, mixed, mixed_t)
    keep[...] = part[:rows, :] + dot_nn(mixed[:rows, :], wx[3])
    put(send, part[rows:, :] + dot_nn(mixed[rows:, :], wx[3]))


def attend_backward_kernel(
    ids, lengths, perm, owner, q_ref, k_ref, v_ref, probs, grads_ref,
    dq, dk, dv, dqt, dkt, dvt, halves=(0, 1),
):
    def visit(head, q_at, k_at, size, kept):
        cols = slice(head * HEAD_DIM, (head + 1) * HEAD_DIM)
        q_rows = pl.ds(q_at, size)
        k_rows = pl.ds(pl.multiple_of(k_at, 256), size)
        queries = (q_ref[q_rows, cols] * SCALE).astype(bf16)
        keys = k_ref[k_rows, cols]
        grads = grads_ref[q_rows, cols]
        grad_probs_t = dot_nt(v_ref[k_rows, cols], grads)
        probs_t = kept[...]
        wide = probs_t.astype(f32)
        delta = jnp.sum(wide * grad_probs_t, axis=0, keepdims=True)
        grad_scores_t = (wide * (grad_probs_t - delta)).astype(bf16)
        grad_v = dot_nn(probs_t, grads).astype(bf16)
        grad_k = dot_nn(grad_scores_t, queries).astype(bf16)
        grad_q_t = (dot_nn(keys.T, grad_scores_t) * SCALE).astype(bf16)
        dv[k_rows, cols] = grad_v
        dk[k_rows, cols] = grad_k
        dq[q_rows, cols] = grad_q_t.T
        dvt[cols, k_rows] = grad_v.T
        dkt[cols, k_rows] = grad_k.T
        dqt[cols, q_rows] = grad_q_t

    attend_blocks(ids, lengths, perm, owner, probs, visit, halves)


def backward_attention(
    ids, lengths, perm, owner, g_a, g_b, wo, q, k, v, probs, dq, dk, dv, dqt, dkt, dvt, grads
):
    for at, g in row_blocks(g_a, g_b):
        grads[at, :] = dot_nt(g, wo).astype(bf16)
    attend_backward_kernel(
        ids, lengths, perm, owner, q, k, v, probs, grads, dq, dk, dv, dqt, dkt, dvt
    )


def row_sum(left_t):
    ones = jnp.ones((8, left_t.shape[1]), bf16)
    return dot_nt(ones, left_t)[:1]


def head_weight_grads(out, lefts, rights, vectors):
    width = lefts[0].shape[0]
    for number, (left, right) in enumerate(zip(lefts, rights)):
        out[number * width : (number + 1) * width, :] = dot_nn(left[...], right).astype(bf16)
    vectors = jnp.concatenate([vectors, jnp.zeros_like(vectors)], axis=0)
    out[len(lefts) * width :, :] = vectors.astype(bf16)


def bias_row(dqt, dvt):
    width = dqt.shape[0]
    return jnp.concatenate(
        [row_sum(dqt[...]), row_sum(dvt[...]), jnp.zeros((1, 2 * width), f32)], axis=1
    )


def attention_back_other_kernel(half, ids, lengths, perm, g, wx, q, k, v, probs, *refs):
    dq, dk, dv, dqt, dkt, dvt, grads = refs[-7:]
    rows = grads.shape[0] // 2
    grads[half * rows : (half + 1) * rows, :] = dot_nt(whole(g), wx[3]).astype(bf16)
    attend_backward_kernel(
        ids, lengths, perm, ids[0] ^ 2, q, k, v, probs, grads,
        dq, dk, dv, dqt, dkt, dvt, halves=(half,),
    )


def heads_grad_other_kernel(
    mixed_t, dqt, dkt, dvt, g_a, g_b, tok_a, tok_b, sums, got_sums, out
):
    vectors = jnp.concatenate([sums[:7] + got_sums[:7], bias_row(dqt, dvt)], axis=0)
    tokens = whole([tok_a, tok_b])
    rights = (whole(g_a + g_b), tokens, tokens, tokens)
    head_weight_grads(out, (mixed_t, dqt, dkt, dvt), rights, vectors)


def attention_back_own_kernel(
    ids, lengths, perm, g_a, g_b, tok_a, tok_b, wo, q, k, v, probs, mixed_t, sums, got_sums, inner_sums,
    dq, dk, dv, out, dqt, dkt, dvt, grads,
):
    backward_attention(
        ids, lengths, perm, ids[0], g_a, g_b, wo[...], q, k, v, probs,
        dq, dk, dv, dqt, dkt, dvt, grads,
    )
    vectors = jnp.concatenate(
        [sums[:6] + got_sums[:6], inner_sums[:1], bias_row(dqt, dvt)], axis=0
    )
    tokens = whole([tok_a, tok_b])
    rights = (whole(g_a + g_b), tokens, tokens, tokens)
    head_weight_grads(out, (mixed_t, dqt, dkt, dvt), rights, vectors)


def token_grad_other_kernel(dq, dk, dv, wx, grad_one, out):
    rows = grad_one.shape[0]
    total = dot_nn(dq[...], wx[0]) + dot_nn(dk[...], wx[1]) + dot_nn(dv[...], wx[2])
    out[:rows, :] = total[:rows, :] + grad_one[...]
    out[rows:, :] = total[rows:, :]


def token_grad_own_kernel(dq, dk, dv, wq, wk, wv, part, keep, send):
    rows = keep.shape[0]
    total = dot_nn(dq[...], wq[...]) + dot_nn(dk[...], wk[...]) + dot_nn(dv[...], wv[...])
    put(send, part[rows:, :] + total[rows:, :])
    keep[...] = part[:rows, :] + total[:rows, :]


def normalize(hidden):
    center = jnp.mean(hidden, axis=1, keepdims=True)
    rinv = lax.rsqrt(jnp.mean(hidden * hidden, axis=1, keepdims=True) - center * center + epsilon)
    return (hidden - center) * rinv, rinv


def norm_back(grad_zhat, zhat, rinv):
    first_mean = jnp.mean(grad_zhat, axis=1, keepdims=True)
    second_mean = jnp.mean(grad_zhat * zhat, axis=1, keepdims=True)
    return rinv * (grad_zhat - first_mean - zhat * second_mean)


def norm_one_kernel(tokens, keep, got, table, hidden, normed, normed_all, normed_bf):
    value = tokens[...].astype(f32) + keep[...] + whole(got).astype(f32) + table[0:1, :]
    hidden[...] = value
    zhat, _ = normalize(value)
    result = zhat * table[1:2, :] + table[2:3, :]
    normed[...] = result
    normed_all[...] = result.astype(bf16)
    put(normed_bf, result)


def norm_two_kernel(
    normed, keep, got, table, cotangent,
    grad_two, grad_two_all, grad_two_bf, sums,
):
    hidden = normed[...] + keep[...] + whole(got).astype(f32) + table[3:4, :]
    zhat, rinv = normalize(hidden)
    grad_out = cotangent[...].astype(f32)
    grad = norm_back(grad_out * table[4:5, :], zhat, rinv)
    grad_two[...] = grad
    grad_two_all[...] = grad.astype(bf16)
    put(grad_two_bf, grad)
    sums[...] = jnp.concatenate(
        [
            jnp.sum(grad, axis=0, keepdims=True),
            jnp.sum(grad_out * zhat, axis=0, keepdims=True),
            jnp.sum(grad_out, axis=0, keepdims=True),
            jnp.zeros((5, grad.shape[1]), f32),
        ],
        axis=0,
    )


def block_out_kernel(normed, keep, got, table, block_out):
    hidden = normed[...] + keep[...] + whole(got).astype(f32) + table[3:4, :]
    zhat, _ = normalize(hidden)
    block_out[...] = (zhat * table[4:5, :] + table[5:6, :]).astype(bf16)


def norm_one_back_kernel(grad_two, keep, got, hidden, table, sums_in, grad_one, grad_one_bf, sums):
    grad_normed = grad_two[...] + keep[...] + whole(got).astype(f32)
    zhat, rinv = normalize(hidden[...])
    grad = norm_back(grad_normed * table[1:2, :], zhat, rinv)
    grad_one[...] = grad
    put(grad_one_bf, grad)
    sums[...] = jnp.concatenate(
        [
            jnp.sum(grad, axis=0, keepdims=True),
            jnp.sum(grad_normed * zhat, axis=0, keepdims=True),
            jnp.sum(grad_normed, axis=0, keepdims=True),
            sums_in[:3],
            jnp.zeros((2, grad.shape[1]), f32),
        ],
        axis=0,
    )


def gelu_parts(values):
    cdf = 0.5 + 0.5 * lax.erf(values * 0.7071067811865476)
    bell = jnp.exp2((-0.5 * 1.4426950408889634) * (values * values))
    return values * cdf, cdf + values * (bell * 0.3989422804014327)


BLOCK = 256


def row_blocks(*sources):
    at = 0
    for source in sources:
        step = max(1, BLOCK // source[0].shape[0])
        for start in range(0, len(source), step):
            block = whole(source[start : start + step])
            yield slice(at, at + block.shape[0]), block
            at += block.shape[0]


def feed_own_kernel(nrm_a, nrm_b, wi, table, wo, active_t, slope, part, normed_t):
    for at, normed in row_blocks(nrm_a, nrm_b):
        normed_t[:, at] = normed.T
        value, rise = gelu_parts(dot_nn(normed, wi[...]) + table[6:7, :])
        part[at, :] = dot_nn(value.astype(bf16), wo[...])
        active_t[:, at] = value.astype(bf16).T
        slope[at, :] = rise.astype(bf16)


def feed_other_kernel(ids, nrm, wi_a, wi_b, wo_a, wo_b, part, slope, send, wi_x, wo_x):
    half, model = wi_a.shape[1], wo_x.shape[1]
    for bit, weights in ((ids[2], wi_a), (1 - ids[2], wi_b)):
        wi_x[:, pl.ds(pl.multiple_of(bit * half, 128), half)] = weights[:model, :]
    for bit, weights in ((ids[1], wo_a), (1 - ids[1], wo_b)):
        wo_x[pl.ds(pl.multiple_of(bit * half, 128), half), :] = whole(weights)
    rows = slope.shape[0]
    feed_units(nrm, wi_a, wi_x, wo_x, part.at[rows:, :], slope, lambda at, total: put_rows(send, at, total))


def feed_other_own_kernel(nrm, lines, wi_x, wo_x, part, slope, keep):
    def store(at, total):
        keep[at, :] = total

    feed_units(nrm, lines, wi_x, wo_x, part, slope, store)


def put_rows(refs, at, value):
    size = refs[0].shape[0]
    put(refs[at.start // size : at.stop // size], value)


def feed_units(nrm, lines, wi, wo, part, slope, store):
    line = lines[-16:, :].astype(f32)
    bias = jnp.concatenate([line[1:2], line[2:3]], axis=1)
    for at, normed in row_blocks(nrm):
        value, rise = gelu_parts(dot_nn(normed, wi[...]) + bias)
        slope[at, :] = rise.astype(bf16)
        store(at, part[at, :] + dot_nn(value.astype(bf16), wo[...]))


def feed_far_kernel(nrm_a, nrm_b, wi, table, active_t, slope, normed_t):
    for at, normed in row_blocks(nrm_a, nrm_b):
        normed_t[:, at] = normed.T
        value, rise = gelu_parts(dot_nn(normed, wi[...]) + table[6:7, :])
        active_t[:, at] = value.astype(bf16).T
        slope[at, :] = rise.astype(bf16)


def feed_back_kernel(half, g, slope, slope_x, wi, wo, wi_x, wo_x, grad_inner, out):
    rows = grad_inner.shape[0]
    grad = whole(g)
    rise = slope[half * rows : (half + 1) * rows, :].astype(f32)
    grad_inner[...] = (dot_nt(grad, wo[...]) * rise).astype(bf16)
    grad_x = (dot_nt(grad, wo_x[...]) * slope_x[...].astype(f32)).astype(bf16)
    total = dot_nt(grad_inner[...], wi[...]) + dot_nt(grad_x, wi_x[...])
    if half:
        put(out, total)
    else:
        out[...] = total


def feed_weights_kernel(g_a, g_b, active_t, normed_t, grad_inner, outer, inner, sums):
    outer[...] = dot_nn(active_t[...], whole(g_a + g_b))
    grads = whole(grad_inner)
    inner[...] = dot_nn(normed_t[...], grads)
    sums[...] = dot_nn(jnp.ones((8, grads.shape[0]), bf16), grads)


def feed_weights_far_kernel(
    ids, g_a, g_b, active_t, normed_t, slope, wo, outer, inner, sums_in,
    outer_keep, outer_send, inner_keep, inner_send, sums, grad_inner,
):
    for at, g in row_blocks(g_a, g_b):
        grad_inner[at, :] = (dot_nt(g, wo[...]) * slope[at, :].astype(f32)).astype(bf16)
    grads = whole(g_a + g_b)
    half = outer_keep.shape[0]
    for index, target in ((1 - ids[1], outer_send), (ids[1], outer_keep)):
        at = pl.ds(pl.multiple_of(index * half, 128), half)
        target[...] = (dot_nn(active_t[at, :], grads) + outer[at, :]).astype(target.dtype)
    for index, target in ((1 - ids[2], inner_send), (ids[2], inner_keep)):
        at = pl.ds(pl.multiple_of(index * half, 128), half)
        target[...] = (dot_nn(normed_t[at, :], grad_inner[...]) + inner[at, :]).astype(
            target.dtype
        )
    sums[...] = sums_in[...] + dot_nn(
        jnp.ones((8, grad_inner.shape[0]), bf16), grad_inner[...]
    )


Y_FIRST = (4, (0, 2, 1, 3))
Z_FIRST = (3, (0, 1, 2, 3))


def quarter_rows(ids, layout, number, rows):
    index, numbers = layout
    return pl.ds(pl.multiple_of((ids[index] ^ numbers[number]) * rows, 16), rows)


def halve_kernel(which, extra, ids, kept, got, keep, send):
    body = kept.shape[0] - extra
    half = body // 2
    bit = ids[which]
    for index, target in ((1 - bit, send), (bit, keep)):
        at = pl.ds(pl.multiple_of(index * half, 16), half)
        target[:half, :] = (kept[at, :].astype(f32) + got[at, :].astype(f32)).astype(target.dtype)
    if extra:
        total = (kept[body:, :].astype(f32) + got[body:, :].astype(f32)).astype(bf16)
        send[half:, :] = total
        keep[half:, :] = total.astype(f32)


def add_two_kernel(kept, got, out):
    out[...] = (kept[...].astype(f32) + got[...].astype(f32)).astype(bf16)


def add_last_kernel(kept, got, out, vectors):
    rows = out.shape[0]
    total = kept[...].astype(f32) + got[...].astype(f32)
    out[...] = total[:rows, :].astype(bf16)
    vectors[...] = total[rows:, :]


def token_out_kernel(kept, got, out):
    out[...] = kept[...] + whole(got).astype(f32)


STEPS = (
    "token_grad",
    "outer_halve",
    "inner_halve",
    "heads_whole",
    "inner_quarter",
    "outer_quarter",
    "token_out",
    "block_out",
    "heads_halve",
    "inner_finish",
    "outer_finish",
    "heads_quarter",
    "heads_finish",
    "inner_place",
    "outer_place",
)
PATHS = ("direct", "y", "direct")
HEADS_BITS = (1, 2)


class Group:
    def __init__(self, order, ids, name, extra, keep):
        self.order, self.ids, self.name, self.extra = order, ids, name, extra
        self.keep = keep

    def halve(self, bit):
        rows, cols = self.keep.shape
        half = (rows - self.extra) // 2 + self.extra
        self.keep, send = self.order.call(
            functools.partial(halve_kernel, bit, self.extra),
            (self.ids,),
            (self.keep, self.got),
            [((half, cols), f32), ((half, cols), bf16)],
            name=self.name + "_halve",
        )
        self.got = swap(send, "batch", bit)

    def quarter(self):
        (self.keep,) = self.order.call(
            add_two_kernel,
            (),
            (self.keep, self.got),
            [(self.keep.shape, bf16)],
            name=self.name + "_quarter",
        )
        stride = 4
        while 2 * stride < lax.axis_size("batch"):
            (self.keep,) = self.order.call(
                add_two_kernel,
                (),
                (self.keep, swap(self.keep, "batch", stride)),
                [(self.keep.shape, bf16)],
                name=self.name + "_%d" % stride,
            )
            stride *= 2
        self.got = swap(self.keep, "batch", stride)

    def finish(self, path):
        rows, cols = self.keep.shape
        outputs = [((rows - self.extra, cols), bf16)]
        if self.extra:
            outputs.append(((self.extra, cols), f32))
        results = self.order.call(
            add_last_kernel if self.extra else add_two_kernel,
            (),
            (self.keep, self.got),
            outputs,
            name=self.name + "_finish",
        )
        self.vectors = results[-1]
        mine = results[0]
        far, near = swap(mine, "batch", 1), swap(mine, "batch", 2)
        if path == "direct":
            across = swap(mine, "batch", 3)
        elif path == "y":
            across = swap(after(near, far), "batch", 1)
        else:
            across = swap(after(far, near), "batch", 2)
        self.pieces = [mine, far, near, across]


def place_kernel(layout, ids, pieces, out):
    rows = pieces[0].shape[0]
    for number, part in enumerate(pieces):
        out[quarter_rows(ids, layout, number, rows), :] = part[...].astype(f32)


def place_heads_kernel(ids, pieces, vectors, grads, lines, biases, scratch):
    index, numbers = Y_FIRST if HEADS_BITS == (1, 2) else Z_FIRST
    for number, part in enumerate(pieces):
        scratch[ids[index] ^ numbers[number]] = part[...].astype(f32)
    for number, out in enumerate(grads):
        out[...] = scratch[number]
    for number, out in enumerate(lines):
        out[...] = vectors[number : number + 1, :].reshape(out.shape)
    for number, out in enumerate(biases):
        width = out.shape[0]
        line = vectors[7:8, number * width : (number + 1) * width]
        out[...] = line.reshape(out.shape)


def body(
    tokens_in,
    cotangent,
    half_length,
    block_perm,
    w_query,
    b_query,
    w_key,
    w_value,
    b_value,
    w_output,
    b_output,
    norm1_gain,
    norm1_shift,
    w_inner,
    b_inner,
    w_outer,
    b_outer,
    norm2_gain,
    norm2_shift,
):
    width = w_query.shape[0]
    model = w_query.shape[1]
    units = w_outer.shape[0]
    rows = tokens_in.shape[0]
    both = 2 * rows
    half = model // 2
    index = lax.axis_index("batch")
    ids = jnp.stack(
        [
            lax.axis_index("heads"),
            index & 1,
            (index >> 1) & 1,
            index & 3,
            (index & 1) * 2 + ((index >> 1) & 1),
        ]
    ).astype(jnp.int32)
    scalars = (ids, half_length, block_perm)
    order = Order()

    (packed,) = order.call(
        pack_attention_kernel,
        (ids,),
        (w_query, w_key, w_value, w_output),
        [((2 * width, model), bf16)],
        scratch=[pltpu.SemaphoreType.DMA((4,))],
        name="pack_attention",
        remote=4,
        far=True,
    )
    first = swap(packed, "heads", 2)
    other_tokens = swap(tokens_in, "heads", 1)
    table, lines = order.call(
        vectors_kernel,
        (),
        (
            b_query,
            b_value,
            b_inner,
            b_output,
            norm1_gain,
            norm1_shift,
            b_outer,
            norm2_gain,
            norm2_shift,
        ),
        [((8, model), f32), ((16, half), bf16)],
        name="vectors",
    )
    inner_half, outer_half = order.call(
        pack_ffn_kernel,
        (ids,),
        (lines, w_inner, w_outer),
        [
            ((model + 16, units // 2), bf16),
            [((units // 2 // OUTER_PIECES, model), bf16)] * OUTER_PIECES,
        ],
        scratch=[pltpu.SemaphoreType.DMA((2 + OUTER_PIECES,))],
        name="pack_ffn",
        remote=2,
    )
    inner_a = swap(inner_half, "heads", 2)
    outer_a = swap(outer_half, "heads", 2)
    second = swap(first, "batch", 1)
    inner_b = swap(inner_a, "batch", 2)
    outer_b = swap(outer_a, "batch", 1)

    head_outputs = [
        ((both, width), bf16),
        ((both, width), bf16),
        ((both, width), bf16),
        ((3, 2, both // 2, both // 2), bf16),
        ((width, both), bf16),
    ]
    mixed = pltpu.VMEM((both, width), bf16)
    q, k, v, probs, mixed_t, part = order.call(
        attention_own_kernel,
        scalars,
        (tokens_in, other_tokens, table, w_query, w_key, w_value, w_output),
        head_outputs + [((both, model), f32)],
        scratch=[mixed]
        + [pltpu.VMEM((width, model), bf16)] * 4
        + [pltpu.SemaphoreType.DMA((4,))],
        name="attention_own",
        remote=4,
    )
    qx, kx, vx, probs_x, mixed_tx, wx, keep, send = order.call(
        attention_other_kernel,
        scalars,
        (tokens_in, other_tokens, first, after(second, inner_a), inner_a, part),
        head_outputs
        + [((4, width, model), bf16), ((rows, model), f32), chunked(rows, model, "projected")],
        scratch=[mixed],
        name="attention_other",
    )
    hidden_one, normed, normed_all, normed_bf = order.call(
        norm_one_kernel,
        (),
        (
            tokens_in,
            keep,
            after(swap(send, "heads", 1), outer_a),
            table,
        ),
        [
            ((rows, model), f32),
            ((rows, model), f32),
            ((rows, model), bf16),
            chunked(rows, model, "normed"),
        ],
        name="norm_one",
    )

    other_normed = swap(normed_bf, "heads", 1)
    far_normed = swap([normed_all], "heads", 2)
    active_t, slope, part, normed_t = order.call(
        feed_own_kernel,
        (),
        (normed_bf, other_normed, w_inner, table, w_outer),
        [
            ((units, both), bf16),
            ((both, units), bf16),
            ((both, model), f32),
            ((model, both), bf16),
        ],
        name="feed_own",
    )
    slope_xb, send, wi_x, wo_x = order.call(
        feed_other_kernel,
        (ids,),
        (other_normed, inner_a, inner_b, outer_a, outer_b, part),
        [
            ((rows, units), bf16),
            chunked(rows, model, "fed"),
            ((model, units), bf16),
            ((units, model), bf16),
        ],
        name="feed_other",
    )
    slope_xa, keep = order.call(
        feed_other_own_kernel,
        (),
        (normed_bf, inner_a, wi_x, wo_x, part),
        [((rows, units), bf16), ((rows, model), f32)],
        name="feed_other_own",
    )
    fed = (normed, keep, swap(send, "heads", 1), table)
    grad_two, grad_two_all, grad_two_bf, sums_two = order.call(
        norm_two_kernel,
        (),
        (*fed, cotangent),
        [
            ((rows, model), f32),
            ((rows, model), bf16),
            chunked(rows, model, "grad_two"),
            ((8, model), f32),
        ],
        name="norm_two",
    )

    far_normed = after(far_normed, sums_two)
    far_other_normed = swap(far_normed, "heads", 1)
    other_grad_two = swap(grad_two_bf, "heads", 1)
    far_grad_two = swap([grad_two_all], "heads", 2)
    grad_inner = [None, None]
    grad_inner[0], keep = order.call(
        functools.partial(feed_back_kernel, 0),
        (),
        (grad_two_bf, slope, slope_xa, w_inner, w_outer, wi_x, wo_x),
        [((rows, units), bf16), ((rows, model), f32)],
        name="feed_back_own",
    )
    grad_inner[1], send = order.call(
        functools.partial(feed_back_kernel, 1),
        (),
        (other_grad_two, slope, slope_xb, w_inner, w_outer, wi_x, wo_x),
        [((rows, units), bf16), chunked(rows, model, "back")],
        name="feed_back_other",
    )
    active_f, slope_f, normed_f = order.call(
        feed_far_kernel,
        (),
        (far_normed, far_other_normed, w_inner, table),
        [((units, both), bf16), ((both, units), bf16), ((model, both), bf16)],
        name="feed_far",
    )
    grad_one, grad_one_bf, sums_one = order.call(
        norm_one_back_kernel,
        (),
        (grad_two, keep, swap(send, "heads", 1), hidden_one, table, sums_two),
        [((rows, model), f32), chunked(rows, model, "grad_one"), ((8, model), f32)],
        name="norm_one_back",
    )

    grads_one = (grad_one_bf, swap(grad_one_bf, "heads", 1))
    row_sums = (sums_one, swap(sums_one, "heads", 1))
    grads_one = (grads_one[0], after(grads_one[1], row_sums[1]))
    head_grads = [((both, width), bf16)] * 3
    group = [((4 * width + 16, model), bf16)]
    head_scratch = [pltpu.VMEM((width, both), bf16)] * 3 + [pltpu.VMEM((both, width), bf16)]
    head_blocks = [((both, width), bf16)] * 3 + [((width, both), bf16)] * 3
    results = []
    for number in range(2):
        results = order.call(
            functools.partial(attention_back_other_kernel, number),
            scalars,
            (grads_one[number], wx, qx, kx, vx, probs_x, *results),
            head_blocks,
            scratch=[pltpu.VMEM((both, width), bf16)],
            name="attention_back_other",
            aliases={
                3 + len(grads_one[number]) + 5 + i: i for i in range(6) if len(results) > 0
            },
        )
    dqx, dkx, dvx, *back_t = results
    far_grad_two = after(far_grad_two, dqx)
    far_other_grad_two = swap(far_grad_two, "heads", 1)
    (far_heads,) = order.call(
        heads_grad_other_kernel,
        (),
        (mixed_tx, *back_t, *grads_one, tokens_in, other_tokens, *row_sums),
        group,
        name="heads_grad_other",
    )
    got_heads = swap(far_heads, "heads", 2)

    outer_part, inner_part, part_sums = order.call(
        feed_weights_kernel,
        (),
        (grad_two_bf, other_grad_two, active_t, normed_t, grad_inner),
        [((units, model), f32), ((model, units), f32), ((8, units), f32)],
        name="feed_weights",
    )
    halves = [((units // 2, model), f32), ((units // 2, model), bf16)]
    outer_keep, outer_send, inner_keep, inner_send, inner_sums = order.call(
        feed_weights_far_kernel,
        (ids,),
        (
            far_grad_two,
            far_other_grad_two,
            active_f,
            normed_f,
            slope_f,
            w_outer,
            outer_part,
            inner_part,
            part_sums,
        ),
        halves + halves + [((8, units), f32)],
        scratch=[pltpu.VMEM((both, units), bf16)],
        name="feed_weights_far",
    )
    outer = Group(order, ids, "outer", 0, outer_keep)
    outer.got = swap(outer_send, "batch", 1)
    inner = Group(order, ids, "inner", 0, inner_keep)
    inner.got = swap(inner_send, "batch", 2)

    (token_part,) = order.call(
        token_grad_other_kernel,
        (),
        (dqx, dkx, dvx, wx, grad_one),
        [((both, model), f32)],
        name="token_grad_other",
    )
    dq, dk, dv, own_heads = order.call(
        attention_back_own_kernel,
        scalars,
        (
            *grads_one,
            tokens_in,
            other_tokens,
            w_output,
            q,
            k,
            v,
            probs,
            mixed_t,
            *row_sums,
            inner_sums,
        ),
        head_grads + group,
        scratch=head_scratch,
        name="attention_back_own",
    )
    heads = Group(order, ids, "heads", 16, own_heads)
    heads.got = got_heads
    tokens_sum = {}

    def token_grad():
        tokens_sum["keep"], send = order.call(
            token_grad_own_kernel,
            (),
            (dq, dk, dv, w_query, w_key, w_value, token_part),
            [((rows, model), f32), chunked(rows, model, "tokens")],
            name="token_grad_own",
        )
        tokens_sum["send"] = send

    def token_out():
        tokens_sum["got"] = swap(after(tokens_sum["send"], order.last), "heads", 1)
        (tokens_sum["out"],) = order.call(
            token_out_kernel,
            (),
            (tokens_sum["keep"], tokens_sum["got"]),
            [((rows, model), f32)],
            name="token_out",
        )

    def place(group, layout, shape):
        (group.whole,) = order.call(
            functools.partial(place_kernel, layout),
            (ids,),
            (group.pieces,),
            [(shape, f32)],
            name="place_" + group.name,
        )

    def block_out():
        (tokens_sum["block"],) = order.call(
            block_out_kernel, (), fed, [((rows, model), bf16)], name="block_out"
        )

    steps = {
        "block_out": block_out,
        "outer_halve": lambda: outer.halve(2),
        "outer_quarter": outer.quarter,
        "outer_finish": lambda: outer.finish(PATHS[0]),
        "outer_place": lambda: place(outer, Y_FIRST, (units, model)),
        "inner_halve": lambda: inner.halve(1),
        "inner_quarter": inner.quarter,
        "inner_finish": lambda: inner.finish(PATHS[1]),
        "inner_place": lambda: place(inner, Z_FIRST, (model, units)),
        "heads_whole": lambda: heads.halve(HEADS_BITS[0]),
        "heads_halve": lambda: heads.halve(HEADS_BITS[1]),
        "heads_quarter": heads.quarter,
        "heads_finish": lambda: heads.finish(PATHS[2]),
        "token_grad": token_grad,
        "token_out": token_out,
    }
    for step in STEPS:
        steps[step]()
    grad_tokens, grad_w_outer, grad_w_inner = tokens_sum["out"], outer.whole, inner.whole
    (grad_o, grad_q, grad_k, grad_v), lines, biases = order.call(
        place_heads_kernel,
        (ids,),
        (heads.pieces, heads.vectors),
        [[((width, model), f32)] * 4, [((model,), f32)] * 7, [((width,), f32)] * 2],
        scratch=[pltpu.VMEM((4, width, model), f32)],
        name="place_heads",
    )

    return (
        tokens_sum["block"],
        grad_tokens,
        grad_q,
        biases[0],
        grad_k,
        grad_v,
        biases[1],
        grad_o,
        lines[0],
        lines[1],
        lines[2],
        grad_w_inner,
        lines[6],
        grad_w_outer,
        lines[3],
        lines[4],
        lines[5],
    )


def solution(mesh):
    placed = (
        P(("batch", "heads"), None),
        P(("batch", "heads"), None),
        P("batch"),
        P(),
        P("heads", None),
        P("heads"),
        P("heads", None),
        P("heads", None),
        P("heads"),
        P("heads", None),
        P(),
        P(),
        P(),
        P(None, "heads"),
        P("heads"),
        P("heads", None),
        P(),
        P(),
        P(),
    )
    return jax.shard_map(
        body,
        mesh=mesh,
        in_specs=placed,
        out_specs=(
            P(("batch", "heads"), None),
            P(("batch", "heads"), None),
            P("heads", None),
            P("heads"),
            P("heads", None),
            P("heads", None),
            P("heads"),
            P("heads", None),
            P(),
            P(),
            P(),
            P(None, "heads"),
            P("heads"),
            P("heads", None),
            P(),
            P(),
            P(),
        ),
        check_vma=False,
    )
```
